512 devices in a mesh: slab: 64 (over x_lo, z, core), pen: 8 (over x_hi, y).
Axes of the slice: x: 4 (x_hi: 2, x_lo: 2; x = x_hi * 2 + x_lo), y: 4, z: 16, core: 2. Of those that a mesh axis runs over, the one named last changes fastest.
Arguments:
- density: float32 [128, 256, 2048], P('slab', None, 'pen'), may hold values from -6 to 6
Outputs:
- coefficients: float32 [128, 256, 2048], P('slab', None, 'pen')
- approximation: float32 [64, 128, 1024], P('slab', None, 'pen')
The draws below stay inside these ranges and needn't reach their ends.
All inputs are finite; a program needn't handle non-finite values.
Results may differ from the reference program's by a relative error of at most 0.00015.
Values sent between devices are 32-bit elements; how exact they have to be, the bound alone decides.
A program may use at most 128 MiB of HBM per device.

```python
import jax
import jax.numpy as jnp
from jax import lax

NX = 2048
NZ = 256
LEVELS = 1
NY = 128


def draw_density(key, part):
    key = jax.random.fold_in(key, 11)
    return jnp.clip(jax.random.normal(key, (NY, NZ, NX), jnp.float32), -6.0, 6.0)


def setup_inputs(seed: int = 0) -> dict:
    key_list = jax.random.split(jax.random.key(seed), 2)
    return {
        "density": draw_density(jax.random.fold_in(key_list[1], 71), 0),
    }


def refine(values, dimension):
    leading = jnp.moveaxis(values, dimension, 0)
    following = jnp.concatenate([leading[1:], leading[-1:]], 0)
    midpoints = 0.5 * (leading + following)
    refined = jnp.stack([leading, midpoints], 1).reshape((2 * leading.shape[0],) + leading.shape[1:])
    return jnp.moveaxis(refined, 0, dimension)

def project(values, dimension):
    leading = jnp.moveaxis(values, dimension, 0)
    half_count = leading.shape[0] // 2
    zeros_row = jnp.zeros_like(leading[:1])
    bordered = jnp.concatenate([zeros_row, leading, zeros_row], 0)
    smoothed = (bordered[:-2] + 4.0 * leading + bordered[2:]) / 6.0
    even_part = smoothed[0::2]
    odd_part = smoothed[1::2]
    previous = jnp.concatenate([zeros_row, odd_part[:-1]], 0)
    weights = jnp.where(jnp.arange(half_count) == half_count - 1, 1.0, 0.5).astype(values.dtype)
    weights = weights.reshape((half_count,) + (1,) * (values.ndim - 1))
    loads = even_part + 0.5 * previous + weights * odd_part
    flattened = loads.reshape(half_count, -1)
    third = jnp.full((half_count - 1,), 1.0 / 3.0, values.dtype)
    nothing = jnp.zeros((1,), values.dtype)
    sub_diagonal = jnp.concatenate([nothing, third])
    super_diagonal = jnp.concatenate([third, nothing])
    main_diagonal = jnp.full((half_count,), 4.0 / 3.0, values.dtype)
    solved = lax.linalg.tridiagonal_solve(sub_diagonal, main_diagonal, super_diagonal, flattened)
    return jnp.moveaxis(solved.reshape(loads.shape), 0, dimension)

def embed_coarse(values):
    expanded = values[:, None, :, None, :, None]
    padded = jnp.pad(expanded, ((0, 0), (0, 1), (0, 0), (0, 1), (0, 0), (0, 1)))
    return padded.reshape(2 * values.shape[0], 2 * values.shape[1], 2 * values.shape[2])

def reference(density):
    current = density
    details = []
    for level_index in range(LEVELS):
        coarse = current[::2, ::2, ::2]
        interpolant = refine(refine(refine(coarse, 2), 1), 0)
        correction = current - interpolant
        projected = project(project(project(correction, 0), 1), 2)
        details.append(correction)
        current = coarse + projected
    result = current
    for correction in reversed(details):
        result = correction + embed_coarse(result)
    return (result, current)
```

```python
import functools
import math

import jax
import jax.numpy as jnp
import ml_dtypes
import numpy as np
from jax import lax
from jax.experimental import pallas as pl
from jax.experimental.pallas import tpu as pltpu
from jax.sharding import PartitionSpec as P

MESH = pl.DeviceIdType.MESH
DECAY = math.log(2.0 + math.sqrt(3.0))
GROUP = 8
STATE_ROWS = 8
F32 = jnp.float32
BF16 = jnp.bfloat16


def inverse_mass(m):
    i = np.arange(m)[:, None]
    j = np.arange(m)[None, :]
    low, high = np.minimum(i, j), np.maximum(i, j)
    sign = np.where((high - low) % 2 == 0, 1.0, -1.0)
    ends = (1 - np.exp(-2 * (low + 1) * DECAY)) * (1 - np.exp(-2 * (m - high) * DECAY))
    scale = 3.0 / (2 * math.sqrt(3.0) * (1 - np.exp(-2 * (m + 1) * DECAY)))
    return scale * sign * np.exp(-(high - low) * DECAY) * ends


def refine_matrix(m):
    matrix = np.zeros((2 * m, m))
    j = np.arange(m)
    matrix[2 * j, j] = 1.0
    matrix[2 * j[:-1] + 1, j[:-1]] = 0.5
    matrix[2 * j[:-1] + 1, j[:-1] + 1] = 0.5
    matrix[2 * m - 1, m - 1] = 1.0
    return matrix


def project_matrix(m):
    j = np.arange(m)
    load = np.zeros((m, 2 * m + 2))
    w = np.where(j == m - 1, 1.0, 0.5)
    for offset, weight in ((-2, 0.5), (-1, 3.0), (0, 5.0), (1, 3.0), (2, 0.5)):
        keep = 2 * j + offset >= 0
        load[j[keep], 2 * j[keep] + offset] = weight / 6.0
    load[0, 0] = 4.5 / 6.0
    load[m - 1, 2 * m - 2] = (4.0 + w[-1] + 0.5) / 6.0
    load[m - 1, 2 * m - 1] = (1.0 + 4.0 * w[-1]) / 6.0
    return inverse_mass(m) @ load[:, : 2 * m]


def falling(m, i, start):
    d = i - start
    sign = np.where(d % 2 == 0, 1.0, -1.0)
    ends = (1 - np.exp(-2.0 * (m - i) * DECAY)) / (1 - np.exp(-2.0 * (m - start) * DECAY))
    return sign * np.exp(-d * DECAY) * ends


def rising(m, i, start):
    d = start - i
    sign = np.where(d % 2 == 0, 1.0, -1.0)
    ends = (1 - np.exp(-2.0 * (i + 1) * DECAY)) / (1 - np.exp(-2.0 * (start + 1) * DECAY))
    return sign * np.exp(-d * DECAY) * ends


class Blocks:
    def __init__(self, m, n):
        whole = project_matrix(m)
        size = m // n
        rows = np.arange(size)
        self.diagonal = np.stack(
            [whole[b * size : (b + 1) * size, 2 * b * size : 2 * (b + 1) * size] for b in range(n)]
        )
        self.to_later = np.zeros((n, 2 * size))
        self.to_earlier = np.zeros((n, 2 * size))
        self.later_first = np.zeros(n)
        self.earlier_last = np.zeros(n)
        self.falling = np.zeros((n, size))
        self.rising = np.zeros((n, size))
        self.from_earlier = np.zeros((n, n))
        self.from_later = np.zeros((n, n))
        inverse = inverse_mass(m)
        self.own_first = inverse[:size, 0]
        self.own_last = inverse[m - size :, m - 1]
        for b in range(n):
            columns = slice(2 * b * size, 2 * (b + 1) * size)
            first, last = b * size, (b + 1) * size - 1
            if b < n - 1:
                self.to_later[b] = whole[last + 1, columns]
            if b > 0:
                self.to_earlier[b] = whole[first - 1, columns]
            self.falling[b] = falling(m, first + rows, first)
            self.rising[b] = rising(m, first + rows, last)
            for c in range(n):
                if c < b:
                    self.from_earlier[b, c] = falling(m, first, (c + 1) * size)
                if c > b:
                    self.from_later[b, c] = rising(m, last, c * size - 1)
        self.first_to_later = inverse[size, 0] if n > 1 else 0.0
        self.last_to_earlier = inverse[m - size - 1, m - 1] if n > 1 else 0.0


def split(matrix):
    matrix = np.asarray(matrix, np.float32)
    high = matrix.astype(ml_dtypes.bfloat16)
    low = (matrix - high.astype(np.float32)).astype(ml_dtypes.bfloat16)
    return high, low


def parts(value):
    high = value.astype(BF16)
    return high, (value - high.astype(F32)).astype(BF16)


def dot(a, b, transposed=False):
    dims = (((1,), (1 if transposed else 0,)), ((), ()))
    return lax.dot_general(a, b, dims, preferred_element_type=F32)


def dot3(a, b, transposed=False):
    return (
        dot(a[0], b[0], transposed) + dot(a[0], b[1], transposed) + dot(a[1], b[0], transposed)
    )


class Scalars:
    def __init__(self, groups):
        g = GROUP
        self.local = 0
        self.to_later = self.local + 2 * g * g
        self.to_earlier = self.to_later + 2 * g
        self.falling = self.to_earlier + 2 * g
        self.rising = self.falling + g
        self.from_earlier = self.rising + g
        self.from_later = self.from_earlier + groups
        self.size = self.from_later + groups


def kernel(
    sizes,
    u_hbm, fixed_hbm, left_hbm, ends_hbm, table, pens,
    fine_hbm, coarse_hbm,
    u, fixed, left, ends, coarse_t, halo_in, halo_out, next_c, lift,
    out_a, in_a, out_b, in_b, out_c, in_c, out_x, in_x,
    fine, coarse,
    load_sem, store_sem,
    h1_send, h1_recv, h2_send, h2_recv,
    a_send, a_recv, b_send, b_recv, c_send, c_recv, x_send, x_recv,
):
    slabs, n_pen, groups, nx, nz, at = sizes
    part = nx // GROUP
    s = lax.axis_index("slab")
    p = lax.axis_index("pen")
    g = s // GROUP
    m = lax.rem(s, GROUP)

    loads = [
        pltpu.make_async_copy(u_hbm, u, load_sem.at[0]),
        pltpu.make_async_copy(fixed_hbm, fixed, load_sem.at[1]),
        pltpu.make_async_copy(left_hbm.at[p], left, load_sem.at[2]),
        pltpu.make_async_copy(ends_hbm.at[p], ends, load_sem.at[3]),
    ]
    for load in loads:
        load.start()

    members = [(g * GROUP + lax.rem(m + k, GROUP), p) for k in range(1, GROUP)]
    others = [(lax.rem(g + k, groups) * GROUP + m, p) for k in range(1, groups)]
    peers = [(s, lax.rem(p + k, n_pen)) for k in range(1, n_pen)]
    above = (lax.rem(s + 1, slabs), p)
    below = (lax.rem(s + slabs - 1, slabs), p)
    barrier = pltpu.get_barrier_semaphore()
    greeted = others + peers + members + [above]
    for device in greeted:
        pl.semaphore_signal(barrier, inc=1, device_id=device, device_id_type=MESH)

    for load in loads:
        load.wait()

    u0 = parts(u[0])
    u1 = parts(u[1])
    lx = (left[0, : nx + 16], left[1, : nx + 16])
    select_x = left[0, nx + 16 :]
    pz = (fixed[0], fixed[1])
    select_z = fixed[2]
    t0 = dot3(lx, u0, True)
    tc = dot(select_x, u0[0], True) + dot(select_x, u0[1], True)
    t1 = dot3(lx, u1, True)
    y0 = dot3(parts(t0), pz)
    y1 = dot3(parts(t1), pz)
    tc = parts(tc)
    c = dot(tc[0], select_z) + dot(tc[1], select_z)
    coarse_t[:nx, :] = c

    z_ends = lift[0:1, :], lift[1:2, :]
    d = c[:, 0:1] * z_ends[0] + c[:, nz - 1 : nz] * z_ends[1]
    cz = c - d
    cz_first, cz_last = cz[0:1, :], cz[nx - 1 : nx, :]
    ex = ends[:, 2:3] * cz_first + ends[:, 3:4] * cz_last
    rows8 = lax.broadcasted_iota(jnp.int32, (STATE_ROWS, nz), 0)
    czx_state = jnp.where(
        rows8 == 0,
        pens[p, 2 * n_pen] * cz_first + pens[p, 2 * n_pen + 1] * cz_last,
        pens[p, 2 * n_pen + 2] * cz_first + pens[p, 2 * n_pen + 3] * cz_last,
    )
    czx = cz + ex
    s0 = jnp.where(s == 0, F32(0.5), F32(0.0))
    s1 = jnp.where(s == 0, F32(-1.0 / 12.0), jnp.where(s == slabs - 1, F32(-0.8), F32(0.0)))
    p0 = y0[:nx] + s0 * czx
    p1 = y1[:nx] + s1 * czx
    n0 = y0[nx : nx + STATE_ROWS] + s0 * czx_state
    n1 = y1[nx + STATE_ROWS : nx + 2 * STATE_ROWS] + s1 * jnp.roll(czx_state, 2, 0)
    out_a[:, 0:part, :] = p0.reshape(GROUP, part, nz)
    out_a[:, part : 2 * part, :] = p1.reshape(GROUP, part, nz)
    out_a[:, 2 * part :, :] = jnp.broadcast_to(
        jnp.where(rows8 < 2, n0, n1)[None], (GROUP, STATE_ROWS, nz)
    )
    in_a[m] = out_a[m]
    halo_out[...] = c[0:8, :]

    pl.semaphore_wait(barrier, len(greeted))

    copies_a = []
    for k in range(1, GROUP):
        to = lax.rem(m + k, GROUP)
        copy = pltpu.make_async_remote_copy(
            src_ref=out_a.at[to], dst_ref=in_a.at[m], send_sem=a_send.at[k], recv_sem=a_recv.at[k],
            device_id=(g * GROUP + to, p), device_id_type=MESH,
        )
        copy.start()
        copies_a.append(copy)
    copy_h1 = pltpu.make_async_remote_copy(
        src_ref=halo_out, dst_ref=halo_in, send_sem=h1_send, recv_sem=h1_recv,
        device_id=(s, lax.rem(p + n_pen - 1, n_pen)), device_id_type=MESH,
    )
    copy_h1.start()

    in_b[g] = jnp.zeros((part + STATE_ROWS, nz), F32)
    rest = d - ex

    copy_h1.wait_recv()
    halo = jnp.where(p == n_pen - 1, c[nx - 1 : nx, :], halo_in[0:1, :])
    coarse_t[nx : nx + 8, :] = jnp.broadcast_to(halo, (8, nz))
    copy_h2 = pltpu.make_async_remote_copy(
        src_ref=coarse_t, dst_ref=next_c, send_sem=h2_send, recv_sem=h2_recv,
        device_id=below, device_id_type=MESH,
    )
    copy_h2.start()

    fine_rows = lax.broadcasted_iota(jnp.int32, (2 * nx, nz), 0)

    def interpolant(values, beyond):
        high, low = parts(values)
        along_x = dot(fixed[3], high) + dot(fixed[3], low)
        along_x = along_x + jnp.where(fine_rows == 2 * nx - 1, 0.5 * beyond, 0.0)
        high, low = parts(along_x)
        return dot(fixed[4], high, True) + dot(fixed[4], low, True)

    zi = lax.broadcasted_iota(jnp.int32, (2 * nz, 2 * nx), 0)
    xi = lax.broadcasted_iota(jnp.int32, (2 * nz, 2 * nx), 1)
    kept = ((zi | xi) & 1) == 0
    fine[0] = jnp.where(kept, 0.0, u[0] - interpolant(c, halo))

    for copy in copies_a:
        copy.wait_recv()

    def weigh(base, step, count, get):
        total = table[g, base] * get(0)
        for k in range(1, count):
            total = total + table[g, base + k * step] * get(k)
        return total

    def plane(k):
        return in_a[k // 2, (k % 2) * part : (k % 2 + 1) * part, :]

    def state(k):
        return in_a[k, 2 * part :, :]

    def states(base):
        even = weigh(base, 2, GROUP, state)
        odd = weigh(base + 1, 2, GROUP, state)
        return even + jnp.roll(odd, STATE_ROWS - 2, 0)

    for way, base in ((0, at.to_later), (1, at.to_earlier)):
        out_b[way, :part, :] = weigh(base, 1, 2 * GROUP, plane)
        out_b[way, part:, :] = states(base)
    copies_b = []
    for k in range(1, groups):
        to = lax.rem(g + k, groups)
        copy = pltpu.make_async_remote_copy(
            src_ref=out_b.at[jnp.where(to > g, 0, 1)], dst_ref=in_b.at[g],
            send_sem=b_send.at[k], recv_sem=b_recv.at[k],
            device_id=(to * GROUP + m, p), device_id_type=MESH,
        )
        copy.start()
        copies_b.append(copy)

    for i in range(GROUP):
        out_c[i] = weigh(at.local + 2 * GROUP * i, 1, 2 * GROUP, plane)
    own_states = states(at.local + 2 * GROUP * m)

    copy_h2.wait_recv()
    last = s == slabs - 1
    after = jnp.where(last, coarse_t[...], next_c[...])
    middle = 0.5 * (coarse_t[...] + after)
    fine[1] = u[1] - interpolant(middle[:nx], middle[nx : nx + 1])
    store_odd = pltpu.make_async_copy(fine.at[1], fine_hbm.at[1], store_sem.at[0])
    store_odd.start()

    for copy in copies_b:
        copy.wait_recv()
    from_earlier = weigh(at.from_earlier, 1, groups, lambda k: in_b[k])
    from_later = weigh(at.from_later, 1, groups, lambda k: in_b[k])
    own_states = (
        own_states
        + table[g, at.falling + m] * from_earlier[part:]
        + table[g, at.rising + m] * from_later[part:]
        - czx_state
    )
    out_x[...] = own_states
    copies_x = []
    for k in range(1, n_pen):
        copy = pltpu.make_async_remote_copy(
            src_ref=out_x, dst_ref=in_x.at[p], send_sem=x_send.at[k], recv_sem=x_recv.at[k],
            device_id=(s, lax.rem(p + k, n_pen)), device_id_type=MESH,
        )
        copy.start()
        copies_x.append(copy)
    for i in range(GROUP):
        out_c[i] = (
            out_c[i]
            + table[g, at.falling + i] * from_earlier[:part]
            + table[g, at.rising + i] * from_later[:part]
        )
    copies_c = []
    for k in range(1, GROUP):
        to = lax.rem(m + k, GROUP)
        copy = pltpu.make_async_remote_copy(
            src_ref=out_c.at[to], dst_ref=in_c.at[m], send_sem=c_send.at[k], recv_sem=c_recv.at[k],
            device_id=(g * GROUP + to, p), device_id_type=MESH,
        )
        copy.start()
        copies_c.append(copy)
    in_c[m] = out_c[m]
    in_x[p] = out_x[...]

    for copy in copies_x:
        copy.wait_recv()
    x_earlier = pens[p, 0] * in_x[0, 0:1, :]
    x_later = pens[p, n_pen] * in_x[0, 1:2, :]
    for k in range(1, n_pen):
        x_earlier = x_earlier + pens[p, k] * in_x[k, 0:1, :]
        x_later = x_later + pens[p, n_pen + k] * in_x[k, 1:2, :]
    rest = rest + ends[:, 0:1] * x_earlier + ends[:, 1:2] * x_later
    for copy in copies_c:
        copy.wait_recv()
    values = (in_c[...].reshape(nx, nz) + rest).T
    coarse[...] = values
    store_coarse = pltpu.make_async_copy(coarse, coarse_hbm.at[0], store_sem.at[1])
    store_coarse.start()
    high, low = parts(values)
    spread = dot(select_z, high) + dot(select_z, low)
    high, low = parts(spread)
    fine[0] = fine[0] + dot(high, select_x) + dot(low, select_x)
    store_even = pltpu.make_async_copy(fine.at[0], fine_hbm.at[0], store_sem.at[2])
    store_even.start()

    for copy in copies_a + copies_b + copies_c + copies_x + [copy_h1, copy_h2]:
        copy.wait_send()
    store_odd.wait()
    store_coarse.wait()
    store_even.wait()


def tables(slabs, n_pen, nx, nz):
    groups = slabs // GROUP
    bx = Blocks(nx * n_pen, n_pen)
    by = Blocks(slabs, groups)
    bz = Blocks(nz, 1)

    pz_high, pz_low = split(bz.diagonal[0].T)
    select = np.zeros((2 * nz, nz))
    select[2 * np.arange(nz), np.arange(nz)] = 1.0
    inner = refine_matrix(nx)
    inner[2 * nx - 1, nx - 1] = 0.5
    fixed = np.stack(
        [pz_high, pz_low, split(select)[0], split(inner)[0], split(refine_matrix(nz))[0]]
    )

    left = np.zeros((n_pen, 2, 2 * nx + 16, 2 * nx), ml_dtypes.bfloat16)
    ends = np.zeros((n_pen, nx, 128), np.float32)
    pens = np.zeros((n_pen, 2 * n_pen + 4), np.float32)
    for b in range(n_pen):
        states = np.zeros((16, 2 * nx))
        states[0] = states[10] = bx.to_later[b]
        states[1] = states[11] = bx.to_earlier[b]
        block = split(np.concatenate([bx.diagonal[b], states]))
        left[b, 0, : nx + 16], left[b, 1, : nx + 16] = block
        left[b, 0, nx + 16 + np.arange(nx), 2 * np.arange(nx)] = 1.0
        ends[b, :, 0] = bx.falling[b]
        ends[b, :, 1] = bx.rising[b]
        pens[b, :n_pen] = bx.from_earlier[b]
        pens[b, n_pen : 2 * n_pen] = bx.from_later[b]
        if b == 0:
            ends[b, :, 2] = -bx.own_first / 3.0
            pens[b, 2 * n_pen] = -bx.first_to_later / 3.0
        if b == n_pen - 1:
            ends[b, :, 3] = bx.own_last * 2.0 / 3.0
            pens[b, 2 * n_pen + 3] = bx.last_to_earlier * 2.0 / 3.0

    at = Scalars(groups)
    table = np.zeros((groups, at.size), np.float32)
    for b in range(groups):
        table[b, at.local : at.to_later] = by.diagonal[b].reshape(-1)
        table[b, at.to_later : at.to_earlier] = by.to_later[b]
        table[b, at.to_earlier : at.falling] = by.to_earlier[b]
        table[b, at.falling : at.rising] = by.falling[b]
        table[b, at.rising : at.from_earlier] = by.rising[b]
        table[b, at.from_earlier : at.from_later] = by.from_earlier[b]
        table[b, at.from_later :] = by.from_later[b]

    inverse = inverse_mass(nz)
    lift = np.zeros((8, nz), np.float32)
    lift[0] = inverse[:, 0] / 3.0
    lift[1] = inverse[:, -1] * (-2.0 / 3.0)
    return at, fixed, left, ends, table, pens, lift


def per_device(slabs, n_pen, density):
    nz, nx = density.shape[1] // 2, density.shape[2] // 2
    groups = slabs // GROUP
    part = nx // GROUP
    at, fixed, left, ends, table, pens, lift = tables(slabs, n_pen, nx, nz)
    anywhere = pl.BlockSpec(memory_space=pl.ANY)
    scalars = pl.BlockSpec(memory_space=pltpu.SMEM)
    vector = pl.BlockSpec(memory_space=pltpu.VMEM)
    dma = pltpu.SemaphoreType.DMA

    def body(u_hbm, fixed_hbm, left_hbm, ends_hbm, table, pens, lift, fine_hbm, coarse_hbm, *rest):
        (u, fixed, left, ends, coarse_t, halo_in, halo_out, next_c, *more) = rest
        kernel(
            (slabs, n_pen, groups, nx, nz, at),
            u_hbm, fixed_hbm, left_hbm, ends_hbm, table, pens, fine_hbm, coarse_hbm,
            u, fixed, left, ends, coarse_t, halo_in, halo_out, next_c, lift, *more,
        )

    return pl.pallas_call(
        body,
        out_shape=(
            jax.ShapeDtypeStruct(density.shape, F32),
            jax.ShapeDtypeStruct((1, nz, nx), F32),
        ),
        in_specs=[anywhere, anywhere, anywhere, anywhere, scalars, scalars, vector],
        out_specs=(anywhere, anywhere),
        scratch_shapes=[
            pltpu.VMEM(density.shape, F32),
            pltpu.VMEM(fixed.shape, BF16),
            pltpu.VMEM(left.shape[1:], BF16),
            pltpu.VMEM(ends.shape[1:], F32),
            pltpu.VMEM((nx + 8, nz), F32),
            pltpu.VMEM((8, nz), F32),
            pltpu.VMEM((8, nz), F32),
            pltpu.VMEM((nx + 8, nz), F32),
            pltpu.VMEM((GROUP, 2 * part + STATE_ROWS, nz), F32),
            pltpu.VMEM((GROUP, 2 * part + STATE_ROWS, nz), F32),
            pltpu.VMEM((2, part + STATE_ROWS, nz), F32),
            pltpu.VMEM((groups, part + STATE_ROWS, nz), F32),
            pltpu.VMEM((GROUP, part, nz), F32),
            pltpu.VMEM((GROUP, part, nz), F32),
            pltpu.VMEM((STATE_ROWS, nz), F32),
            pltpu.VMEM((n_pen, STATE_ROWS, nz), F32),
            pltpu.VMEM(density.shape, F32),
            pltpu.VMEM((nz, nx), F32),
            dma((4,)),
            dma((3,)),
            dma, dma, dma, dma,
            dma((GROUP,)), dma((GROUP,)), dma((groups,)), dma((groups,)),
            dma((GROUP,)), dma((GROUP,)), dma((n_pen,)), dma((n_pen,)),
        ],
        compiler_params=pltpu.CompilerParams(
            collective_id=0, has_side_effects=True, vmem_limit_bytes=32 * 1024 * 1024
        ),
        name="decompose",
    )(density, fixed, left, ends, table, pens, lift)


def solution(mesh):
    slabs, n_pen = mesh.shape["slab"], mesh.shape["pen"]
    return jax.shard_map(
        functools.partial(per_device, slabs, n_pen),
        mesh=mesh,
        in_specs=(P("slab", None, "pen"),),
        out_specs=(P("slab", None, "pen"), P("slab", None, "pen")),
        check_vma=False,
    )
```

```python
import functools
import math

import jax
import jax.numpy as jnp
import ml_dtypes
import numpy as np
from jax import lax
from jax.experimental import pallas as pl
from jax.experimental.pallas import tpu as pltpu
from jax.sharding import PartitionSpec as P

MESH = pl.DeviceIdType.MESH
DECAY = math.log(2.0 + math.sqrt(3.0))
GROUP = 8
STATE_ROWS = 8
F32 = jnp.float32
BF16 = jnp.bfloat16


def inverse_mass(m):
    i = np.arange(m)[:, None]
    j = np.arange(m)[None, :]
    low, high = np.minimum(i, j), np.maximum(i, j)
    sign = np.where((high - low) % 2 == 0, 1.0, -1.0)
    ends = (1 - np.exp(-2 * (low + 1) * DECAY)) * (1 - np.exp(-2 * (m - high) * DECAY))
    scale = 3.0 / (2 * math.sqrt(3.0) * (1 - np.exp(-2 * (m + 1) * DECAY)))
    return scale * sign * np.exp(-(high - low) * DECAY) * ends


def refine_matrix(m):
    matrix = np.zeros((2 * m, m))
    j = np.arange(m)
    matrix[2 * j, j] = 1.0
    matrix[2 * j[:-1] + 1, j[:-1]] = 0.5
    matrix[2 * j[:-1] + 1, j[:-1] + 1] = 0.5
    matrix[2 * m - 1, m - 1] = 1.0
    return matrix


def project_matrix(m):
    j = np.arange(m)
    load = np.zeros((m, 2 * m + 2))
    w = np.where(j == m - 1, 1.0, 0.5)
    for offset, weight in ((-2, 0.5), (-1, 3.0), (0, 5.0), (1, 3.0), (2, 0.5)):
        keep = 2 * j + offset >= 0
        load[j[keep], 2 * j[keep] + offset] = weight / 6.0
    load[0, 0] = 4.5 / 6.0
    load[m - 1, 2 * m - 2] = (4.0 + w[-1] + 0.5) / 6.0
    load[m - 1, 2 * m - 1] = (1.0 + 4.0 * w[-1]) / 6.0
    return inverse_mass(m) @ load[:, : 2 * m]


def falling(m, i, start):
    d = i - start
    sign = np.where(d % 2 == 0, 1.0, -1.0)
    ends = (1 - np.exp(-2.0 * (m - i) * DECAY)) / (1 - np.exp(-2.0 * (m - start) * DECAY))
    return sign * np.exp(-d * DECAY) * ends


def rising(m, i, start):
    d = start - i
    sign = np.where(d % 2 == 0, 1.0, -1.0)
    ends = (1 - np.exp(-2.0 * (i + 1) * DECAY)) / (1 - np.exp(-2.0 * (start + 1) * DECAY))
    return sign * np.exp(-d * DECAY) * ends


class Blocks:
    def __init__(self, m, n):
        whole = project_matrix(m)
        size = m // n
        rows = np.arange(size)
        self.diagonal = np.stack(
            [whole[b * size : (b + 1) * size, 2 * b * size : 2 * (b + 1) * size] for b in range(n)]
        )
        self.to_later = np.zeros((n, 2 * size))
        self.to_earlier = np.zeros((n, 2 * size))
        self.later_first = np.zeros(n)
        self.earlier_last = np.zeros(n)
        self.falling = np.zeros((n, size))
        self.rising = np.zeros((n, size))
        self.from_earlier = np.zeros((n, n))
        self.from_later = np.zeros((n, n))
        inverse = inverse_mass(m)
        self.own_first = inverse[:size, 0]
        self.own_last = inverse[m - size :, m - 1]
        for b in range(n):
            columns = slice(2 * b * size, 2 * (b + 1) * size)
            first, last = b * size, (b + 1) * size - 1
            if b < n - 1:
                self.to_later[b] = whole[last + 1, columns]
            if b > 0:
                self.to_earlier[b] = whole[first - 1, columns]
            self.falling[b] = falling(m, first + rows, first)
            self.rising[b] = rising(m, first + rows, last)
            for c in range(n):
                if c < b:
                    self.from_earlier[b, c] = falling(m, first, (c + 1) * size)
                if c > b:
                    self.from_later[b, c] = rising(m, last, c * size - 1)
        self.first_to_later = inverse[size, 0] if n > 1 else 0.0
        self.last_to_earlier = inverse[m - size - 1, m - 1] if n > 1 else 0.0


def split(matrix):
    matrix = np.asarray(matrix, np.float32)
    high = matrix.astype(ml_dtypes.bfloat16)
    low = (matrix - high.astype(np.float32)).astype(ml_dtypes.bfloat16)
    return high, low


def parts(value):
    high = value.astype(BF16)
    return high, (value - high.astype(F32)).astype(BF16)


def dot(a, b, transposed=False):
    dims = (((1,), (1 if transposed else 0,)), ((), ()))
    return lax.dot_general(a, b, dims, preferred_element_type=F32)


def dot3(a, b, transposed=False):
    return (
        dot(a[0], b[0], transposed) + dot(a[0], b[1], transposed) + dot(a[1], b[0], transposed)
    )


class Scalars:
    def __init__(self, groups):
        g = GROUP
        self.local = 0
        self.to_later = self.local + 2 * g * g
        self.to_earlier = self.to_later + 2 * g
        self.falling = self.to_earlier + 2 * g
        self.rising = self.falling + g
        self.from_earlier = self.rising + g
        self.from_later = self.from_earlier + groups
        self.size = self.from_later + groups


def kernel(
    sizes,
    u_hbm, fixed_hbm, left_hbm, ends_hbm, table_hbm,
    fine_hbm, coarse_hbm,
    u, fixed, left, ends, table, coarse_t, halo_in, halo_out, next_c,
    out_a, in_a, out_b, in_b, out_c, in_c, out_x, in_x,
    fine, coarse,
    load_sem, store_sem,
    h1_send, h1_recv, h2_send, h2_recv,
    onward, a_send, a_recv, b_send, b_recv, c_send, c_recv, x_send, x_recv,
):
    slabs, n_pen, groups, nx, nz, at = sizes
    part = nx // GROUP
    s = lax.axis_index("slab")
    p = lax.axis_index("pen")
    g = s // GROUP
    m = lax.rem(s, GROUP)

    loads = [
        pltpu.make_async_copy(u_hbm, u, load_sem.at[0]),
        pltpu.make_async_copy(fixed_hbm, fixed, load_sem.at[1]),
        pltpu.make_async_copy(left_hbm.at[p], left, load_sem.at[2]),
        pltpu.make_async_copy(ends_hbm.at[p], ends, load_sem.at[3]),
        pltpu.make_async_copy(table_hbm, table, load_sem.at[4]),
    ]
    for load in loads:
        load.start()

    turns = groups // 2
    turn, side = lax.rem(g, turns), g // turns

    def group_at(ahead, flips):
        return lax.rem(side + flips, 2) * turns + lax.rem(turn + ahead, turns)

    steps = sorted(range(turns), key=lambda k: -min(k, turns - k))
    far_first = [(k, flips) for k in steps for flips in (1, 0) if (k, flips) != (0, 0)]
    near = [(k, flips) for k, flips in far_first if min(k, turns - k) <= 1]
    members = [(g * GROUP + lax.rem(m + k, GROUP), p) for k in range(1, GROUP)]
    others = [(group_at(*step) * GROUP + m, p) for step in near]
    peers = [(s, lax.rem(p + k, n_pen)) for k in range(1, n_pen)]
    above = (lax.rem(s + 1, slabs), p)
    below = (lax.rem(s + slabs - 1, slabs), p)
    barrier = pltpu.get_barrier_semaphore()
    greeted = others + peers + members + [above]
    for device in greeted:
        pl.semaphore_signal(barrier, inc=1, device_id=device, device_id_type=MESH)

    for load in loads:
        load.wait()

    u0 = parts(u[0])
    u1 = parts(u[1])
    lx = (left[0, : nx + 16], left[1, : nx + 16])
    select_x = left[0, nx + 16 :]
    pz = (fixed[0], fixed[1])
    select_z = fixed[2]
    t0 = dot3(lx, u0, True)
    tc = dot(select_x, u0[0], True) + dot(select_x, u0[1], True)
    t1 = dot3(lx, u1, True)
    y0 = dot3(parts(t0), pz)
    y1 = dot3(parts(t1), pz)
    tc = parts(tc)
    c = dot(tc[0], select_z) + dot(tc[1], select_z)
    coarse_t[:nx, :] = c

    def pen(k):
        return table[groups + p, k]

    z_ends = ends[nx : nx + 1, :], ends[nx + 1 : nx + 2, :]
    d = c[:, 0:1] * z_ends[0] + c[:, nz - 1 : nz] * z_ends[1]
    cz = c - d
    cz_first, cz_last = cz[0:1, :], cz[nx - 1 : nx, :]
    ex = ends[:nx, 2:3] * cz_first + ends[:nx, 3:4] * cz_last
    rows8 = lax.broadcasted_iota(jnp.int32, (STATE_ROWS, nz), 0)
    czx_state = jnp.where(
        rows8 == 0,
        pen(2 * n_pen) * cz_first + pen(2 * n_pen + 1) * cz_last,
        pen(2 * n_pen + 2) * cz_first + pen(2 * n_pen + 3) * cz_last,
    )
    czx = cz + ex
    s0 = jnp.where(s == 0, F32(0.5), F32(0.0))
    s1 = jnp.where(s == 0, F32(-1.0 / 12.0), jnp.where(s == slabs - 1, F32(-0.8), F32(0.0)))
    p0 = y0[:nx] + s0 * czx
    p1 = y1[:nx] + s1 * czx
    n0 = y0[nx : nx + STATE_ROWS] + s0 * czx_state
    n1 = y1[nx + STATE_ROWS : nx + 2 * STATE_ROWS] + s1 * jnp.roll(czx_state, 2, 0)
    out_a[:, 0:part, :] = p0.reshape(GROUP, part, nz)
    out_a[:, part : 2 * part, :] = p1.reshape(GROUP, part, nz)
    out_a[:, 2 * part :, :] = jnp.broadcast_to(
        jnp.where(rows8 < 2, n0, n1)[None], (GROUP, STATE_ROWS, nz)
    )
    in_a[m] = out_a[m]
    halo_out[...] = c[0:8, :]

    pl.semaphore_wait(barrier, len(greeted))

    copies_a = []
    for k in range(1, GROUP):
        to = lax.rem(m + k, GROUP)
        copy = pltpu.make_async_remote_copy(
            src_ref=out_a.at[to], dst_ref=in_a.at[m], send_sem=a_send.at[k], recv_sem=a_recv.at[k],
            device_id=(g * GROUP + to, p), device_id_type=MESH,
        )
        copy.start()
        copies_a.append(copy)
    behind = (group_at(turns - 1, 0) * GROUP + m, p)
    pl.semaphore_signal(onward, inc=1, device_id=behind, device_id_type=MESH)
    copy_h1 = pltpu.make_async_remote_copy(
        src_ref=halo_out, dst_ref=halo_in, send_sem=h1_send, recv_sem=h1_recv,
        device_id=(s, lax.rem(p + n_pen - 1, n_pen)), device_id_type=MESH,
    )
    copy_h1.start()

    in_b[g] = jnp.zeros((part + STATE_ROWS, nz), F32)
    rest = d - ex

    copy_h1.wait_recv()
    halo = jnp.where(p == n_pen - 1, c[nx - 1 : nx, :], halo_in[0:1, :])
    coarse_t[nx : nx + 8, :] = jnp.broadcast_to(halo, (8, nz))
    copy_h2 = pltpu.make_async_remote_copy(
        src_ref=coarse_t, dst_ref=next_c, send_sem=h2_send, recv_sem=h2_recv,
        device_id=below, device_id_type=MESH,
    )
    copy_h2.start()

    fine_rows = lax.broadcasted_iota(jnp.int32, (2 * nx, nz), 0)

    def interpolant(values, beyond):
        high, low = parts(values)
        along_x = dot(fixed[3], high) + dot(fixed[3], low)
        along_x = along_x + jnp.where(fine_rows == 2 * nx - 1, 0.5 * beyond, 0.0)
        high, low = parts(along_x)
        return dot(fixed[4], high, True) + dot(fixed[4], low, True)

    zi = lax.broadcasted_iota(jnp.int32, (2 * nz, 2 * nx), 0)
    xi = lax.broadcasted_iota(jnp.int32, (2 * nz, 2 * nx), 1)
    kept = ((zi | xi) & 1) == 0
    fine[0] = jnp.where(kept, 0.0, u[0] - interpolant(c, halo))

    for copy in copies_a:
        copy.wait_recv()

    def weigh(base, step, count, get):
        total = table[g, base] * get(0)
        for k in range(1, count):
            total = total + table[g, base + k * step] * get(k)
        return total

    def plane(k):
        return in_a[k // 2, (k % 2) * part : (k % 2 + 1) * part, :]

    def state(k):
        return in_a[k, 2 * part :, :]

    def states(base):
        even = weigh(base, 2, GROUP, state)
        odd = weigh(base + 1, 2, GROUP, state)
        return even + jnp.roll(odd, STATE_ROWS - 2, 0)

    for way, base in ((0, at.to_later), (1, at.to_earlier)):
        out_b[way, :part, :] = weigh(base, 1, 2 * GROUP, plane)
        out_b[way, part:, :] = states(base)
    pl.semaphore_wait(onward, 1)
    copies_b = []
    for k, step in enumerate(far_first):
        to = group_at(*step)
        copy = pltpu.make_async_remote_copy(
            src_ref=out_b.at[jnp.where(to > g, 0, 1)], dst_ref=in_b.at[g],
            send_sem=b_send.at[k], recv_sem=b_recv.at[k],
            device_id=(to * GROUP + m, p), device_id_type=MESH,
        )
        copy.start()
        copies_b.append(copy)

    for i in range(GROUP):
        out_c[i] = weigh(at.local + 2 * GROUP * i, 1, 2 * GROUP, plane)
    own_states = states(at.local + 2 * GROUP * m)

    copy_h2.wait_recv()
    last = s == slabs - 1
    after = jnp.where(last, coarse_t[...], next_c[...])
    middle = 0.5 * (coarse_t[...] + after)
    fine[1] = u[1] - interpolant(middle[:nx], middle[nx : nx + 1])
    store_odd = pltpu.make_async_copy(fine.at[1], fine_hbm.at[1], store_sem.at[0])
    store_odd.start()

    for copy in copies_b:
        copy.wait_recv()
    from_earlier = weigh(at.from_earlier, 1, groups, lambda k: in_b[k])
    from_later = weigh(at.from_later, 1, groups, lambda k: in_b[k])
    own_states = (
        own_states
        + table[g, at.falling + m] * from_earlier[part:]
        + table[g, at.rising + m] * from_later[part:]
        - czx_state
    )
    out_x[...] = own_states
    copies_x = []
    for k in range(1, n_pen):
        copy = pltpu.make_async_remote_copy(
            src_ref=out_x, dst_ref=in_x.at[p], send_sem=x_send.at[k], recv_sem=x_recv.at[k],
            device_id=(s, lax.rem(p + k, n_pen)), device_id_type=MESH,
        )
        copy.start()
        copies_x.append(copy)
    for i in range(GROUP):
        out_c[i] = (
            out_c[i]
            + table[g, at.falling + i] * from_earlier[:part]
            + table[g, at.rising + i] * from_later[:part]
        )
    copies_c = []
    for k in range(1, GROUP):
        to = lax.rem(m + k, GROUP)
        copy = pltpu.make_async_remote_copy(
            src_ref=out_c.at[to], dst_ref=in_c.at[m], send_sem=c_send.at[k], recv_sem=c_recv.at[k],
            device_id=(g * GROUP + to, p), device_id_type=MESH,
        )
        copy.start()
        copies_c.append(copy)
    in_c[m] = out_c[m]
    in_x[p] = out_x[...]

    for copy in copies_x:
        copy.wait_recv()
    x_earlier = pen(0) * in_x[0, 0:1, :]
    x_later = pen(n_pen) * in_x[0, 1:2, :]
    for k in range(1, n_pen):
        x_earlier = x_earlier + pen(k) * in_x[k, 0:1, :]
        x_later = x_later + pen(n_pen + k) * in_x[k, 1:2, :]
    rest = rest + ends[:nx, 0:1] * x_earlier + ends[:nx, 1:2] * x_later
    for copy in copies_c:
        copy.wait_recv()
    values = (in_c[...].reshape(nx, nz) + rest).T
    coarse[...] = values
    store_coarse = pltpu.make_async_copy(coarse, coarse_hbm.at[0], store_sem.at[1])
    store_coarse.start()
    high, low = parts(values)
    spread = dot(select_z, high) + dot(select_z, low)
    high, low = parts(spread)
    fine[0] = fine[0] + dot(high, select_x) + dot(low, select_x)
    store_even = pltpu.make_async_copy(fine.at[0], fine_hbm.at[0], store_sem.at[2])
    store_even.start()

    for copy in copies_a + copies_b + copies_c + copies_x + [copy_h1, copy_h2]:
        copy.wait_send()
    store_odd.wait()
    store_coarse.wait()
    store_even.wait()


def tables(slabs, n_pen, nx, nz):
    groups = slabs // GROUP
    bx = Blocks(nx * n_pen, n_pen)
    by = Blocks(slabs, groups)
    bz = Blocks(nz, 1)

    pz_high, pz_low = split(bz.diagonal[0].T)
    select = np.zeros((2 * nz, nz))
    select[2 * np.arange(nz), np.arange(nz)] = 1.0
    inner = refine_matrix(nx)
    inner[2 * nx - 1, nx - 1] = 0.5
    fixed = np.stack(
        [pz_high, pz_low, split(select)[0], split(inner)[0], split(refine_matrix(nz))[0]]
    )

    left = np.zeros((n_pen, 2, 2 * nx + 16, 2 * nx), ml_dtypes.bfloat16)
    inverse = inverse_mass(nz)
    ends = np.zeros((n_pen, nx + 8, nz), np.float32)
    ends[:, nx] = inverse[:, 0] / 3.0
    ends[:, nx + 1] = inverse[:, -1] * (-2.0 / 3.0)
    pens = np.zeros((n_pen, 2 * n_pen + 4), np.float32)
    for b in range(n_pen):
        states = np.zeros((16, 2 * nx))
        states[0] = states[10] = bx.to_later[b]
        states[1] = states[11] = bx.to_earlier[b]
        block = split(np.concatenate([bx.diagonal[b], states]))
        left[b, 0, : nx + 16], left[b, 1, : nx + 16] = block
        left[b, 0, nx + 16 + np.arange(nx), 2 * np.arange(nx)] = 1.0
        ends[b, :nx, 0] = bx.falling[b]
        ends[b, :nx, 1] = bx.rising[b]
        pens[b, :n_pen] = bx.from_earlier[b]
        pens[b, n_pen : 2 * n_pen] = bx.from_later[b]
        if b == 0:
            ends[b, :nx, 2] = -bx.own_first / 3.0
            pens[b, 2 * n_pen] = -bx.first_to_later / 3.0
        if b == n_pen - 1:
            ends[b, :nx, 3] = bx.own_last * 2.0 / 3.0
            pens[b, 2 * n_pen + 3] = bx.last_to_earlier * 2.0 / 3.0

    at = Scalars(groups)
    table = np.zeros((groups + n_pen, at.size), np.float32)
    table[groups:, : pens.shape[1]] = pens
    for b in range(groups):
        table[b, at.local : at.to_later] = by.diagonal[b].reshape(-1)
        table[b, at.to_later : at.to_earlier] = by.to_later[b]
        table[b, at.to_earlier : at.falling] = by.to_earlier[b]
        table[b, at.falling : at.rising] = by.falling[b]
        table[b, at.rising : at.from_earlier] = by.rising[b]
        table[b, at.from_earlier : at.from_later] = by.from_earlier[b]
        table[b, at.from_later :] = by.from_later[b]
    return at, fixed, left, ends, table


def per_device(slabs, n_pen, density):
    nz, nx = density.shape[1] // 2, density.shape[2] // 2
    groups = slabs // GROUP
    part = nx // GROUP
    at, fixed, left, ends, table = tables(slabs, n_pen, nx, nz)
    anywhere = pl.BlockSpec(memory_space=pl.ANY)
    dma = pltpu.SemaphoreType.DMA
    return pl.pallas_call(
        functools.partial(kernel, (slabs, n_pen, groups, nx, nz, at)),
        out_shape=(
            jax.ShapeDtypeStruct(density.shape, F32),
            jax.ShapeDtypeStruct((1, nz, nx), F32),
        ),
        in_specs=[pl.BlockSpec(memory_space=pltpu.HBM)] * 5,
        out_specs=(anywhere, anywhere),
        scratch_shapes=[
            pltpu.VMEM(density.shape, F32),
            pltpu.VMEM(fixed.shape, BF16),
            pltpu.VMEM(left.shape[1:], BF16),
            pltpu.VMEM(ends.shape[1:], F32),
            pltpu.SMEM(table.shape, F32),
            pltpu.VMEM((nx + 8, nz), F32),
            pltpu.VMEM((8, nz), F32),
            pltpu.VMEM((8, nz), F32),
            pltpu.VMEM((nx + 8, nz), F32),
            pltpu.VMEM((GROUP, 2 * part + STATE_ROWS, nz), F32),
            pltpu.VMEM((GROUP, 2 * part + STATE_ROWS, nz), F32),
            pltpu.VMEM((2, part + STATE_ROWS, nz), F32),
            pltpu.VMEM((groups, part + STATE_ROWS, nz), F32),
            pltpu.VMEM((GROUP, part, nz), F32),
            pltpu.VMEM((GROUP, part, nz), F32),
            pltpu.VMEM((STATE_ROWS, nz), F32),
            pltpu.VMEM((n_pen, STATE_ROWS, nz), F32),
            pltpu.VMEM(density.shape, F32),
            pltpu.VMEM((nz, nx), F32),
            dma((5,)),
            dma((3,)),
            dma, dma, dma, dma,
            pltpu.SemaphoreType.REGULAR,
            dma((GROUP,)), dma((GROUP,)), dma((groups,)), dma((groups,)),
            dma((GROUP,)), dma((GROUP,)), dma((n_pen,)), dma((n_pen,)),
        ],
        compiler_params=pltpu.CompilerParams(
            collective_id=0, has_side_effects=True, vmem_limit_bytes=32 * 1024 * 1024
        ),
        name="decompose",
    )(density, fixed, left, ends, table)


def solution(mesh):
    slabs, n_pen = mesh.shape["slab"], mesh.shape["pen"]
    return jax.shard_map(
        functools.partial(per_device, slabs, n_pen),
        mesh=mesh,
        in_specs=(P("slab", None, "pen"),),
        out_specs=(P("slab", None, "pen"), P("slab", None, "pen")),
        check_vma=False,
    )
```

```python
import functools
import math

import jax
import jax.numpy as jnp
import ml_dtypes
import numpy as np
from jax import lax
from jax.experimental import pallas as pl
from jax.experimental.pallas import tpu as pltpu
from jax.sharding import PartitionSpec as P

MESH = pl.DeviceIdType.MESH
DECAY = math.log(2.0 + math.sqrt(3.0))
GROUP = 8
STATE_ROWS = 8
F32 = jnp.float32
BF16 = jnp.bfloat16


def inverse_mass(m):
    i = np.arange(m)[:, None]
    j = np.arange(m)[None, :]
    low, high = np.minimum(i, j), np.maximum(i, j)
    sign = np.where((high - low) % 2 == 0, 1.0, -1.0)
    ends = (1 - np.exp(-2 * (low + 1) * DECAY)) * (1 - np.exp(-2 * (m - high) * DECAY))
    scale = 3.0 / (2 * math.sqrt(3.0) * (1 - np.exp(-2 * (m + 1) * DECAY)))
    return scale * sign * np.exp(-(high - low) * DECAY) * ends


def refine_matrix(m):
    matrix = np.zeros((2 * m, m))
    j = np.arange(m)
    matrix[2 * j, j] = 1.0
    matrix[2 * j[:-1] + 1, j[:-1]] = 0.5
    matrix[2 * j[:-1] + 1, j[:-1] + 1] = 0.5
    matrix[2 * m - 1, m - 1] = 1.0
    return matrix


def project_matrix(m):
    j = np.arange(m)
    load = np.zeros((m, 2 * m + 2))
    w = np.where(j == m - 1, 1.0, 0.5)
    for offset, weight in ((-2, 0.5), (-1, 3.0), (0, 5.0), (1, 3.0), (2, 0.5)):
        keep = 2 * j + offset >= 0
        load[j[keep], 2 * j[keep] + offset] = weight / 6.0
    load[0, 0] = 4.5 / 6.0
    load[m - 1, 2 * m - 2] = (4.0 + w[-1] + 0.5) / 6.0
    load[m - 1, 2 * m - 1] = (1.0 + 4.0 * w[-1]) / 6.0
    return inverse_mass(m) @ load[:, : 2 * m]


def falling(m, i, start):
    d = i - start
    sign = np.where(d % 2 == 0, 1.0, -1.0)
    ends = (1 - np.exp(-2.0 * (m - i) * DECAY)) / (1 - np.exp(-2.0 * (m - start) * DECAY))
    return sign * np.exp(-d * DECAY) * ends


def rising(m, i, start):
    d = start - i
    sign = np.where(d % 2 == 0, 1.0, -1.0)
    ends = (1 - np.exp(-2.0 * (i + 1) * DECAY)) / (1 - np.exp(-2.0 * (start + 1) * DECAY))
    return sign * np.exp(-d * DECAY) * ends


class Blocks:
    def __init__(self, m, n):
        whole = project_matrix(m)
        size = m // n
        rows = np.arange(size)
        self.diagonal = np.stack(
            [whole[b * size : (b + 1) * size, 2 * b * size : 2 * (b + 1) * size] for b in range(n)]
        )
        self.to_later = np.zeros((n, 2 * size))
        self.to_earlier = np.zeros((n, 2 * size))
        self.later_first = np.zeros(n)
        self.earlier_last = np.zeros(n)
        self.falling = np.zeros((n, size))
        self.rising = np.zeros((n, size))
        self.from_earlier = np.zeros((n, n))
        self.from_later = np.zeros((n, n))
        inverse = inverse_mass(m)
        self.own_first = inverse[:size, 0]
        self.own_last = inverse[m - size :, m - 1]
        for b in range(n):
            columns = slice(2 * b * size, 2 * (b + 1) * size)
            first, last = b * size, (b + 1) * size - 1
            if b < n - 1:
                self.to_later[b] = whole[last + 1, columns]
            if b > 0:
                self.to_earlier[b] = whole[first - 1, columns]
            self.falling[b] = falling(m, first + rows, first)
            self.rising[b] = rising(m, first + rows, last)
            for c in range(n):
                if c < b:
                    self.from_earlier[b, c] = falling(m, first, (c + 1) * size)
                if c > b:
                    self.from_later[b, c] = rising(m, last, c * size - 1)
        self.first_to_later = inverse[size, 0] if n > 1 else 0.0
        self.last_to_earlier = inverse[m - size - 1, m - 1] if n > 1 else 0.0


def split(matrix):
    matrix = np.asarray(matrix, np.float32)
    high = matrix.astype(ml_dtypes.bfloat16)
    low = (matrix - high.astype(np.float32)).astype(ml_dtypes.bfloat16)
    return high, low


def parts(value):
    high = value.astype(BF16)
    return high, (value - high.astype(F32)).astype(BF16)


def dot(a, b, transposed=False):
    dims = (((1,), (1 if transposed else 0,)), ((), ()))
    return lax.dot_general(a, b, dims, preferred_element_type=F32)


def dot3(a, b, transposed=False):
    return (
        dot(a[0], b[0], transposed) + dot(a[0], b[1], transposed) + dot(a[1], b[0], transposed)
    )


class Scalars:
    def __init__(self, groups):
        g = GROUP
        self.local = 0
        self.to_later = self.local + 2 * g * g
        self.to_earlier = self.to_later + 2 * g
        self.falling = self.to_earlier + 2 * g
        self.rising = self.falling + g
        self.from_earlier = self.rising + g
        self.from_later = self.from_earlier + groups
        self.size = self.from_later + groups


def kernel(
    sizes,
    u_hbm, fixed_hbm, left_hbm, ends_hbm, table_hbm,
    fine, coarse,
    u, fixed, left, ends, table, coarse_t, halo_in, halo_out, next_c,
    out_a, in_a, out_b, in_b, out_c, in_c, out_x, in_x,
    load_sem,
    h1_send, h1_recv, h2_send, h2_recv,
    onward, a_send, a_recv, b_send, b_recv, c_send, c_recv, x_send, x_recv,
):
    slabs, n_pen, groups, nx, nz, at = sizes
    part = nx // GROUP
    s = lax.axis_index("slab")
    p = lax.axis_index("pen")
    g = s // GROUP
    m = lax.rem(s, GROUP)

    loads = [
        pltpu.make_async_copy(u_hbm, u, load_sem.at[0]),
        pltpu.make_async_copy(fixed_hbm, fixed, load_sem.at[1]),
        pltpu.make_async_copy(left_hbm.at[p], left, load_sem.at[2]),
        pltpu.make_async_copy(ends_hbm.at[p], ends, load_sem.at[3]),
        pltpu.make_async_copy(table_hbm, table, load_sem.at[4]),
    ]
    for load in loads:
        load.start()

    turns = groups // 2
    turn, side = lax.rem(g, turns), g // turns

    def group_at(ahead, flips):
        return lax.rem(side + flips, 2) * turns + lax.rem(turn + ahead, turns)

    steps = sorted(range(turns), key=lambda k: -min(k, turns - k))
    far_first = [(k, flips) for k in steps for flips in (1, 0) if (k, flips) != (0, 0)]
    near = [(k, flips) for k, flips in far_first if min(k, turns - k) <= 1]
    members = [(g * GROUP + lax.rem(m + k, GROUP), p) for k in range(1, GROUP)]
    others = [(group_at(*step) * GROUP + m, p) for step in near]
    peers = [(s, lax.rem(p + k, n_pen)) for k in range(1, n_pen)]
    above = (lax.rem(s + 1, slabs), p)
    below = (lax.rem(s + slabs - 1, slabs), p)
    barrier = pltpu.get_barrier_semaphore()
    greeted = others + peers + members + [above]
    for device in greeted:
        pl.semaphore_signal(barrier, inc=1, device_id=device, device_id_type=MESH)

    for load in loads:
        load.wait()

    u0 = parts(u[0])
    u1 = parts(u[1])
    lx = (left[0, : nx + 16], left[1, : nx + 16])
    select_x = left[0, nx + 16 :]
    pz = (fixed[0], fixed[1])
    select_z = fixed[2]
    t0 = dot3(lx, u0, True)
    tc = dot(select_x, u0[0], True) + dot(select_x, u0[1], True)
    t1 = dot3(lx, u1, True)
    y0 = dot3(parts(t0), pz)
    y1 = dot3(parts(t1), pz)
    tc = parts(tc)
    c = dot(tc[0], select_z) + dot(tc[1], select_z)
    coarse_t[:nx, :] = c

    def pen(k):
        return table[groups + p, k]

    z_ends = ends[nx : nx + 1, :], ends[nx + 1 : nx + 2, :]
    d = c[:, 0:1] * z_ends[0] + c[:, nz - 1 : nz] * z_ends[1]
    cz = c - d
    cz_first, cz_last = cz[0:1, :], cz[nx - 1 : nx, :]
    ex = ends[:nx, 2:3] * cz_first + ends[:nx, 3:4] * cz_last
    rows8 = lax.broadcasted_iota(jnp.int32, (STATE_ROWS, nz), 0)
    czx_state = jnp.where(
        rows8 == 0,
        pen(2 * n_pen) * cz_first + pen(2 * n_pen + 1) * cz_last,
        pen(2 * n_pen + 2) * cz_first + pen(2 * n_pen + 3) * cz_last,
    )
    czx = cz + ex
    s0 = jnp.where(s == 0, F32(0.5), F32(0.0))
    s1 = jnp.where(s == 0, F32(-1.0 / 12.0), jnp.where(s == slabs - 1, F32(-0.8), F32(0.0)))
    p0 = y0[:nx] + s0 * czx
    p1 = y1[:nx] + s1 * czx
    n0 = y0[nx : nx + STATE_ROWS] + s0 * czx_state
    n1 = y1[nx + STATE_ROWS : nx + 2 * STATE_ROWS] + s1 * jnp.roll(czx_state, 2, 0)
    out_a[:, 0:part, :] = p0.reshape(GROUP, part, nz)
    out_a[:, part : 2 * part, :] = p1.reshape(GROUP, part, nz)
    out_a[:, 2 * part :, :] = jnp.broadcast_to(
        jnp.where(rows8 < 2, n0, n1)[None], (GROUP, STATE_ROWS, nz)
    )
    in_a[m] = out_a[m]
    halo_out[...] = c[0:8, :]

    pl.semaphore_wait(barrier, len(greeted))

    copies_a = []
    for k in range(1, GROUP):
        to = lax.rem(m + k, GROUP)
        copy = pltpu.make_async_remote_copy(
            src_ref=out_a.at[to], dst_ref=in_a.at[m], send_sem=a_send.at[k], recv_sem=a_recv.at[k],
            device_id=(g * GROUP + to, p), device_id_type=MESH,
        )
        copy.start()
        copies_a.append(copy)
    behind = (group_at(turns - 1, 0) * GROUP + m, p)
    pl.semaphore_signal(onward, inc=1, device_id=behind, device_id_type=MESH)
    copy_h1 = pltpu.make_async_remote_copy(
        src_ref=halo_out, dst_ref=halo_in, send_sem=h1_send, recv_sem=h1_recv,
        device_id=(s, lax.rem(p + n_pen - 1, n_pen)), device_id_type=MESH,
    )
    copy_h1.start()

    in_b[g] = jnp.zeros((part + STATE_ROWS, nz), F32)
    rest = d - ex

    copy_h1.wait_recv()
    halo = jnp.where(p == n_pen - 1, c[nx - 1 : nx, :], halo_in[0:1, :])
    coarse_t[nx : nx + 8, :] = jnp.broadcast_to(halo, (8, nz))
    copy_h2 = pltpu.make_async_remote_copy(
        src_ref=coarse_t, dst_ref=next_c, send_sem=h2_send, recv_sem=h2_recv,
        device_id=below, device_id_type=MESH,
    )
    copy_h2.start()

    fine_rows = lax.broadcasted_iota(jnp.int32, (2 * nx, nz), 0)

    def interpolant(values, beyond):
        high, low = parts(values)
        along_x = dot(fixed[3], high) + dot(fixed[3], low)
        along_x = along_x + jnp.where(fine_rows == 2 * nx - 1, 0.5 * beyond, 0.0)
        high, low = parts(along_x)
        return dot(fixed[4], high, True) + dot(fixed[4], low, True)

    zi = lax.broadcasted_iota(jnp.int32, (2 * nz, 2 * nx), 0)
    xi = lax.broadcasted_iota(jnp.int32, (2 * nz, 2 * nx), 1)
    kept = ((zi | xi) & 1) == 0
    fine[0] = jnp.where(kept, 0.0, u[0] - interpolant(c, halo))

    for copy in copies_a:
        copy.wait_recv()

    def weigh(base, step, count, get):
        total = table[g, base] * get(0)
        for k in range(1, count):
            total = total + table[g, base + k * step] * get(k)
        return total

    def plane(k):
        return in_a[k // 2, (k % 2) * part : (k % 2 + 1) * part, :]

    def state(k):
        return in_a[k, 2 * part :, :]

    def states(base):
        even = weigh(base, 2, GROUP, state)
        odd = weigh(base + 1, 2, GROUP, state)
        return even + jnp.roll(odd, STATE_ROWS - 2, 0)

    for way, base in ((0, at.to_later), (1, at.to_earlier)):
        out_b[way, :part, :] = weigh(base, 1, 2 * GROUP, plane)
        out_b[way, part:, :] = states(base)
    pl.semaphore_wait(onward, 1)
    copies_b = []
    for k, step in enumerate(far_first):
        to = group_at(*step)
        copy = pltpu.make_async_remote_copy(
            src_ref=out_b.at[jnp.where(to > g, 0, 1)], dst_ref=in_b.at[g],
            send_sem=b_send.at[k], recv_sem=b_recv.at[k],
            device_id=(to * GROUP + m, p), device_id_type=MESH,
        )
        copy.start()
        copies_b.append(copy)

    for i in range(GROUP):
        out_c[i] = weigh(at.local + 2 * GROUP * i, 1, 2 * GROUP, plane)
    own_states = states(at.local + 2 * GROUP * m)

    copy_h2.wait_recv()
    last = s == slabs - 1
    after = jnp.where(last, coarse_t[...], next_c[...])
    middle = 0.5 * (coarse_t[...] + after)
    fine[1] = u[1] - interpolant(middle[:nx], middle[nx : nx + 1])

    for copy in copies_b:
        copy.wait_recv()
    from_earlier = weigh(at.from_earlier, 1, groups, lambda k: in_b[k])
    from_later = weigh(at.from_later, 1, groups, lambda k: in_b[k])
    own_states = (
        own_states
        + table[g, at.falling + m] * from_earlier[part:]
        + table[g, at.rising + m] * from_later[part:]
        - czx_state
    )
    out_x[...] = own_states
    copies_x = []
    for k in range(1, n_pen):
        copy = pltpu.make_async_remote_copy(
            src_ref=out_x, dst_ref=in_x.at[p], send_sem=x_send.at[k], recv_sem=x_recv.at[k],
            device_id=(s, lax.rem(p + k, n_pen)), device_id_type=MESH,
        )
        copy.start()
        copies_x.append(copy)
    for i in range(GROUP):
        out_c[i] = (
            out_c[i]
            + table[g, at.falling + i] * from_earlier[:part]
            + table[g, at.rising + i] * from_later[:part]
        )
    copies_c = []
    for k in range(1, GROUP):
        to = lax.rem(m + k, GROUP)
        copy = pltpu.make_async_remote_copy(
            src_ref=out_c.at[to], dst_ref=in_c.at[m], send_sem=c_send.at[k], recv_sem=c_recv.at[k],
            device_id=(g * GROUP + to, p), device_id_type=MESH,
        )
        copy.start()
        copies_c.append(copy)
    in_c[m] = out_c[m]
    in_x[p] = out_x[...]

    for copy in copies_x:
        copy.wait_recv()
    x_earlier = pen(0) * in_x[0, 0:1, :]
    x_later = pen(n_pen) * in_x[0, 1:2, :]
    for k in range(1, n_pen):
        x_earlier = x_earlier + pen(k) * in_x[k, 0:1, :]
        x_later = x_later + pen(n_pen + k) * in_x[k, 1:2, :]
    rest = rest + ends[:nx, 0:1] * x_earlier + ends[:nx, 1:2] * x_later
    for copy in copies_c:
        copy.wait_recv()
    values = (in_c[...].reshape(nx, nz) + rest).T
    coarse[0] = values
    high, low = parts(values)
    spread = dot(select_z, high) + dot(select_z, low)
    high, low = parts(spread)
    fine[0] = fine[0] + dot(high, select_x) + dot(low, select_x)

    for copy in copies_a + copies_b + copies_c + copies_x + [copy_h1, copy_h2]:
        copy.wait_send()


def tables(slabs, n_pen, nx, nz):
    groups = slabs // GROUP
    bx = Blocks(nx * n_pen, n_pen)
    by = Blocks(slabs, groups)
    bz = Blocks(nz, 1)

    pz_high, pz_low = split(bz.diagonal[0].T)
    select = np.zeros((2 * nz, nz))
    select[2 * np.arange(nz), np.arange(nz)] = 1.0
    inner = refine_matrix(nx)
    inner[2 * nx - 1, nx - 1] = 0.5
    fixed = np.stack(
        [pz_high, pz_low, split(select)[0], split(inner)[0], split(refine_matrix(nz))[0]]
    )

    left = np.zeros((n_pen, 2, 2 * nx + 16, 2 * nx), ml_dtypes.bfloat16)
    inverse = inverse_mass(nz)
    ends = np.zeros((n_pen, nx + 8, nz), np.float32)
    ends[:, nx] = inverse[:, 0] / 3.0
    ends[:, nx + 1] = inverse[:, -1] * (-2.0 / 3.0)
    pens = np.zeros((n_pen, 2 * n_pen + 4), np.float32)
    for b in range(n_pen):
        states = np.zeros((16, 2 * nx))
        states[0] = states[10] = bx.to_later[b]
        states[1] = states[11] = bx.to_earlier[b]
        block = split(np.concatenate([bx.diagonal[b], states]))
        left[b, 0, : nx + 16], left[b, 1, : nx + 16] = block
        left[b, 0, nx + 16 + np.arange(nx), 2 * np.arange(nx)] = 1.0
        ends[b, :nx, 0] = bx.falling[b]
        ends[b, :nx, 1] = bx.rising[b]
        pens[b, :n_pen] = bx.from_earlier[b]
        pens[b, n_pen : 2 * n_pen] = bx.from_later[b]
        if b == 0:
            ends[b, :nx, 2] = -bx.own_first / 3.0
            pens[b, 2 * n_pen] = -bx.first_to_later / 3.0
        if b == n_pen - 1:
            ends[b, :nx, 3] = bx.own_last * 2.0 / 3.0
            pens[b, 2 * n_pen + 3] = bx.last_to_earlier * 2.0 / 3.0

    at = Scalars(groups)
    table = np.zeros((groups + n_pen, at.size), np.float32)
    table[groups:, : pens.shape[1]] = pens
    for b in range(groups):
        table[b, at.local : at.to_later] = by.diagonal[b].reshape(-1)
        table[b, at.to_later : at.to_earlier] = by.to_later[b]
        table[b, at.to_earlier : at.falling] = by.to_earlier[b]
        table[b, at.falling : at.rising] = by.falling[b]
        table[b, at.rising : at.from_earlier] = by.rising[b]
        table[b, at.from_earlier : at.from_later] = by.from_earlier[b]
        table[b, at.from_later :] = by.from_later[b]
    return at, fixed, left, ends, table


def per_device(slabs, n_pen, density):
    nz, nx = density.shape[1] // 2, density.shape[2] // 2
    groups = slabs // GROUP
    part = nx // GROUP
    at, fixed, left, ends, table = tables(slabs, n_pen, nx, nz)
    anywhere = pl.BlockSpec(memory_space=pl.ANY)
    vector = pl.BlockSpec(memory_space=pltpu.VMEM)
    dma = pltpu.SemaphoreType.DMA
    return pl.pallas_call(
        functools.partial(kernel, (slabs, n_pen, groups, nx, nz, at)),
        out_shape=(
            pltpu.VMEM(density.shape, F32),
            pltpu.VMEM((1, nz, nx), F32),
        ),
        in_specs=[anywhere] * 5,
        out_specs=(vector, vector),
        scratch_shapes=[
            pltpu.VMEM(density.shape, F32),
            pltpu.VMEM(fixed.shape, BF16),
            pltpu.VMEM(left.shape[1:], BF16),
            pltpu.VMEM(ends.shape[1:], F32),
            pltpu.SMEM(table.shape, F32),
            pltpu.VMEM((nx + 8, nz), F32),
            pltpu.VMEM((8, nz), F32),
            pltpu.VMEM((8, nz), F32),
            pltpu.VMEM((nx + 8, nz), F32),
            pltpu.VMEM((GROUP, 2 * part + STATE_ROWS, nz), F32),
            pltpu.VMEM((GROUP, 2 * part + STATE_ROWS, nz), F32),
            pltpu.VMEM((2, part + STATE_ROWS, nz), F32),
            pltpu.VMEM((groups, part + STATE_ROWS, nz), F32),
            pltpu.VMEM((GROUP, part, nz), F32),
            pltpu.VMEM((GROUP, part, nz), F32),
            pltpu.VMEM((STATE_ROWS, nz), F32),
            pltpu.VMEM((n_pen, STATE_ROWS, nz), F32),
            dma((5,)),
            dma, dma, dma, dma,
            pltpu.SemaphoreType.REGULAR,
            dma((GROUP,)), dma((GROUP,)), dma((groups,)), dma((groups,)),
            dma((GROUP,)), dma((GROUP,)), dma((n_pen,)), dma((n_pen,)),
        ],
        compiler_params=pltpu.CompilerParams(
            collective_id=0, has_side_effects=True, vmem_limit_bytes=32 * 1024 * 1024
        ),
        name="decompose",
    )(*[pltpu.with_memory_space_constraint(a, pltpu.HBM) for a in (density, fixed, left, ends, table)])


def solution(mesh):
    slabs, n_pen = mesh.shape["slab"], mesh.shape["pen"]
    return jax.shard_map(
        functools.partial(per_device, slabs, n_pen),
        mesh=mesh,
        in_specs=(P("slab", None, "pen"),),
        out_specs=(P("slab", None, "pen"), P("slab", None, "pen")),
        check_vma=False,
    )
```

```python
import functools
import math

import jax
import jax.numpy as jnp
import ml_dtypes
import numpy as np
from jax import lax
from jax.experimental import pallas as pl
from jax.experimental.pallas import tpu as pltpu
from jax.sharding import PartitionSpec as P

MESH = pl.DeviceIdType.MESH
DECAY = math.log(2.0 + math.sqrt(3.0))
GROUP = 8
STATE_ROWS = 8
F32 = jnp.float32
BF16 = jnp.bfloat16


def inverse_mass(m):
    i = np.arange(m)[:, None]
    j = np.arange(m)[None, :]
    low, high = np.minimum(i, j), np.maximum(i, j)
    sign = np.where((high - low) % 2 == 0, 1.0, -1.0)
    ends = (1 - np.exp(-2 * (low + 1) * DECAY)) * (1 - np.exp(-2 * (m - high) * DECAY))
    scale = 3.0 / (2 * math.sqrt(3.0) * (1 - np.exp(-2 * (m + 1) * DECAY)))
    return scale * sign * np.exp(-(high - low) * DECAY) * ends


def refine_matrix(m):
    matrix = np.zeros((2 * m, m))
    j = np.arange(m)
    matrix[2 * j, j] = 1.0
    matrix[2 * j[:-1] + 1, j[:-1]] = 0.5
    matrix[2 * j[:-1] + 1, j[:-1] + 1] = 0.5
    matrix[2 * m - 1, m - 1] = 1.0
    return matrix


def project_matrix(m):
    j = np.arange(m)
    load = np.zeros((m, 2 * m + 2))
    w = np.where(j == m - 1, 1.0, 0.5)
    for offset, weight in ((-2, 0.5), (-1, 3.0), (0, 5.0), (1, 3.0), (2, 0.5)):
        keep = 2 * j + offset >= 0
        load[j[keep], 2 * j[keep] + offset] = weight / 6.0
    load[0, 0] = 4.5 / 6.0
    load[m - 1, 2 * m - 2] = (4.0 + w[-1] + 0.5) / 6.0
    load[m - 1, 2 * m - 1] = (1.0 + 4.0 * w[-1]) / 6.0
    return inverse_mass(m) @ load[:, : 2 * m]


def falling(m, i, start):
    d = i - start
    sign = np.where(d % 2 == 0, 1.0, -1.0)
    ends = (1 - np.exp(-2.0 * (m - i) * DECAY)) / (1 - np.exp(-2.0 * (m - start) * DECAY))
    return sign * np.exp(-d * DECAY) * ends


def rising(m, i, start):
    d = start - i
    sign = np.where(d % 2 == 0, 1.0, -1.0)
    ends = (1 - np.exp(-2.0 * (i + 1) * DECAY)) / (1 - np.exp(-2.0 * (start + 1) * DECAY))
    return sign * np.exp(-d * DECAY) * ends


class Blocks:
    def __init__(self, m, n):
        whole = project_matrix(m)
        size = m // n
        rows = np.arange(size)
        self.diagonal = np.stack(
            [whole[b * size : (b + 1) * size, 2 * b * size : 2 * (b + 1) * size] for b in range(n)]
        )
        self.to_later = np.zeros((n, 2 * size))
        self.to_earlier = np.zeros((n, 2 * size))
        self.later_first = np.zeros(n)
        self.earlier_last = np.zeros(n)
        self.falling = np.zeros((n, size))
        self.rising = np.zeros((n, size))
        self.from_earlier = np.zeros((n, n))
        self.from_later = np.zeros((n, n))
        inverse = inverse_mass(m)
        self.own_first = inverse[:size, 0]
        self.own_last = inverse[m - size :, m - 1]
        for b in range(n):
            columns = slice(2 * b * size, 2 * (b + 1) * size)
            first, last = b * size, (b + 1) * size - 1
            if b < n - 1:
                self.to_later[b] = whole[last + 1, columns]
            if b > 0:
                self.to_earlier[b] = whole[first - 1, columns]
            self.falling[b] = falling(m, first + rows, first)
            self.rising[b] = rising(m, first + rows, last)
            for c in range(n):
                if c < b:
                    self.from_earlier[b, c] = falling(m, first, (c + 1) * size)
                if c > b:
                    self.from_later[b, c] = rising(m, last, c * size - 1)
        self.first_to_later = inverse[size, 0] if n > 1 else 0.0
        self.last_to_earlier = inverse[m - size - 1, m - 1] if n > 1 else 0.0


def split(matrix):
    matrix = np.asarray(matrix, np.float32)
    high = matrix.astype(ml_dtypes.bfloat16)
    low = (matrix - high.astype(np.float32)).astype(ml_dtypes.bfloat16)
    return high, low


def parts(value):
    high = value.astype(BF16)
    return high, (value - high.astype(F32)).astype(BF16)


def dot(a, b, transposed=False):
    dims = (((1,), (1 if transposed else 0,)), ((), ()))
    return lax.dot_general(a, b, dims, preferred_element_type=F32)


def dot3(a, b, transposed=False):
    return (
        dot(a[0], b[0], transposed) + dot(a[0], b[1], transposed) + dot(a[1], b[0], transposed)
    )


class Scalars:
    def __init__(self, groups):
        g = GROUP
        self.local = 0
        self.to_later = self.local + 2 * g * g
        self.to_earlier = self.to_later + 2 * g
        self.falling = self.to_earlier + 2 * g
        self.rising = self.falling + g
        self.from_earlier = self.rising + g
        self.from_later = self.from_earlier + groups
        self.size = self.from_later + groups


def kernel(
    sizes,
    u_hbm, left_hbm, pz_hbm, ends_hbm, table_hbm,
    fine, coarse, select,
    u, left, pz, ends, table, refine_x, refine_z, coarse_t, halo_in, halo_out, next_c,
    out_a, in_a, out_s, in_s, out_b, in_b, out_c, in_c, out_x, in_x,
    load_sem,
    h1_send, h1_recv, h2_send, h2_recv,
    onward, a_send, a_recv, s_send, s_recv, b_send, b_recv, c_send, c_recv, x_send, x_recv,
):
    slabs, n_pen, groups, nx, nz, at = sizes
    part = nx // GROUP
    s = lax.axis_index("slab")
    p = lax.axis_index("pen")
    g = s // GROUP
    m = lax.rem(s, GROUP)

    load_u0 = pltpu.make_async_copy(u_hbm.at[0], u.at[0], load_sem.at[0])
    load_left = pltpu.make_async_copy(left_hbm.at[p], left, load_sem.at[1])
    load_u1 = pltpu.make_async_copy(u_hbm.at[1], u.at[1], load_sem.at[2])
    load_pz = pltpu.make_async_copy(pz_hbm, pz, load_sem.at[3])
    load_ends = pltpu.make_async_copy(ends_hbm.at[p], ends, load_sem.at[4])
    load_table = pltpu.make_async_copy(table_hbm, table, load_sem.at[5])
    load_u0.start()
    load_left.start()

    turns = groups // 2
    turn, side = lax.rem(g, turns), g // turns

    def mirrored(member, at_turn):
        there = 2 * at_turn // turns
        return member + there * (GROUP - 2 - 2 * member + 2 * lax.rem(member, 2))

    held = mirrored(m, turn)

    def group_at(ahead, flips):
        return lax.rem(side + flips, 2) * turns + lax.rem(turn + ahead, turns)

    def partner(step):
        group = group_at(*step)
        return group, group * GROUP + mirrored(held, lax.rem(group, turns))

    steps = sorted(range(turns), key=lambda k: -min(k, turns - k))
    far_first = [(k, flips) for k in steps for flips in (1, 0) if (k, flips) != (0, 0)]
    near = [(k, flips) for k, flips in far_first if min(k, turns - k) <= 1]
    members = [(g * GROUP + lax.rem(m + k, GROUP), p) for k in range(1, GROUP)]
    others = [(partner(step)[1], p) for step in near]
    peers = [(s, lax.rem(p + k, n_pen)) for k in range(1, n_pen)]
    above = (lax.rem(s + 1, slabs), p)
    below = (lax.rem(s + slabs - 1, slabs), p)
    barrier = pltpu.get_barrier_semaphore()
    for device in members:
        pl.semaphore_signal(barrier, inc=1, device_id=device, device_id_type=MESH)
    for load in (load_u1, load_pz, load_ends, load_table):
        load.start()
    greeted = [above] + others + peers
    for device in greeted:
        pl.semaphore_signal(barrier, inc=1, device_id=device, device_id_type=MESH)

    def spread_matrix(m, weight):
        row = lax.broadcasted_iota(jnp.int32, (2 * m, m), 0)
        column = lax.broadcasted_iota(jnp.int32, (2 * m, m), 1)
        return weight(row, row - 2 * column).astype(BF16)

    def even(row, away):
        return jnp.where(away == 0, 1.0, 0.0)

    def inner(row, away):
        return jnp.where(away == 0, 1.0, jnp.where(jnp.abs(away) == 1, 0.5, 0.0))

    def ending(row, away):
        return jnp.where((row == 2 * nz - 1) & (away == 1), 1.0, inner(row, away))

    select[0] = spread_matrix(nz, even)
    select[1] = spread_matrix(nx, even)
    refine_x[...] = spread_matrix(nx, inner)
    refine_z[...] = spread_matrix(nz, ending)
    row = lax.broadcasted_iota(jnp.int32, (nx, 2 * nx), 0)
    column = lax.broadcasted_iota(jnp.int32, (nx, 2 * nx), 1)
    take_x = jnp.where(column == 2 * row, 1.0, 0.0).astype(BF16)

    load_u0.wait()
    load_left.wait()
    u0 = parts(u[0])
    lx = (left[0], left[1])
    t0 = dot3(lx, u0, True)
    tc = parts(dot(take_x, u0[0], True) + dot(take_x, u0[1], True))
    load_u1.wait()
    t1 = dot3(lx, parts(u[1]), True)
    load_pz.wait()
    to_z = (pz[0], pz[1])
    y0 = dot3(parts(t0), to_z)
    y1 = dot3(parts(t1), to_z)
    c = dot(tc[0], select[0]) + dot(tc[1], select[0])
    coarse_t[:nx, :] = c
    load_ends.wait()
    load_table.wait()

    def pen(k):
        return table[groups + p, k]

    z_ends = ends[nx : nx + 1, :], ends[nx + 1 : nx + 2, :]
    d = c[:, 0:1] * z_ends[0] + c[:, nz - 1 : nz] * z_ends[1]
    cz = c - d
    cz_first, cz_last = cz[0:1, :], cz[nx - 1 : nx, :]
    ex = ends[:nx, 2:3] * cz_first + ends[:nx, 3:4] * cz_last
    rows8 = lax.broadcasted_iota(jnp.int32, (STATE_ROWS, nz), 0)
    czx_state = jnp.where(
        rows8 == 0,
        pen(2 * n_pen) * cz_first + pen(2 * n_pen + 1) * cz_last,
        pen(2 * n_pen + 2) * cz_first + pen(2 * n_pen + 3) * cz_last,
    )
    czx = cz + ex
    s0 = jnp.where(s == 0, F32(0.5), F32(0.0))
    s1 = jnp.where(s == 0, F32(-1.0 / 12.0), jnp.where(s == slabs - 1, F32(-0.8), F32(0.0)))
    p0 = y0[:nx] + s0 * czx
    p1 = y1[:nx] + s1 * czx
    n0 = y0[nx : nx + STATE_ROWS] + s0 * czx_state
    n1 = y1[nx + STATE_ROWS : nx + 2 * STATE_ROWS] + s1 * jnp.roll(czx_state, 2, 0)
    out_a[:, 0:part, :] = p0.reshape(GROUP, part, nz)
    out_a[:, part : 2 * part, :] = p1.reshape(GROUP, part, nz)
    out_s[...] = jnp.where(rows8 < 2, n0, n1)[0:4]
    in_a[m] = out_a[held]
    in_s[m] = out_s[...]
    halo_out[...] = c[0:8, :]

    pl.semaphore_wait(barrier, len(members) + len(greeted))

    copies_a = []
    for k in range(1, GROUP):
        to = lax.rem(m + k, GROUP)
        copy = pltpu.make_async_remote_copy(
            src_ref=out_a.at[mirrored(to, turn)], dst_ref=in_a.at[m],
            send_sem=a_send.at[k], recv_sem=a_recv.at[k],
            device_id=(g * GROUP + to, p), device_id_type=MESH,
        )
        copy.start()
        copies_a.append(copy)
    for k in range(1, GROUP):
        copy = pltpu.make_async_remote_copy(
            src_ref=out_s, dst_ref=in_s.at[m], send_sem=s_send.at[k], recv_sem=s_recv.at[k],
            device_id=(g * GROUP + lax.rem(m + k, GROUP), p), device_id_type=MESH,
        )
        copy.start()
        copies_a.append(copy)
    behind = (partner((turns - 1, 0))[1], p)
    pl.semaphore_signal(onward, inc=1, device_id=behind, device_id_type=MESH)
    copy_h1 = pltpu.make_async_remote_copy(
        src_ref=halo_out, dst_ref=halo_in, send_sem=h1_send, recv_sem=h1_recv,
        device_id=(s, lax.rem(p + n_pen - 1, n_pen)), device_id_type=MESH,
    )
    copy_h1.start()

    in_b[g] = jnp.zeros((part + STATE_ROWS, nz), F32)
    rest = d - ex

    copy_h1.wait_recv()
    halo = jnp.where(p == n_pen - 1, c[nx - 1 : nx, :], halo_in[0:1, :])
    coarse_t[nx : nx + 8, :] = jnp.broadcast_to(halo, (8, nz))
    copy_h2 = pltpu.make_async_remote_copy(
        src_ref=coarse_t, dst_ref=next_c, send_sem=h2_send, recv_sem=h2_recv,
        device_id=below, device_id_type=MESH,
    )
    copy_h2.start()

    fine_rows = lax.broadcasted_iota(jnp.int32, (2 * nx, nz), 0)

    def interpolant(values, beyond):
        high, low = parts(values)
        along_x = dot(refine_x[...], high) + dot(refine_x[...], low)
        along_x = along_x + jnp.where(fine_rows == 2 * nx - 1, 0.5 * beyond, 0.0)
        high, low = parts(along_x)
        return dot(refine_z[...], high, True) + dot(refine_z[...], low, True)

    zi = lax.broadcasted_iota(jnp.int32, (2 * nz, 2 * nx), 0)
    xi = lax.broadcasted_iota(jnp.int32, (2 * nz, 2 * nx), 1)
    kept = ((zi | xi) & 1) == 0
    fine[0] = jnp.where(kept, 0.0, u[0] - interpolant(c, halo))

    for copy in copies_a:
        copy.wait_recv()

    def weigh(base, step, count, get):
        total = table[g, base] * get(0)
        for k in range(1, count):
            total = total + table[g, base + k * step] * get(k)
        return total

    def plane(k):
        return in_a[k // 2, (k % 2) * part : (k % 2 + 1) * part, :]

    def state(k):
        return in_s[k]

    def states(base):
        even = weigh(base, 2, GROUP, state)
        odd = weigh(base + 1, 2, GROUP, state)
        return jnp.concatenate([even[0:2] + odd[2:4]] * (STATE_ROWS // 2), 0)

    for way, base in ((0, at.to_later), (1, at.to_earlier)):
        out_b[way, :part, :] = weigh(base, 1, 2 * GROUP, plane)
        out_b[way, part:, :] = states(base)
    pl.semaphore_wait(onward, 1)
    copies_b = []
    for k, step in enumerate(far_first):
        to, device = partner(step)
        copy = pltpu.make_async_remote_copy(
            src_ref=out_b.at[jnp.where(to > g, 0, 1)], dst_ref=in_b.at[g],
            send_sem=b_send.at[k], recv_sem=b_recv.at[k],
            device_id=(device, p), device_id_type=MESH,
        )
        copy.start()
        copies_b.append(copy)

    for i in range(GROUP):
        out_c[i] = weigh(at.local + 2 * GROUP * i, 1, 2 * GROUP, plane)
    own_states = states(at.local + 2 * GROUP * m)

    copy_h2.wait_recv()
    last = s == slabs - 1
    after = jnp.where(last, coarse_t[...], next_c[...])
    middle = 0.5 * (coarse_t[...] + after)
    fine[1] = u[1] - interpolant(middle[:nx], middle[nx : nx + 1])

    for copy in copies_b:
        copy.wait_recv()
    from_earlier = weigh(at.from_earlier, 1, groups, lambda k: in_b[k])
    from_later = weigh(at.from_later, 1, groups, lambda k: in_b[k])
    own_states = (
        own_states
        + table[g, at.falling + m] * from_earlier[part:]
        + table[g, at.rising + m] * from_later[part:]
        - czx_state
    )
    out_x[...] = own_states
    copies_x = []
    for k in range(1, n_pen):
        copy = pltpu.make_async_remote_copy(
            src_ref=out_x, dst_ref=in_x.at[p], send_sem=x_send.at[k], recv_sem=x_recv.at[k],
            device_id=(s, lax.rem(p + k, n_pen)), device_id_type=MESH,
        )
        copy.start()
        copies_x.append(copy)
    for i in range(GROUP):
        out_c[i] = (
            out_c[i]
            + table[g, at.falling + i] * from_earlier[:part]
            + table[g, at.rising + i] * from_later[:part]
        )
    copies_c = []
    for k in range(1, GROUP):
        to = lax.rem(m + k, GROUP)
        copy = pltpu.make_async_remote_copy(
            src_ref=out_c.at[to], dst_ref=in_c.at[held], send_sem=c_send.at[k], recv_sem=c_recv.at[k],
            device_id=(g * GROUP + to, p), device_id_type=MESH,
        )
        copy.start()
        copies_c.append(copy)
    in_c[held] = out_c[m]
    in_x[p] = out_x[...]

    for copy in copies_x:
        copy.wait_recv()
    x_earlier = pen(0) * in_x[0, 0:1, :]
    x_later = pen(n_pen) * in_x[0, 1:2, :]
    for k in range(1, n_pen):
        x_earlier = x_earlier + pen(k) * in_x[k, 0:1, :]
        x_later = x_later + pen(n_pen + k) * in_x[k, 1:2, :]
    rest = rest + ends[:nx, 0:1] * x_earlier + ends[:nx, 1:2] * x_later
    for copy in copies_c:
        copy.wait_recv()
    coarse[...] = (in_c[...].reshape(nx, nz) + rest).T

    for copy in copies_a + copies_b + copies_c + copies_x + [copy_h1, copy_h2]:
        copy.wait_send()


def finish(part, coarse, select, fine_hbm, coarse_hbm, even, sem):
    odd_out = pltpu.make_async_copy(part.at[1], fine_hbm.at[1], sem.at[0])
    coarse_out = pltpu.make_async_copy(coarse, coarse_hbm.at[0], sem.at[1])
    odd_out.start()
    coarse_out.start()
    high, low = parts(coarse[...])
    high, low = parts(dot(select[0], high) + dot(select[0], low))
    even[...] = part[0] + dot(high, select[1], True) + dot(low, select[1], True)
    even_out = pltpu.make_async_copy(even, fine_hbm.at[0], sem.at[2])
    even_out.start()
    odd_out.wait()
    coarse_out.wait()
    even_out.wait()


def tables(slabs, n_pen, nx, nz):
    groups = slabs // GROUP
    bx = Blocks(nx * n_pen, n_pen)
    by = Blocks(slabs, groups)
    bz = Blocks(nz, 1)

    pz = np.stack(split(bz.diagonal[0].T))
    left = np.zeros((n_pen, 2, nx + 16, 2 * nx), ml_dtypes.bfloat16)
    inverse = inverse_mass(nz)
    ends = np.zeros((n_pen, nx + 8, nz), np.float32)
    ends[:, nx] = inverse[:, 0] / 3.0
    ends[:, nx + 1] = inverse[:, -1] * (-2.0 / 3.0)
    pens = np.zeros((n_pen, 2 * n_pen + 4), np.float32)
    for b in range(n_pen):
        states = np.zeros((16, 2 * nx))
        states[0] = states[10] = bx.to_later[b]
        states[1] = states[11] = bx.to_earlier[b]
        left[b, 0], left[b, 1] = split(np.concatenate([bx.diagonal[b], states]))
        ends[b, :nx, 0] = bx.falling[b]
        ends[b, :nx, 1] = bx.rising[b]
        pens[b, :n_pen] = bx.from_earlier[b]
        pens[b, n_pen : 2 * n_pen] = bx.from_later[b]
        if b == 0:
            ends[b, :nx, 2] = -bx.own_first / 3.0
            pens[b, 2 * n_pen] = -bx.first_to_later / 3.0
        if b == n_pen - 1:
            ends[b, :nx, 3] = bx.own_last * 2.0 / 3.0
            pens[b, 2 * n_pen + 3] = bx.last_to_earlier * 2.0 / 3.0

    at = Scalars(groups)
    table = np.zeros((groups + n_pen, at.size), np.float32)
    table[groups:, : pens.shape[1]] = pens
    for b in range(groups):
        table[b, at.local : at.to_later] = by.diagonal[b].reshape(-1)
        table[b, at.to_later : at.to_earlier] = by.to_later[b]
        table[b, at.to_earlier : at.falling] = by.to_earlier[b]
        table[b, at.falling : at.rising] = by.falling[b]
        table[b, at.rising : at.from_earlier] = by.rising[b]
        table[b, at.from_earlier : at.from_later] = by.from_earlier[b]
        table[b, at.from_later :] = by.from_later[b]
    return at, left, pz, ends, table


def per_device(slabs, n_pen, density):
    nz, nx = density.shape[1] // 2, density.shape[2] // 2
    groups = slabs // GROUP
    part = nx // GROUP
    at, *operands = tables(slabs, n_pen, nx, nz)
    left, pz, ends, table = operands
    operands = [pltpu.with_memory_space_constraint(a, pltpu.HBM) for a in (density, *operands)]
    anywhere = pl.BlockSpec(memory_space=pl.ANY)
    vector = pl.BlockSpec(memory_space=pltpu.VMEM)
    dma = pltpu.SemaphoreType.DMA
    spread = (2 * nz, nz), (2 * nx, nx)

    def tile(*shape):
        return pltpu.VMEM(shape, F32)

    partial, coarse, select = pl.pallas_call(
        functools.partial(kernel, (slabs, n_pen, groups, nx, nz, at)),
        out_shape=(
            tile(*density.shape),
            tile(nz, nx),
            pltpu.VMEM((2, 2 * nz, nz), BF16),
        ),
        in_specs=[anywhere] * 5,
        out_specs=(vector, vector, vector),
        scratch_shapes=[
            tile(*density.shape),
            pltpu.VMEM(left.shape[1:], BF16),
            pltpu.VMEM(pz.shape, BF16),
            tile(*ends.shape[1:]),
            pltpu.SMEM(table.shape, F32),
            pltpu.VMEM(spread[1], BF16),
            pltpu.VMEM(spread[0], BF16),
            tile(nx + 8, nz),
            tile(8, nz), tile(8, nz),
            tile(nx + 8, nz),
            tile(GROUP, 2 * part, nz), tile(GROUP, 2 * part, nz),
            tile(4, nz), tile(GROUP, 4, nz),
            tile(2, part + STATE_ROWS, nz), tile(groups, part + STATE_ROWS, nz),
            tile(GROUP, part, nz), tile(GROUP, part, nz),
            tile(STATE_ROWS, nz), tile(n_pen, STATE_ROWS, nz),
            dma((6,)),
            dma, dma, dma, dma,
            pltpu.SemaphoreType.REGULAR,
            dma((GROUP,)), dma((GROUP,)), dma((GROUP,)), dma((GROUP,)),
            dma((groups,)), dma((groups,)),
            dma((GROUP,)), dma((GROUP,)), dma((n_pen,)), dma((n_pen,)),
        ],
        compiler_params=pltpu.CompilerParams(
            collective_id=0, has_side_effects=True, vmem_limit_bytes=32 * 1024 * 1024
        ),
        name="decompose",
    )(*operands)
    return pl.pallas_call(
        finish,
        out_shape=(
            jax.ShapeDtypeStruct(density.shape, F32),
            jax.ShapeDtypeStruct((1, nz, nx), F32),
        ),
        in_specs=[vector] * 3,
        out_specs=(anywhere, anywhere),
        scratch_shapes=[tile(2 * nz, 2 * nx), dma((3,))],
        compiler_params=pltpu.CompilerParams(vmem_limit_bytes=16 * 1024 * 1024),
        name="finish",
    )(partial, coarse, select)


def solution(mesh):
    slabs, n_pen = mesh.shape["slab"], mesh.shape["pen"]
    return jax.shard_map(
        functools.partial(per_device, slabs, n_pen),
        mesh=mesh,
        in_specs=(P("slab", None, "pen"),),
        out_specs=(P("slab", None, "pen"), P("slab", None, "pen")),
        check_vma=False,
    )
```

```python
import functools
import math

import jax
import jax.numpy as jnp
import ml_dtypes
import numpy as np
from jax import lax
from jax.experimental import pallas as pl
from jax.experimental.pallas import tpu as pltpu
from jax.sharding import PartitionSpec as P

MESH = pl.DeviceIdType.MESH
DECAY = math.log(2.0 + math.sqrt(3.0))
GROUP = 8
STATE_ROWS = 8
F32 = jnp.float32
BF16 = jnp.bfloat16


def inverse_mass(m):
    i = np.arange(m)[:, None]
    j = np.arange(m)[None, :]
    low, high = np.minimum(i, j), np.maximum(i, j)
    sign = np.where((high - low) % 2 == 0, 1.0, -1.0)
    ends = (1 - np.exp(-2 * (low + 1) * DECAY)) * (1 - np.exp(-2 * (m - high) * DECAY))
    scale = 3.0 / (2 * math.sqrt(3.0) * (1 - np.exp(-2 * (m + 1) * DECAY)))
    return scale * sign * np.exp(-(high - low) * DECAY) * ends


def refine_matrix(m):
    matrix = np.zeros((2 * m, m))
    j = np.arange(m)
    matrix[2 * j, j] = 1.0
    matrix[2 * j[:-1] + 1, j[:-1]] = 0.5
    matrix[2 * j[:-1] + 1, j[:-1] + 1] = 0.5
    matrix[2 * m - 1, m - 1] = 1.0
    return matrix


def project_matrix(m):
    j = np.arange(m)
    load = np.zeros((m, 2 * m + 2))
    w = np.where(j == m - 1, 1.0, 0.5)
    for offset, weight in ((-2, 0.5), (-1, 3.0), (0, 5.0), (1, 3.0), (2, 0.5)):
        keep = 2 * j + offset >= 0
        load[j[keep], 2 * j[keep] + offset] = weight / 6.0
    load[0, 0] = 4.5 / 6.0
    load[m - 1, 2 * m - 2] = (4.0 + w[-1] + 0.5) / 6.0
    load[m - 1, 2 * m - 1] = (1.0 + 4.0 * w[-1]) / 6.0
    return inverse_mass(m) @ load[:, : 2 * m]


def falling(m, i, start):
    d = i - start
    sign = np.where(d % 2 == 0, 1.0, -1.0)
    ends = (1 - np.exp(-2.0 * (m - i) * DECAY)) / (1 - np.exp(-2.0 * (m - start) * DECAY))
    return sign * np.exp(-d * DECAY) * ends


def rising(m, i, start):
    d = start - i
    sign = np.where(d % 2 == 0, 1.0, -1.0)
    ends = (1 - np.exp(-2.0 * (i + 1) * DECAY)) / (1 - np.exp(-2.0 * (start + 1) * DECAY))
    return sign * np.exp(-d * DECAY) * ends


class Blocks:
    def __init__(self, m, n):
        whole = project_matrix(m)
        size = m // n
        rows = np.arange(size)
        self.diagonal = np.stack(
            [whole[b * size : (b + 1) * size, 2 * b * size : 2 * (b + 1) * size] for b in range(n)]
        )
        self.to_later = np.zeros((n, 2 * size))
        self.to_earlier = np.zeros((n, 2 * size))
        self.later_first = np.zeros(n)
        self.earlier_last = np.zeros(n)
        self.falling = np.zeros((n, size))
        self.rising = np.zeros((n, size))
        self.from_earlier = np.zeros((n, n))
        self.from_later = np.zeros((n, n))
        inverse = inverse_mass(m)
        self.own_first = inverse[:size, 0]
        self.own_last = inverse[m - size :, m - 1]
        for b in range(n):
            columns = slice(2 * b * size, 2 * (b + 1) * size)
            first, last = b * size, (b + 1) * size - 1
            if b < n - 1:
                self.to_later[b] = whole[last + 1, columns]
            if b > 0:
                self.to_earlier[b] = whole[first - 1, columns]
            self.falling[b] = falling(m, first + rows, first)
            self.rising[b] = rising(m, first + rows, last)
            for c in range(n):
                if c < b:
                    self.from_earlier[b, c] = falling(m, first, (c + 1) * size)
                if c > b:
                    self.from_later[b, c] = rising(m, last, c * size - 1)
        self.first_to_later = inverse[size, 0] if n > 1 else 0.0
        self.last_to_earlier = inverse[m - size - 1, m - 1] if n > 1 else 0.0


def split(matrix):
    matrix = np.asarray(matrix, np.float32)
    high = matrix.astype(ml_dtypes.bfloat16)
    low = (matrix - high.astype(np.float32)).astype(ml_dtypes.bfloat16)
    return high, low


def parts(value):
    high = value.astype(BF16)
    return high, (value - high.astype(F32)).astype(BF16)


def dot(a, b, transposed=False):
    dims = (((1,), (1 if transposed else 0,)), ((), ()))
    return lax.dot_general(a, b, dims, preferred_element_type=F32)


def dot3(a, b, transposed=False):
    return (
        dot(a[0], b[0], transposed) + dot(a[0], b[1], transposed) + dot(a[1], b[0], transposed)
    )


class Scalars:
    def __init__(self, groups):
        g = GROUP
        self.local = 0
        self.to_later = self.local + 2 * g * g
        self.to_earlier = self.to_later + 2 * g
        self.falling = self.to_earlier + 2 * g
        self.rising = self.falling + g
        self.from_earlier = self.rising + g
        self.from_later = self.from_earlier + groups
        self.size = self.from_later + groups


def kernel(
    sizes,
    u_hbm, left_hbm, pz_hbm, ends_hbm, table_hbm,
    fine, coarse, select,
    u, left, pz, ends, table, refine_x, refine_z, coarse_t, halo_in, halo_out, next_c,
    out_a, in_a, out_s, in_s, out_b, in_b, out_c, in_c, out_x, in_x,
    load_sem,
    h1_send, h1_recv, h2_send, h2_recv,
    onward, along, across, a_send, a_recv, s_send, s_recv, b_send, b_recv, c_send, c_recv, x_send, x_recv,
):
    slabs, n_pen, groups, nx, nz, at = sizes
    part = nx // GROUP
    s = lax.axis_index("slab")
    p = lax.axis_index("pen")
    g = s // GROUP
    m = lax.rem(s, GROUP)

    load_u0 = pltpu.make_async_copy(u_hbm.at[0], u.at[0], load_sem.at[0])
    load_left = pltpu.make_async_copy(left_hbm.at[p], left, load_sem.at[1])
    load_u1 = pltpu.make_async_copy(u_hbm.at[1], u.at[1], load_sem.at[2])
    load_pz = pltpu.make_async_copy(pz_hbm, pz, load_sem.at[3])
    load_ends = pltpu.make_async_copy(ends_hbm.at[p], ends, load_sem.at[4])
    load_table = pltpu.make_async_copy(table_hbm, table, load_sem.at[5])
    load_u0.start()
    load_left.start()

    turns = groups // 2
    turn, side = lax.rem(g, turns), g // turns

    def mirrored(member, at_turn):
        there = 2 * at_turn // turns
        return member + there * (GROUP - 2 - 2 * member + 2 * lax.rem(member, 2))

    held = mirrored(m, turn)

    def group_at(ahead, flips):
        return lax.rem(side + flips, 2) * turns + lax.rem(turn + ahead, turns)

    def partner(step):
        group = group_at(*step)
        return group, group * GROUP + mirrored(held, lax.rem(group, turns))

    steps = sorted(range(turns), key=lambda k: -min(k, turns - k))
    far_first = [(k, flips) for k in steps for flips in (1, 0) if (k, flips) != (0, 0)]
    near = [(k, flips) for k, flips in far_first if min(k, turns - k) <= 1]
    members = [(g * GROUP + lax.rem(m + k, GROUP), p) for k in range(1, GROUP)]
    others = [(partner(step)[1], p) for step in near]
    around = n_pen // 2
    ring, place = p // around, lax.rem(p, around)

    def pen_at(ahead, flips):
        return lax.rem(ring + flips, 2) * around + lax.rem(place + ahead, around)

    next_pen, previous_pen, across_pen = pen_at(1, 0), pen_at(around - 1, 0), pen_at(0, 1)
    peers = [(s, q) for q in (across_pen, next_pen, previous_pen)]
    above = (lax.rem(s + 1, slabs), p)
    below = (lax.rem(s + slabs - 1, slabs), p)
    barrier = pltpu.get_barrier_semaphore()
    for device in members:
        pl.semaphore_signal(barrier, inc=1, device_id=device, device_id_type=MESH)
    for load in (load_u1, load_pz, load_ends, load_table):
        load.start()
    greeted = [above] + others + peers
    for device in greeted:
        pl.semaphore_signal(barrier, inc=1, device_id=device, device_id_type=MESH)

    def spread_matrix(m, weight):
        row = lax.broadcasted_iota(jnp.int32, (2 * m, m), 0)
        column = lax.broadcasted_iota(jnp.int32, (2 * m, m), 1)
        return weight(row, row - 2 * column).astype(BF16)

    def even(row, away):
        return jnp.where(away == 0, 1.0, 0.0)

    def inner(row, away):
        return jnp.where(away == 0, 1.0, jnp.where(jnp.abs(away) == 1, 0.5, 0.0))

    def ending(row, away):
        return jnp.where((row == 2 * nz - 1) & (away == 1), 1.0, inner(row, away))

    select[0] = spread_matrix(nz, even)
    select[1] = spread_matrix(nx, even)
    refine_x[...] = spread_matrix(nx, inner)
    refine_z[...] = spread_matrix(nz, ending)
    row = lax.broadcasted_iota(jnp.int32, (nx, 2 * nx), 0)
    column = lax.broadcasted_iota(jnp.int32, (nx, 2 * nx), 1)
    take_x = jnp.where(column == 2 * row, 1.0, 0.0).astype(BF16)

    load_u0.wait()
    load_left.wait()
    u0 = parts(u[0])
    lx = (left[0], left[1])
    t0 = dot3(lx, u0, True)
    tc = parts(dot(take_x, u0[0], True) + dot(take_x, u0[1], True))
    load_u1.wait()
    t1 = dot3(lx, parts(u[1]), True)
    load_pz.wait()
    to_z = (pz[0], pz[1])
    y0 = dot3(parts(t0), to_z)
    y1 = dot3(parts(t1), to_z)
    c = dot(tc[0], select[0]) + dot(tc[1], select[0])
    coarse_t[:nx, :] = c
    load_ends.wait()
    load_table.wait()

    def pen(k):
        return table[groups + p, k]

    z_ends = ends[nx : nx + 1, :], ends[nx + 1 : nx + 2, :]
    d = c[:, 0:1] * z_ends[0] + c[:, nz - 1 : nz] * z_ends[1]
    cz = c - d
    cz_first, cz_last = cz[0:1, :], cz[nx - 1 : nx, :]
    ex = ends[:nx, 2:3] * cz_first + ends[:nx, 3:4] * cz_last
    rows8 = lax.broadcasted_iota(jnp.int32, (STATE_ROWS, nz), 0)
    czx_state = jnp.where(
        rows8 == 0,
        pen(2 * n_pen) * cz_first + pen(2 * n_pen + 1) * cz_last,
        pen(2 * n_pen + 2) * cz_first + pen(2 * n_pen + 3) * cz_last,
    )
    czx = cz + ex
    s0 = jnp.where(s == 0, F32(0.5), F32(0.0))
    s1 = jnp.where(s == 0, F32(-1.0 / 12.0), jnp.where(s == slabs - 1, F32(-0.8), F32(0.0)))
    p0 = y0[:nx] + s0 * czx
    p1 = y1[:nx] + s1 * czx
    n0 = y0[nx : nx + STATE_ROWS] + s0 * czx_state
    n1 = y1[nx + STATE_ROWS : nx + 2 * STATE_ROWS] + s1 * jnp.roll(czx_state, 2, 0)
    out_a[:, 0:part, :] = p0.reshape(GROUP, part, nz)
    out_a[:, part : 2 * part, :] = p1.reshape(GROUP, part, nz)
    out_s[...] = jnp.where(rows8 < 2, n0, n1)[0:4]
    in_a[m] = out_a[held]
    in_s[m] = out_s[...]
    halo_out[...] = c[0:8, :]

    pl.semaphore_wait(barrier, len(members) + len(greeted))

    copies_a = []
    for k in range(1, GROUP):
        to = lax.rem(m + k, GROUP)
        copy = pltpu.make_async_remote_copy(
            src_ref=out_a.at[mirrored(to, turn)], dst_ref=in_a.at[m],
            send_sem=a_send.at[k], recv_sem=a_recv.at[k],
            device_id=(g * GROUP + to, p), device_id_type=MESH,
        )
        copy.start()
        copies_a.append(copy)
    for k in range(1, GROUP):
        copy = pltpu.make_async_remote_copy(
            src_ref=out_s, dst_ref=in_s.at[m], send_sem=s_send.at[k], recv_sem=s_recv.at[k],
            device_id=(g * GROUP + lax.rem(m + k, GROUP), p), device_id_type=MESH,
        )
        copy.start()
        copies_a.append(copy)
    behind = (partner((turns - 1, 0))[1], p)
    pl.semaphore_signal(onward, inc=1, device_id=behind, device_id_type=MESH)
    pl.semaphore_signal(along, inc=1, device_id=(s, previous_pen), device_id_type=MESH)
    in_b[g] = jnp.zeros((part + STATE_ROWS, nz), F32)
    rest = d - ex

    pl.semaphore_wait(along, 1)
    pl.semaphore_signal(across, inc=1, device_id=(s, across_pen), device_id_type=MESH)

    for copy in copies_a:
        copy.wait_recv()

    def weigh(base, step, count, get):
        total = table[g, base] * get(0)
        for k in range(1, count):
            total = total + table[g, base + k * step] * get(k)
        return total

    def plane(k):
        return in_a[k // 2, (k % 2) * part : (k % 2 + 1) * part, :]

    def state(k):
        return in_s[k]

    def states(base):
        even = weigh(base, 2, GROUP, state)
        odd = weigh(base + 1, 2, GROUP, state)
        return jnp.concatenate([even[0:2] + odd[2:4]] * (STATE_ROWS // 2), 0)

    for way, base in ((0, at.to_later), (1, at.to_earlier)):
        out_b[way, :part, :] = weigh(base, 1, 2 * GROUP, plane)
        out_b[way, part:, :] = states(base)
    pl.semaphore_wait(onward, 1)
    copies_b = []
    for k, step in enumerate(far_first):
        to, device = partner(step)
        copy = pltpu.make_async_remote_copy(
            src_ref=out_b.at[jnp.where(to > g, 0, 1)], dst_ref=in_b.at[g],
            send_sem=b_send.at[k], recv_sem=b_recv.at[k],
            device_id=(device, p), device_id_type=MESH,
        )
        copy.start()
        copies_b.append(copy)

    pl.semaphore_wait(across, 1)
    copy_h1 = pltpu.make_async_remote_copy(
        src_ref=halo_out, dst_ref=halo_in, send_sem=h1_send, recv_sem=h1_recv,
        device_id=(s, lax.rem(p + n_pen - 1, n_pen)), device_id_type=MESH,
    )
    copy_h1.start()

    for i in range(GROUP):
        out_c[i] = weigh(at.local + 2 * GROUP * i, 1, 2 * GROUP, plane)
    own_states = states(at.local + 2 * GROUP * m)

    copy_h1.wait_recv()
    halo = jnp.where(p == n_pen - 1, c[nx - 1 : nx, :], halo_in[0:1, :])
    coarse_t[nx : nx + 8, :] = jnp.broadcast_to(halo, (8, nz))
    copy_h2 = pltpu.make_async_remote_copy(
        src_ref=coarse_t, dst_ref=next_c, send_sem=h2_send, recv_sem=h2_recv,
        device_id=below, device_id_type=MESH,
    )
    copy_h2.start()

    for copy in copies_b:
        copy.wait_recv()
    from_earlier = weigh(at.from_earlier, 1, groups, lambda k: in_b[k])
    from_later = weigh(at.from_later, 1, groups, lambda k: in_b[k])
    own_states = (
        own_states
        + table[g, at.falling + m] * from_earlier[part:]
        + table[g, at.rising + m] * from_later[part:]
        - czx_state
    )
    out_x[...] = own_states
    copies_x = []
    for k in range(1, n_pen):
        copy = pltpu.make_async_remote_copy(
            src_ref=out_x, dst_ref=in_x.at[p], send_sem=x_send.at[k], recv_sem=x_recv.at[k],
            device_id=(s, lax.rem(p + k, n_pen)), device_id_type=MESH,
        )
        copy.start()
        copies_x.append(copy)
    for i in range(GROUP):
        out_c[i] = (
            out_c[i]
            + table[g, at.falling + i] * from_earlier[:part]
            + table[g, at.rising + i] * from_later[:part]
        )
    copies_c = []
    for k in range(1, GROUP):
        to = lax.rem(m + k, GROUP)
        copy = pltpu.make_async_remote_copy(
            src_ref=out_c.at[to], dst_ref=in_c.at[held], send_sem=c_send.at[k], recv_sem=c_recv.at[k],
            device_id=(g * GROUP + to, p), device_id_type=MESH,
        )
        copy.start()
        copies_c.append(copy)
    in_c[held] = out_c[m]
    in_x[p] = out_x[...]

    fine_rows = lax.broadcasted_iota(jnp.int32, (2 * nx, nz), 0)

    def interpolant(values, beyond):
        high, low = parts(values)
        along_x = dot(refine_x[...], high) + dot(refine_x[...], low)
        along_x = along_x + jnp.where(fine_rows == 2 * nx - 1, 0.5 * beyond, 0.0)
        high, low = parts(along_x)
        return dot(refine_z[...], high, True) + dot(refine_z[...], low, True)

    zi = lax.broadcasted_iota(jnp.int32, (2 * nz, 2 * nx), 0)
    xi = lax.broadcasted_iota(jnp.int32, (2 * nz, 2 * nx), 1)
    kept = ((zi | xi) & 1) == 0
    fine[0] = jnp.where(kept, 0.0, u[0] - interpolant(c, halo))

    copy_h2.wait_recv()
    last = s == slabs - 1
    after = jnp.where(last, coarse_t[...], next_c[...])
    middle = 0.5 * (coarse_t[...] + after)
    fine[1] = u[1] - interpolant(middle[:nx], middle[nx : nx + 1])

    for copy in copies_x:
        copy.wait_recv()
    x_earlier = pen(0) * in_x[0, 0:1, :]
    x_later = pen(n_pen) * in_x[0, 1:2, :]
    for k in range(1, n_pen):
        x_earlier = x_earlier + pen(k) * in_x[k, 0:1, :]
        x_later = x_later + pen(n_pen + k) * in_x[k, 1:2, :]
    rest = rest + ends[:nx, 0:1] * x_earlier + ends[:nx, 1:2] * x_later
    for copy in copies_c:
        copy.wait_recv()
    coarse[...] = (in_c[...].reshape(nx, nz) + rest).T

    for copy in copies_a + copies_b + copies_c + copies_x + [copy_h1, copy_h2]:
        copy.wait_send()


def finish(part, coarse, select, fine_hbm, coarse_hbm, even, sem):
    odd_out = pltpu.make_async_copy(part.at[1], fine_hbm.at[1], sem.at[0])
    coarse_out = pltpu.make_async_copy(coarse, coarse_hbm.at[0], sem.at[1])
    odd_out.start()
    coarse_out.start()
    high, low = parts(coarse[...])
    high, low = parts(dot(select[0], high) + dot(select[0], low))
    even[...] = part[0] + dot(high, select[1], True) + dot(low, select[1], True)
    even_out = pltpu.make_async_copy(even, fine_hbm.at[0], sem.at[2])
    even_out.start()
    odd_out.wait()
    coarse_out.wait()
    even_out.wait()


def tables(slabs, n_pen, nx, nz):
    groups = slabs // GROUP
    bx = Blocks(nx * n_pen, n_pen)
    by = Blocks(slabs, groups)
    bz = Blocks(nz, 1)

    pz = np.stack(split(bz.diagonal[0].T))
    left = np.zeros((n_pen, 2, nx + 16, 2 * nx), ml_dtypes.bfloat16)
    inverse = inverse_mass(nz)
    ends = np.zeros((n_pen, nx + 8, nz), np.float32)
    ends[:, nx] = inverse[:, 0] / 3.0
    ends[:, nx + 1] = inverse[:, -1] * (-2.0 / 3.0)
    pens = np.zeros((n_pen, 2 * n_pen + 4), np.float32)
    for b in range(n_pen):
        states = np.zeros((16, 2 * nx))
        states[0] = states[10] = bx.to_later[b]
        states[1] = states[11] = bx.to_earlier[b]
        left[b, 0], left[b, 1] = split(np.concatenate([bx.diagonal[b], states]))
        ends[b, :nx, 0] = bx.falling[b]
        ends[b, :nx, 1] = bx.rising[b]
        pens[b, :n_pen] = bx.from_earlier[b]
        pens[b, n_pen : 2 * n_pen] = bx.from_later[b]
        if b == 0:
            ends[b, :nx, 2] = -bx.own_first / 3.0
            pens[b, 2 * n_pen] = -bx.first_to_later / 3.0
        if b == n_pen - 1:
            ends[b, :nx, 3] = bx.own_last * 2.0 / 3.0
            pens[b, 2 * n_pen + 3] = bx.last_to_earlier * 2.0 / 3.0

    at = Scalars(groups)
    table = np.zeros((groups + n_pen, at.size), np.float32)
    table[groups:, : pens.shape[1]] = pens
    for b in range(groups):
        table[b, at.local : at.to_later] = by.diagonal[b].reshape(-1)
        table[b, at.to_later : at.to_earlier] = by.to_later[b]
        table[b, at.to_earlier : at.falling] = by.to_earlier[b]
        table[b, at.falling : at.rising] = by.falling[b]
        table[b, at.rising : at.from_earlier] = by.rising[b]
        table[b, at.from_earlier : at.from_later] = by.from_earlier[b]
        table[b, at.from_later :] = by.from_later[b]
    return at, left, pz, ends, table


def per_device(slabs, n_pen, density):
    nz, nx = density.shape[1] // 2, density.shape[2] // 2
    groups = slabs // GROUP
    part = nx // GROUP
    at, *operands = tables(slabs, n_pen, nx, nz)
    left, pz, ends, table = operands
    operands = [pltpu.with_memory_space_constraint(a, pltpu.HBM) for a in (density, *operands)]
    anywhere = pl.BlockSpec(memory_space=pl.ANY)
    vector = pl.BlockSpec(memory_space=pltpu.VMEM)
    dma = pltpu.SemaphoreType.DMA
    spread = (2 * nz, nz), (2 * nx, nx)

    def tile(*shape):
        return pltpu.VMEM(shape, F32)

    partial, coarse, select = pl.pallas_call(
        functools.partial(kernel, (slabs, n_pen, groups, nx, nz, at)),
        out_shape=(
            tile(*density.shape),
            tile(nz, nx),
            pltpu.VMEM((2, 2 * nz, nz), BF16),
        ),
        in_specs=[anywhere] * 5,
        out_specs=(vector, vector, vector),
        scratch_shapes=[
            tile(*density.shape),
            pltpu.VMEM(left.shape[1:], BF16),
            pltpu.VMEM(pz.shape, BF16),
            tile(*ends.shape[1:]),
            pltpu.SMEM(table.shape, F32),
            pltpu.VMEM(spread[1], BF16),
            pltpu.VMEM(spread[0], BF16),
            tile(nx + 8, nz),
            tile(8, nz), tile(8, nz),
            tile(nx + 8, nz),
            tile(GROUP, 2 * part, nz), tile(GROUP, 2 * part, nz),
            tile(4, nz), tile(GROUP, 4, nz),
            tile(2, part + STATE_ROWS, nz), tile(groups, part + STATE_ROWS, nz),
            tile(GROUP, part, nz), tile(GROUP, part, nz),
            tile(STATE_ROWS, nz), tile(n_pen, STATE_ROWS, nz),
            dma((6,)),
            dma, dma, dma, dma,
            *[pltpu.SemaphoreType.REGULAR] * 3,
            dma((GROUP,)), dma((GROUP,)), dma((GROUP,)), dma((GROUP,)),
            dma((groups,)), dma((groups,)),
            dma((GROUP,)), dma((GROUP,)), dma((n_pen,)), dma((n_pen,)),
        ],
        compiler_params=pltpu.CompilerParams(
            collective_id=0, has_side_effects=True, vmem_limit_bytes=32 * 1024 * 1024
        ),
        name="decompose",
    )(*operands)
    return pl.pallas_call(
        finish,
        out_shape=(
            jax.ShapeDtypeStruct(density.shape, F32),
            jax.ShapeDtypeStruct((1, nz, nx), F32),
        ),
        in_specs=[vector] * 3,
        out_specs=(anywhere, anywhere),
        scratch_shapes=[tile(2 * nz, 2 * nx), dma((3,))],
        compiler_params=pltpu.CompilerParams(vmem_limit_bytes=16 * 1024 * 1024),
        name="finish",
    )(partial, coarse, select)


def solution(mesh):
    slabs, n_pen = mesh.shape["slab"], mesh.shape["pen"]
    return jax.shard_map(
        functools.partial(per_device, slabs, n_pen),
        mesh=mesh,
        in_specs=(P("slab", None, "pen"),),
        out_specs=(P("slab", None, "pen"), P("slab", None, "pen")),
        check_vma=False,
    )
```

```python
import functools
import math

import jax
import jax.numpy as jnp
import ml_dtypes
import numpy as np
from jax import lax
from jax.experimental import pallas as pl
from jax.experimental.pallas import tpu as pltpu
from jax.sharding import PartitionSpec as P

MESH = pl.DeviceIdType.MESH
DECAY = math.log(2.0 + math.sqrt(3.0))
GROUP = 8
STATE_ROWS = 8
F32 = jnp.float32
BF16 = jnp.bfloat16


def inverse_mass(m):
    i = np.arange(m)[:, None]
    j = np.arange(m)[None, :]
    low, high = np.minimum(i, j), np.maximum(i, j)
    sign = np.where((high - low) % 2 == 0, 1.0, -1.0)
    ends = (1 - np.exp(-2 * (low + 1) * DECAY)) * (1 - np.exp(-2 * (m - high) * DECAY))
    scale = 3.0 / (2 * math.sqrt(3.0) * (1 - np.exp(-2 * (m + 1) * DECAY)))
    return scale * sign * np.exp(-(high - low) * DECAY) * ends


def refine_matrix(m):
    matrix = np.zeros((2 * m, m))
    j = np.arange(m)
    matrix[2 * j, j] = 1.0
    matrix[2 * j[:-1] + 1, j[:-1]] = 0.5
    matrix[2 * j[:-1] + 1, j[:-1] + 1] = 0.5
    matrix[2 * m - 1, m - 1] = 1.0
    return matrix


def project_matrix(m):
    j = np.arange(m)
    load = np.zeros((m, 2 * m + 2))
    w = np.where(j == m - 1, 1.0, 0.5)
    for offset, weight in ((-2, 0.5), (-1, 3.0), (0, 5.0), (1, 3.0), (2, 0.5)):
        keep = 2 * j + offset >= 0
        load[j[keep], 2 * j[keep] + offset] = weight / 6.0
    load[0, 0] = 4.5 / 6.0
    load[m - 1, 2 * m - 2] = (4.0 + w[-1] + 0.5) / 6.0
    load[m - 1, 2 * m - 1] = (1.0 + 4.0 * w[-1]) / 6.0
    return inverse_mass(m) @ load[:, : 2 * m]


def falling(m, i, start):
    d = i - start
    sign = np.where(d % 2 == 0, 1.0, -1.0)
    ends = (1 - np.exp(-2.0 * (m - i) * DECAY)) / (1 - np.exp(-2.0 * (m - start) * DECAY))
    return sign * np.exp(-d * DECAY) * ends


def rising(m, i, start):
    d = start - i
    sign = np.where(d % 2 == 0, 1.0, -1.0)
    ends = (1 - np.exp(-2.0 * (i + 1) * DECAY)) / (1 - np.exp(-2.0 * (start + 1) * DECAY))
    return sign * np.exp(-d * DECAY) * ends


class Blocks:
    def __init__(self, m, n):
        whole = project_matrix(m)
        size = m // n
        rows = np.arange(size)
        self.diagonal = np.stack(
            [whole[b * size : (b + 1) * size, 2 * b * size : 2 * (b + 1) * size] for b in range(n)]
        )
        self.to_later = np.zeros((n, 2 * size))
        self.to_earlier = np.zeros((n, 2 * size))
        self.later_first = np.zeros(n)
        self.earlier_last = np.zeros(n)
        self.falling = np.zeros((n, size))
        self.rising = np.zeros((n, size))
        self.from_earlier = np.zeros((n, n))
        self.from_later = np.zeros((n, n))
        inverse = inverse_mass(m)
        self.own_first = inverse[:size, 0]
        self.own_last = inverse[m - size :, m - 1]
        for b in range(n):
            columns = slice(2 * b * size, 2 * (b + 1) * size)
            first, last = b * size, (b + 1) * size - 1
            if b < n - 1:
                self.to_later[b] = whole[last + 1, columns]
            if b > 0:
                self.to_earlier[b] = whole[first - 1, columns]
            self.falling[b] = falling(m, first + rows, first)
            self.rising[b] = rising(m, first + rows, last)
            for c in range(n):
                if c < b:
                    self.from_earlier[b, c] = falling(m, first, (c + 1) * size)
                if c > b:
                    self.from_later[b, c] = rising(m, last, c * size - 1)
        self.first_to_later = inverse[size, 0] if n > 1 else 0.0
        self.last_to_earlier = inverse[m - size - 1, m - 1] if n > 1 else 0.0


def split(matrix):
    matrix = np.asarray(matrix, np.float32)
    high = matrix.astype(ml_dtypes.bfloat16)
    low = (matrix - high.astype(np.float32)).astype(ml_dtypes.bfloat16)
    return high, low


def parts(value):
    high = value.astype(BF16)
    return high, (value - high.astype(F32)).astype(BF16)


def dot(a, b, transposed=False):
    dims = (((1,), (1 if transposed else 0,)), ((), ()))
    return lax.dot_general(a, b, dims, preferred_element_type=F32)


def dot3(a, b, transposed=False):
    return (
        dot(a[0], b[0], transposed) + dot(a[0], b[1], transposed) + dot(a[1], b[0], transposed)
    )


class Scalars:
    def __init__(self, groups):
        g = GROUP
        self.local = 0
        self.to_later = self.local + 2 * g * g
        self.to_earlier = self.to_later + 2 * g
        self.falling = self.to_earlier + 2 * g
        self.rising = self.falling + g
        self.from_earlier = self.rising + g
        self.from_later = self.from_earlier + groups
        self.size = self.from_later + groups


def kernel(
    sizes,
    u_hbm, left_hbm, pz_hbm, ends_hbm, table_hbm,
    fine, coarse, select,
    u, left, pz, ends, table, refine_x, refine_z, coarse_t, halo_in, halo_out, next_c,
    out_a, in_a, out_s, in_s, out_b, in_b, out_t, in_t, out_c, in_c, out_x, in_x,
    x_falling, x_rising,
    load_sem,
    h1_send, h1_recv, h2_send, h2_recv,
    onward, along, across, a_send, a_recv, s_send, s_recv, b_send, b_recv, t_send, t_recv, c_send, c_recv, x_send, x_recv,
):
    slabs, n_pen, groups, nx, nz, at = sizes
    part = nx // GROUP
    s = lax.axis_index("slab")
    p = lax.axis_index("pen")
    g = s // GROUP
    m = lax.rem(s, GROUP)

    load_u0 = pltpu.make_async_copy(u_hbm.at[0], u.at[0], load_sem.at[0])
    load_left = pltpu.make_async_copy(left_hbm.at[p], left, load_sem.at[1])
    load_u1 = pltpu.make_async_copy(u_hbm.at[1], u.at[1], load_sem.at[2])
    load_pz = pltpu.make_async_copy(pz_hbm, pz, load_sem.at[3])
    load_ends = pltpu.make_async_copy(ends_hbm.at[p], ends, load_sem.at[4])
    load_table = pltpu.make_async_copy(table_hbm, table, load_sem.at[5])
    load_u0.start()
    load_left.start()

    turns = groups // 2
    turn, side = lax.rem(g, turns), g // turns

    def mirrored(member, at_turn):
        there = 2 * at_turn // turns
        return member + there * (GROUP - 2 - 2 * member + 2 * lax.rem(member, 2))

    held = mirrored(m, turn)

    def group_at(ahead, flips):
        return lax.rem(side + flips, 2) * turns + lax.rem(turn + ahead, turns)

    def partner(step):
        group = group_at(*step)
        return group, group * GROUP + mirrored(held, lax.rem(group, turns))

    steps = sorted(range(turns), key=lambda k: -min(k, turns - k))
    far_first = [(k, flips) for k in steps for flips in (1, 0) if (k, flips) != (0, 0)]
    near = [(k, flips) for k, flips in far_first if min(k, turns - k) <= 1]
    members = [(g * GROUP + lax.rem(m + k, GROUP), p) for k in range(1, GROUP)]
    others = [(partner(step)[1], p) for step in near]
    around = n_pen // 2
    ring, place = p // around, lax.rem(p, around)

    def pen_at(ahead, flips):
        return lax.rem(ring + flips, 2) * around + lax.rem(place + ahead, around)

    next_pen, previous_pen, across_pen = pen_at(1, 0), pen_at(around - 1, 0), pen_at(0, 1)
    around_first = sorted(range(around), key=lambda k: -min(k, around - k))
    far_pens = [(k, flips) for flips in (1, 0) for k in around_first if (k, flips) != (0, 0)]
    peers = [(s, q) for q in (across_pen, next_pen, previous_pen)]
    above = (lax.rem(s + 1, slabs), p)
    below = (lax.rem(s + slabs - 1, slabs), p)
    barrier = pltpu.get_barrier_semaphore()
    for device in members:
        pl.semaphore_signal(barrier, inc=1, device_id=device, device_id_type=MESH)
    for load in (load_u1, load_pz, load_ends, load_table):
        load.start()
    greeted = [above] + others + peers
    for device in greeted:
        pl.semaphore_signal(barrier, inc=1, device_id=device, device_id_type=MESH)

    def spread_matrix(m, weight):
        row = lax.broadcasted_iota(jnp.int32, (2 * m, m), 0)
        column = lax.broadcasted_iota(jnp.int32, (2 * m, m), 1)
        return weight(row, row - 2 * column).astype(BF16)

    def even(row, away):
        return jnp.where(away == 0, 1.0, 0.0)

    def inner(row, away):
        return jnp.where(away == 0, 1.0, jnp.where(jnp.abs(away) == 1, 0.5, 0.0))

    def ending(row, away):
        return jnp.where((row == 2 * nz - 1) & (away == 1), 1.0, inner(row, away))

    select[0] = spread_matrix(nz, even)
    select[1] = spread_matrix(nx, even)
    refine_x[...] = spread_matrix(nx, inner)
    refine_z[...] = spread_matrix(nz, ending)
    row = lax.broadcasted_iota(jnp.int32, (nx, 2 * nx), 0)
    column = lax.broadcasted_iota(jnp.int32, (nx, 2 * nx), 1)
    take_x = jnp.where(column == 2 * row, 1.0, 0.0).astype(BF16)

    load_u0.wait()
    load_left.wait()
    u0 = parts(u[0])
    lx = (left[0], left[1])
    t0 = dot3(lx, u0, True)
    tc = parts(dot(take_x, u0[0], True) + dot(take_x, u0[1], True))
    load_u1.wait()
    t1 = dot3(lx, parts(u[1]), True)
    load_pz.wait()
    to_z = (pz[0], pz[1])
    y0 = dot3(parts(t0), to_z)
    y1 = dot3(parts(t1), to_z)
    c = dot(tc[0], select[0]) + dot(tc[1], select[0])
    coarse_t[:nx, :] = c
    load_ends.wait()
    load_table.wait()

    def pen(k):
        return table[groups + p, k]

    z_ends = ends[nx : nx + 1, :], ends[nx + 1 : nx + 2, :]
    d = c[:, 0:1] * z_ends[0] + c[:, nz - 1 : nz] * z_ends[1]
    cz = c - d
    cz_first, cz_last = cz[0:1, :], cz[nx - 1 : nx, :]
    ex = ends[:nx, 2:3] * cz_first + ends[:nx, 3:4] * cz_last
    rows8 = lax.broadcasted_iota(jnp.int32, (STATE_ROWS, nz), 0)
    czx_state = jnp.where(
        rows8 == 0,
        pen(2 * n_pen) * cz_first + pen(2 * n_pen + 1) * cz_last,
        pen(2 * n_pen + 2) * cz_first + pen(2 * n_pen + 3) * cz_last,
    )
    czx = cz + ex
    s0 = jnp.where(s == 0, F32(0.5), F32(0.0))
    s1 = jnp.where(s == 0, F32(-1.0 / 12.0), jnp.where(s == slabs - 1, F32(-0.8), F32(0.0)))
    p0 = y0[:nx] + s0 * czx
    p1 = y1[:nx] + s1 * czx
    n0 = y0[nx : nx + STATE_ROWS] + s0 * czx_state
    n1 = y1[nx + STATE_ROWS : nx + 2 * STATE_ROWS] + s1 * jnp.roll(czx_state, 2, 0)
    out_a[:, 0:part, :] = p0.reshape(GROUP, part, nz)
    out_a[:, part : 2 * part, :] = p1.reshape(GROUP, part, nz)
    out_s[...] = jnp.where(rows8 < 2, n0, n1)[0:4]
    in_a[m] = out_a[held]
    in_s[m] = out_s[...]
    halo_out[...] = c[0:8, :]

    pl.semaphore_wait(barrier, len(members) + len(greeted))

    copies_s, copies_a = [], []
    for k in range(1, GROUP):
        copy = pltpu.make_async_remote_copy(
            src_ref=out_s, dst_ref=in_s.at[m], send_sem=s_send.at[k], recv_sem=s_recv.at[k],
            device_id=(g * GROUP + lax.rem(m + k, GROUP), p), device_id_type=MESH,
        )
        copy.start()
        copies_s.append(copy)
    for k in range(1, GROUP):
        to = lax.rem(m + k, GROUP)
        copy = pltpu.make_async_remote_copy(
            src_ref=out_a.at[mirrored(to, turn)], dst_ref=in_a.at[m],
            send_sem=a_send.at[k], recv_sem=a_recv.at[k],
            device_id=(g * GROUP + to, p), device_id_type=MESH,
        )
        copy.start()
        copies_a.append(copy)
    behind = (partner((turns - 1, 0))[1], p)
    pl.semaphore_signal(onward, inc=1, device_id=behind, device_id_type=MESH)
    pl.semaphore_signal(along, inc=1, device_id=(s, previous_pen), device_id_type=MESH)
    in_b[g] = jnp.zeros((part, nz), F32)
    in_t[g] = jnp.zeros((2, nz), F32)
    rest = d - ex
    x_falling[...] = jnp.broadcast_to(ends[:nx, 0:1], (nx, nz))
    x_rising[...] = jnp.broadcast_to(ends[:nx, 1:2], (nx, nz))

    pl.semaphore_wait(along, 1)
    pl.semaphore_signal(across, inc=1, device_id=(s, across_pen), device_id_type=MESH)

    def weigh(base, step, count, get):
        total = table[g, base] * get(0)
        for k in range(1, count):
            total = total + table[g, base + k * step] * get(k)
        return total

    def plane(k):
        return in_a[k // 2, (k % 2) * part : (k % 2 + 1) * part, :]

    def states(base):
        even = weigh(base, 2, GROUP, lambda k: in_s[k])
        odd = weigh(base + 1, 2, GROUP, lambda k: in_s[k])
        return even[0:2] + odd[2:4]

    def to_groups(source, landing, send_sem, recv_sem):
        copies = []
        for k, step in enumerate(far_first):
            to, device = partner(step)
            copy = pltpu.make_async_remote_copy(
                src_ref=source.at[jnp.where(to > g, 0, 1)], dst_ref=landing.at[g],
                send_sem=send_sem.at[k], recv_sem=recv_sem.at[k],
                device_id=(device, p), device_id_type=MESH,
            )
            copy.start()
            copies.append(copy)
        return copies

    for copy in copies_s:
        copy.wait_recv()
    out_t[0] = states(at.to_later)
    out_t[1] = states(at.to_earlier)
    pl.semaphore_wait(onward, 1)
    copies_t = to_groups(out_t, in_t, t_send, t_recv)
    own_states = states(at.local + 2 * GROUP * m)

    for copy in copies_a:
        copy.wait_recv()
    out_b[0] = weigh(at.to_later, 1, 2 * GROUP, plane)
    out_b[1] = weigh(at.to_earlier, 1, 2 * GROUP, plane)
    copies_b = to_groups(out_b, in_b, b_send, b_recv)

    pl.semaphore_wait(across, 1)
    copy_h1 = pltpu.make_async_remote_copy(
        src_ref=halo_out, dst_ref=halo_in, send_sem=h1_send, recv_sem=h1_recv,
        device_id=(s, lax.rem(p + n_pen - 1, n_pen)), device_id_type=MESH,
    )
    copy_h1.start()

    for i in range(GROUP):
        out_c[i] = weigh(at.local + 2 * GROUP * i, 1, 2 * GROUP, plane)

    for copy in copies_t:
        copy.wait_recv()
    own_states = (
        own_states
        + table[g, at.falling + m] * weigh(at.from_earlier, 1, groups, lambda k: in_t[k])
        + table[g, at.rising + m] * weigh(at.from_later, 1, groups, lambda k: in_t[k])
        - czx_state[0:2]
    )
    out_x[...] = own_states
    in_x[p] = own_states
    copies_x = []
    for k, step in enumerate(far_pens):
        copy = pltpu.make_async_remote_copy(
            src_ref=out_x, dst_ref=in_x.at[p], send_sem=x_send.at[k], recv_sem=x_recv.at[k],
            device_id=(s, pen_at(*step)), device_id_type=MESH,
        )
        copy.start()
        copies_x.append(copy)

    copy_h1.wait_recv()
    halo = jnp.where(p == n_pen - 1, c[nx - 1 : nx, :], halo_in[0:1, :])
    coarse_t[nx : nx + 8, :] = jnp.broadcast_to(halo, (8, nz))
    copy_h2 = pltpu.make_async_remote_copy(
        src_ref=coarse_t, dst_ref=next_c, send_sem=h2_send, recv_sem=h2_recv,
        device_id=below, device_id_type=MESH,
    )
    copy_h2.start()

    for copy in copies_b:
        copy.wait_recv()
    from_earlier = weigh(at.from_earlier, 1, groups, lambda k: in_b[k])
    from_later = weigh(at.from_later, 1, groups, lambda k: in_b[k])
    for i in range(GROUP):
        out_c[i] = (
            out_c[i]
            + table[g, at.falling + i] * from_earlier
            + table[g, at.rising + i] * from_later
        )
    copies_c = []
    for k in range(1, GROUP):
        to = lax.rem(m + k, GROUP)
        copy = pltpu.make_async_remote_copy(
            src_ref=out_c.at[to], dst_ref=in_c.at[held], send_sem=c_send.at[k], recv_sem=c_recv.at[k],
            device_id=(g * GROUP + to, p), device_id_type=MESH,
        )
        copy.start()
        copies_c.append(copy)
    in_c[held] = out_c[m]

    fine_rows = lax.broadcasted_iota(jnp.int32, (2 * nx, nz), 0)

    def interpolant(values, beyond):
        high, low = parts(values)
        along_x = dot(refine_x[...], high) + dot(refine_x[...], low)
        along_x = along_x + jnp.where(fine_rows == 2 * nx - 1, 0.5 * beyond, 0.0)
        high, low = parts(along_x)
        return dot(refine_z[...], high, True) + dot(refine_z[...], low, True)

    zi = lax.broadcasted_iota(jnp.int32, (2 * nz, 2 * nx), 0)
    xi = lax.broadcasted_iota(jnp.int32, (2 * nz, 2 * nx), 1)
    kept = ((zi | xi) & 1) == 0
    fine[0] = jnp.where(kept, 0.0, u[0] - interpolant(c, halo))

    copy_h2.wait_recv()
    last = s == slabs - 1
    after = jnp.where(last, coarse_t[...], next_c[...])
    middle = 0.5 * (coarse_t[...] + after)
    fine[1] = u[1] - interpolant(middle[:nx], middle[nx : nx + 1])

    for copy in copies_s + copies_a + copies_t + copies_b + copies_x + copies_c + [copy_h1, copy_h2]:
        copy.wait_send()
    for copy in copies_x:
        copy.wait_recv()
    x_earlier = pen(0) * in_x[0, 0:1, :]
    x_later = pen(n_pen) * in_x[0, 1:2, :]
    for k in range(1, n_pen):
        x_earlier = x_earlier + pen(k) * in_x[k, 0:1, :]
        x_later = x_later + pen(n_pen + k) * in_x[k, 1:2, :]
    rest = rest + x_falling[...] * x_earlier + x_rising[...] * x_later
    for copy in copies_c:
        copy.wait_recv()
    coarse[...] = (in_c[...].reshape(nx, nz) + rest).T


def finish(part, coarse, select, fine_hbm, coarse_hbm, even, sem):
    odd_out = pltpu.make_async_copy(part.at[1], fine_hbm.at[1], sem.at[0])
    coarse_out = pltpu.make_async_copy(coarse, coarse_hbm.at[0], sem.at[1])
    odd_out.start()
    coarse_out.start()
    high, low = parts(coarse[...])
    high, low = parts(dot(select[0], high) + dot(select[0], low))
    even[...] = part[0] + dot(high, select[1], True) + dot(low, select[1], True)
    even_out = pltpu.make_async_copy(even, fine_hbm.at[0], sem.at[2])
    even_out.start()
    odd_out.wait()
    coarse_out.wait()
    even_out.wait()


def tables(slabs, n_pen, nx, nz):
    groups = slabs // GROUP
    bx = Blocks(nx * n_pen, n_pen)
    by = Blocks(slabs, groups)
    bz = Blocks(nz, 1)

    pz = np.stack(split(bz.diagonal[0].T))
    left = np.zeros((n_pen, 2, nx + 16, 2 * nx), ml_dtypes.bfloat16)
    inverse = inverse_mass(nz)
    ends = np.zeros((n_pen, nx + 8, nz), np.float32)
    ends[:, nx] = inverse[:, 0] / 3.0
    ends[:, nx + 1] = inverse[:, -1] * (-2.0 / 3.0)
    pens = np.zeros((n_pen, 2 * n_pen + 4), np.float32)
    for b in range(n_pen):
        states = np.zeros((16, 2 * nx))
        states[0] = states[10] = bx.to_later[b]
        states[1] = states[11] = bx.to_earlier[b]
        left[b, 0], left[b, 1] = split(np.concatenate([bx.diagonal[b], states]))
        ends[b, :nx, 0] = bx.falling[b]
        ends[b, :nx, 1] = bx.rising[b]
        pens[b, :n_pen] = bx.from_earlier[b]
        pens[b, n_pen : 2 * n_pen] = bx.from_later[b]
        if b == 0:
            ends[b, :nx, 2] = -bx.own_first / 3.0
            pens[b, 2 * n_pen] = -bx.first_to_later / 3.0
        if b == n_pen - 1:
            ends[b, :nx, 3] = bx.own_last * 2.0 / 3.0
            pens[b, 2 * n_pen + 3] = bx.last_to_earlier * 2.0 / 3.0

    at = Scalars(groups)
    table = np.zeros((groups + n_pen, at.size), np.float32)
    table[groups:, : pens.shape[1]] = pens
    for b in range(groups):
        table[b, at.local : at.to_later] = by.diagonal[b].reshape(-1)
        table[b, at.to_later : at.to_earlier] = by.to_later[b]
        table[b, at.to_earlier : at.falling] = by.to_earlier[b]
        table[b, at.falling : at.rising] = by.falling[b]
        table[b, at.rising : at.from_earlier] = by.rising[b]
        table[b, at.from_earlier : at.from_later] = by.from_earlier[b]
        table[b, at.from_later :] = by.from_later[b]
    return at, left, pz, ends, table


def per_device(slabs, n_pen, density):
    nz, nx = density.shape[1] // 2, density.shape[2] // 2
    groups = slabs // GROUP
    part = nx // GROUP
    at, *operands = tables(slabs, n_pen, nx, nz)
    left, pz, ends, table = operands
    operands = [pltpu.with_memory_space_constraint(a, pltpu.HBM) for a in (density, *operands)]
    anywhere = pl.BlockSpec(memory_space=pl.ANY)
    vector = pl.BlockSpec(memory_space=pltpu.VMEM)
    dma = pltpu.SemaphoreType.DMA
    spread = (2 * nz, nz), (2 * nx, nx)

    def tile(*shape):
        return pltpu.VMEM(shape, F32)

    partial, coarse, select = pl.pallas_call(
        functools.partial(kernel, (slabs, n_pen, groups, nx, nz, at)),
        out_shape=(
            tile(*density.shape),
            tile(nz, nx),
            pltpu.VMEM((2, 2 * nz, nz), BF16),
        ),
        in_specs=[anywhere] * 5,
        out_specs=(vector, vector, vector),
        scratch_shapes=[
            tile(*density.shape),
            pltpu.VMEM(left.shape[1:], BF16),
            pltpu.VMEM(pz.shape, BF16),
            tile(*ends.shape[1:]),
            pltpu.SMEM(table.shape, F32),
            pltpu.VMEM(spread[1], BF16),
            pltpu.VMEM(spread[0], BF16),
            tile(nx + 8, nz),
            tile(8, nz), tile(8, nz),
            tile(nx + 8, nz),
            tile(GROUP, 2 * part, nz), tile(GROUP, 2 * part, nz),
            tile(4, nz), tile(GROUP, 4, nz),
            tile(2, part, nz), tile(groups, part, nz),
            tile(2, 2, nz), tile(groups, 2, nz),
            tile(GROUP, part, nz), tile(GROUP, part, nz),
            tile(2, nz), tile(n_pen, 2, nz),
            tile(nx, nz), tile(nx, nz),
            dma((6,)),
            dma, dma, dma, dma,
            *[pltpu.SemaphoreType.REGULAR] * 3,
            dma((GROUP,)), dma((GROUP,)), dma((GROUP,)), dma((GROUP,)),
            dma((groups,)), dma((groups,)), dma((groups,)), dma((groups,)),
            dma((GROUP,)), dma((GROUP,)), dma((n_pen,)), dma((n_pen,)),
        ],
        compiler_params=pltpu.CompilerParams(
            collective_id=0, has_side_effects=True, vmem_limit_bytes=32 * 1024 * 1024
        ),
        name="decompose",
    )(*operands)
    return pl.pallas_call(
        finish,
        out_shape=(
            jax.ShapeDtypeStruct(density.shape, F32),
            jax.ShapeDtypeStruct((1, nz, nx), F32),
        ),
        in_specs=[vector] * 3,
        out_specs=(anywhere, anywhere),
        scratch_shapes=[tile(2 * nz, 2 * nx), dma((3,))],
        compiler_params=pltpu.CompilerParams(vmem_limit_bytes=16 * 1024 * 1024),
        name="finish",
    )(partial, coarse, select)


def solution(mesh):
    slabs, n_pen = mesh.shape["slab"], mesh.shape["pen"]
    return jax.shard_map(
        functools.partial(per_device, slabs, n_pen),
        mesh=mesh,
        in_specs=(P("slab", None, "pen"),),
        out_specs=(P("slab", None, "pen"), P("slab", None, "pen")),
        check_vma=False,
    )
```

```python
import functools
import math

import jax
import jax.numpy as jnp
import ml_dtypes
import numpy as np
from jax import lax
from jax.experimental import pallas as pl
from jax.experimental.pallas import tpu as pltpu
from jax.sharding import PartitionSpec as P

MESH = pl.DeviceIdType.MESH
DECAY = math.log(2.0 + math.sqrt(3.0))
GROUP = 8
STATE_ROWS = 8
F32 = jnp.float32
BF16 = jnp.bfloat16


def inverse_mass(m):
    i = np.arange(m)[:, None]
    j = np.arange(m)[None, :]
    low, high = np.minimum(i, j), np.maximum(i, j)
    sign = np.where((high - low) % 2 == 0, 1.0, -1.0)
    ends = (1 - np.exp(-2 * (low + 1) * DECAY)) * (1 - np.exp(-2 * (m - high) * DECAY))
    scale = 3.0 / (2 * math.sqrt(3.0) * (1 - np.exp(-2 * (m + 1) * DECAY)))
    return scale * sign * np.exp(-(high - low) * DECAY) * ends


def refine_matrix(m):
    matrix = np.zeros((2 * m, m))
    j = np.arange(m)
    matrix[2 * j, j] = 1.0
    matrix[2 * j[:-1] + 1, j[:-1]] = 0.5
    matrix[2 * j[:-1] + 1, j[:-1] + 1] = 0.5
    matrix[2 * m - 1, m - 1] = 1.0
    return matrix


def project_matrix(m):
    j = np.arange(m)
    load = np.zeros((m, 2 * m + 2))
    w = np.where(j == m - 1, 1.0, 0.5)
    for offset, weight in ((-2, 0.5), (-1, 3.0), (0, 5.0), (1, 3.0), (2, 0.5)):
        keep = 2 * j + offset >= 0
        load[j[keep], 2 * j[keep] + offset] = weight / 6.0
    load[0, 0] = 4.5 / 6.0
    load[m - 1, 2 * m - 2] = (4.0 + w[-1] + 0.5) / 6.0
    load[m - 1, 2 * m - 1] = (1.0 + 4.0 * w[-1]) / 6.0
    return inverse_mass(m) @ load[:, : 2 * m]


def falling(m, i, start):
    d = i - start
    sign = np.where(d % 2 == 0, 1.0, -1.0)
    ends = (1 - np.exp(-2.0 * (m - i) * DECAY)) / (1 - np.exp(-2.0 * (m - start) * DECAY))
    return sign * np.exp(-d * DECAY) * ends


def rising(m, i, start):
    d = start - i
    sign = np.where(d % 2 == 0, 1.0, -1.0)
    ends = (1 - np.exp(-2.0 * (i + 1) * DECAY)) / (1 - np.exp(-2.0 * (start + 1) * DECAY))
    return sign * np.exp(-d * DECAY) * ends


class Blocks:
    def __init__(self, m, n):
        whole = project_matrix(m)
        size = m // n
        rows = np.arange(size)
        self.diagonal = np.stack(
            [whole[b * size : (b + 1) * size, 2 * b * size : 2 * (b + 1) * size] for b in range(n)]
        )
        self.to_later = np.zeros((n, 2 * size))
        self.to_earlier = np.zeros((n, 2 * size))
        self.later_first = np.zeros(n)
        self.earlier_last = np.zeros(n)
        self.falling = np.zeros((n, size))
        self.rising = np.zeros((n, size))
        self.from_earlier = np.zeros((n, n))
        self.from_later = np.zeros((n, n))
        inverse = inverse_mass(m)
        self.own_first = inverse[:size, 0]
        self.own_last = inverse[m - size :, m - 1]
        for b in range(n):
            columns = slice(2 * b * size, 2 * (b + 1) * size)
            first, last = b * size, (b + 1) * size - 1
            if b < n - 1:
                self.to_later[b] = whole[last + 1, columns]
            if b > 0:
                self.to_earlier[b] = whole[first - 1, columns]
            self.falling[b] = falling(m, first + rows, first)
            self.rising[b] = rising(m, first + rows, last)
            for c in range(n):
                if c < b:
                    self.from_earlier[b, c] = falling(m, first, (c + 1) * size)
                if c > b:
                    self.from_later[b, c] = rising(m, last, c * size - 1)
        self.first_to_later = inverse[size, 0] if n > 1 else 0.0
        self.last_to_earlier = inverse[m - size - 1, m - 1] if n > 1 else 0.0


def split(matrix):
    matrix = np.asarray(matrix, np.float32)
    high = matrix.astype(ml_dtypes.bfloat16)
    low = (matrix - high.astype(np.float32)).astype(ml_dtypes.bfloat16)
    return high, low


def parts(value):
    high = value.astype(BF16)
    return high, (value - high.astype(F32)).astype(BF16)


def dot(a, b, transposed=False):
    dims = (((1,), (1 if transposed else 0,)), ((), ()))
    return lax.dot_general(a, b, dims, preferred_element_type=F32)


def dot3(a, b, transposed=False):
    return (
        dot(a[0], b[0], transposed) + dot(a[0], b[1], transposed) + dot(a[1], b[0], transposed)
    )


class Scalars:
    def __init__(self, groups):
        g = GROUP
        self.local = 0
        self.to_later = self.local + 2 * g * g
        self.to_earlier = self.to_later + 2 * g
        self.falling = self.to_earlier + 2 * g
        self.rising = self.falling + g
        self.from_earlier = self.rising + g
        self.from_later = self.from_earlier + groups
        self.size = self.from_later + groups


def kernel(
    sizes,
    u_hbm, left_hbm, pz_hbm, ends_hbm, table_hbm,
    fine, coarse, select,
    u, left, pz, ends, table, refine_x, refine_z, coarse_t, halo_in, halo_out, next_c,
    out_a, in_a, out_s, in_s, out_b, in_b, out_t, in_t, out_c, in_c, out_x, in_x,
    x_falling, x_rising,
    load_sem,
    h1_send, h1_recv, h2_send, h2_recv,
    onward, sideways, along, across, a_send, a_recv, s_send, s_recv, b_send, b_recv, t_send, t_recv, c_send, c_recv, x_send, x_recv,
):
    slabs, n_pen, groups, nx, nz, at = sizes
    part = nx // GROUP
    s = lax.axis_index("slab")
    p = lax.axis_index("pen")
    g = s // GROUP
    m = lax.rem(s, GROUP)

    load_u0 = pltpu.make_async_copy(u_hbm.at[0], u.at[0], load_sem.at[0])
    load_left = pltpu.make_async_copy(left_hbm.at[p], left, load_sem.at[1])
    load_u1 = pltpu.make_async_copy(u_hbm.at[1], u.at[1], load_sem.at[2])
    load_pz = pltpu.make_async_copy(pz_hbm, pz, load_sem.at[3])
    load_ends = pltpu.make_async_copy(ends_hbm.at[p], ends, load_sem.at[4])
    load_table = pltpu.make_async_copy(table_hbm, table, load_sem.at[5])
    load_u0.start()
    load_left.start()

    turns = groups // 2
    turn, side = lax.rem(g, turns), g // turns

    def mirrored(member, at_turn):
        there = 2 * at_turn // turns
        return member + there * (GROUP - 2 - 2 * member + 2 * lax.rem(member, 2))

    held = mirrored(m, turn)

    def group_at(ahead, flips):
        return lax.rem(side + flips, 2) * turns + lax.rem(turn + ahead, turns)

    def partner(step):
        group = group_at(*step)
        return group, group * GROUP + mirrored(held, lax.rem(group, turns))

    steps = sorted(range(turns), key=lambda k: -min(k, turns - k))
    far_first = [(k, flips) for k in steps for flips in (1, 0) if (k, flips) != (0, 0)]
    pair = turn + 1 - 2 * lax.rem(turn, 2)
    fellow = (side * turns + pair) * GROUP + m
    other_half = lax.rem(2 * turn - pair + turns, turns)
    abreast = [
        (lax.rem(side + flips, 2) * turns + other_half) * GROUP + mirrored(held, other_half)
        for flips in (0, 1)
    ]
    beside = partner((0, 1))[1]
    members = [(g * GROUP + lax.rem(m + k, GROUP), p) for k in range(1, GROUP)]
    others = [(device, p) for device in (fellow, *abreast, beside)]
    around = n_pen // 2
    ring, place = p // around, lax.rem(p, around)

    def pen_at(ahead, flips):
        return lax.rem(ring + flips, 2) * around + lax.rem(place + ahead, around)

    next_pen, previous_pen, across_pen = pen_at(1, 0), pen_at(around - 1, 0), pen_at(0, 1)
    around_first = sorted(range(around), key=lambda k: -min(k, around - k))
    far_pens = [(k, flips) for flips in (1, 0) for k in around_first if (k, flips) != (0, 0)]
    peers = [(s, q) for q in (across_pen, next_pen, previous_pen)]
    above = (lax.rem(s + 1, slabs), p)
    below = (lax.rem(s + slabs - 1, slabs), p)
    barrier = pltpu.get_barrier_semaphore()
    for device in members:
        pl.semaphore_signal(barrier, inc=1, device_id=device, device_id_type=MESH)
    for load in (load_u1, load_pz, load_ends, load_table):
        load.start()
    greeted = [above] + others + peers
    for device in greeted:
        pl.semaphore_signal(barrier, inc=1, device_id=device, device_id_type=MESH)

    def spread_matrix(m, weight):
        row = lax.broadcasted_iota(jnp.int32, (2 * m, m), 0)
        column = lax.broadcasted_iota(jnp.int32, (2 * m, m), 1)
        return weight(row, row - 2 * column).astype(BF16)

    def even(row, away):
        return jnp.where(away == 0, 1.0, 0.0)

    def inner(row, away):
        return jnp.where(away == 0, 1.0, jnp.where(jnp.abs(away) == 1, 0.5, 0.0))

    def ending(row, away):
        return jnp.where((row == 2 * nz - 1) & (away == 1), 1.0, inner(row, away))

    select[0] = spread_matrix(nz, even)
    select[1] = spread_matrix(nx, even)
    refine_x[...] = spread_matrix(nx, inner)
    refine_z[...] = spread_matrix(nz, ending)
    row = lax.broadcasted_iota(jnp.int32, (nx, 2 * nx), 0)
    column = lax.broadcasted_iota(jnp.int32, (nx, 2 * nx), 1)
    take_x = jnp.where(column == 2 * row, 1.0, 0.0).astype(BF16)

    load_u0.wait()
    load_left.wait()
    u0 = parts(u[0])
    lx = (left[0], left[1])
    t0 = dot3(lx, u0, True)
    tc = parts(dot(take_x, u0[0], True) + dot(take_x, u0[1], True))
    load_u1.wait()
    t1 = dot3(lx, parts(u[1]), True)
    load_pz.wait()
    to_z = (pz[0], pz[1])
    y0 = dot3(parts(t0), to_z)
    y1 = dot3(parts(t1), to_z)
    c = dot(tc[0], select[0]) + dot(tc[1], select[0])
    coarse_t[:nx, :] = c
    load_ends.wait()
    load_table.wait()

    def pen(k):
        return table[groups + p, k]

    z_ends = ends[nx : nx + 1, :], ends[nx + 1 : nx + 2, :]
    d = c[:, 0:1] * z_ends[0] + c[:, nz - 1 : nz] * z_ends[1]
    cz = c - d
    cz_first, cz_last = cz[0:1, :], cz[nx - 1 : nx, :]
    ex = ends[:nx, 2:3] * cz_first + ends[:nx, 3:4] * cz_last
    rows8 = lax.broadcasted_iota(jnp.int32, (STATE_ROWS, nz), 0)
    czx_state = jnp.where(
        rows8 == 0,
        pen(2 * n_pen) * cz_first + pen(2 * n_pen + 1) * cz_last,
        pen(2 * n_pen + 2) * cz_first + pen(2 * n_pen + 3) * cz_last,
    )
    czx = cz + ex
    s0 = jnp.where(s == 0, F32(0.5), F32(0.0))
    s1 = jnp.where(s == 0, F32(-1.0 / 12.0), jnp.where(s == slabs - 1, F32(-0.8), F32(0.0)))
    p0 = y0[:nx] + s0 * czx
    p1 = y1[:nx] + s1 * czx
    n0 = y0[nx : nx + STATE_ROWS] + s0 * czx_state
    n1 = y1[nx + STATE_ROWS : nx + 2 * STATE_ROWS] + s1 * jnp.roll(czx_state, 2, 0)
    out_a[:, 0:part, :] = p0.reshape(GROUP, part, nz)
    out_a[:, part : 2 * part, :] = p1.reshape(GROUP, part, nz)
    out_s[...] = jnp.where(rows8 < 2, n0, n1)[0:4]
    in_a[m] = out_a[held]
    in_s[m] = out_s[...]
    halo_out[...] = c[0:8, :]

    pl.semaphore_wait(barrier, len(members) + len(greeted))

    copies_s, copies_a = [], []
    for k in range(1, GROUP):
        copy = pltpu.make_async_remote_copy(
            src_ref=out_s, dst_ref=in_s.at[m], send_sem=s_send.at[k], recv_sem=s_recv.at[k],
            device_id=(g * GROUP + lax.rem(m + k, GROUP), p), device_id_type=MESH,
        )
        copy.start()
        copies_s.append(copy)
    for k in range(1, GROUP):
        to = lax.rem(m + k, GROUP)
        copy = pltpu.make_async_remote_copy(
            src_ref=out_a.at[mirrored(to, turn)], dst_ref=in_a.at[m],
            send_sem=a_send.at[k], recv_sem=a_recv.at[k],
            device_id=(g * GROUP + to, p), device_id_type=MESH,
        )
        copy.start()
        copies_a.append(copy)
    pl.semaphore_signal(onward, inc=1, device_id=(fellow, p), device_id_type=MESH)
    pl.semaphore_signal(sideways, inc=1, device_id=(beside, p), device_id_type=MESH)
    pl.semaphore_signal(along, inc=1, device_id=(s, previous_pen), device_id_type=MESH)
    in_b[g] = jnp.zeros((part, nz), F32)
    in_t[g] = jnp.zeros((2, nz), F32)
    rest = d - ex
    x_falling[...] = jnp.broadcast_to(ends[:nx, 0:1], (nx, nz))
    x_rising[...] = jnp.broadcast_to(ends[:nx, 1:2], (nx, nz))

    pl.semaphore_wait(along, 1)
    pl.semaphore_signal(across, inc=1, device_id=(s, across_pen), device_id_type=MESH)

    def weigh(base, step, count, get):
        total = table[g, base] * get(0)
        for k in range(1, count):
            total = total + table[g, base + k * step] * get(k)
        return total

    def plane(k):
        return in_a[k // 2, (k % 2) * part : (k % 2 + 1) * part, :]

    def states(base):
        even = weigh(base, 2, GROUP, lambda k: in_s[k])
        odd = weigh(base + 1, 2, GROUP, lambda k: in_s[k])
        return even[0:2] + odd[2:4]

    def to_groups(source, landing, send_sem, recv_sem):
        copies = []
        for k, step in enumerate(far_first):
            to, device = partner(step)
            copy = pltpu.make_async_remote_copy(
                src_ref=source.at[jnp.where(to > g, 0, 1)], dst_ref=landing.at[g],
                send_sem=send_sem.at[k], recv_sem=recv_sem.at[k],
                device_id=(device, p), device_id_type=MESH,
            )
            copy.start()
            copies.append(copy)
        return copies

    for copy in copies_s:
        copy.wait_recv()
    out_t[0] = states(at.to_later)
    out_t[1] = states(at.to_earlier)
    pl.semaphore_wait(onward, 1)
    pl.semaphore_wait(sideways, 1)
    copies_t = to_groups(out_t, in_t, t_send, t_recv)
    own_states = states(at.local + 2 * GROUP * m)

    for copy in copies_a:
        copy.wait_recv()
    out_b[0] = weigh(at.to_later, 1, 2 * GROUP, plane)
    out_b[1] = weigh(at.to_earlier, 1, 2 * GROUP, plane)
    copies_b = to_groups(out_b, in_b, b_send, b_recv)

    pl.semaphore_wait(across, 1)
    copy_h1 = pltpu.make_async_remote_copy(
        src_ref=halo_out, dst_ref=halo_in, send_sem=h1_send, recv_sem=h1_recv,
        device_id=(s, lax.rem(p + n_pen - 1, n_pen)), device_id_type=MESH,
    )
    copy_h1.start()

    for i in range(GROUP):
        out_c[i] = weigh(at.local + 2 * GROUP * i, 1, 2 * GROUP, plane)

    for copy in copies_t:
        copy.wait_recv()
    own_states = (
        own_states
        + table[g, at.falling + m] * weigh(at.from_earlier, 1, groups, lambda k: in_t[k])
        + table[g, at.rising + m] * weigh(at.from_later, 1, groups, lambda k: in_t[k])
        - czx_state[0:2]
    )
    out_x[...] = own_states
    in_x[p] = own_states
    copies_x = []
    for k, step in enumerate(far_pens):
        copy = pltpu.make_async_remote_copy(
            src_ref=out_x, dst_ref=in_x.at[p], send_sem=x_send.at[k], recv_sem=x_recv.at[k],
            device_id=(s, pen_at(*step)), device_id_type=MESH,
        )
        copy.start()
        copies_x.append(copy)

    copy_h1.wait_recv()
    halo = jnp.where(p == n_pen - 1, c[nx - 1 : nx, :], halo_in[0:1, :])
    coarse_t[nx : nx + 8, :] = jnp.broadcast_to(halo, (8, nz))
    copy_h2 = pltpu.make_async_remote_copy(
        src_ref=coarse_t, dst_ref=next_c, send_sem=h2_send, recv_sem=h2_recv,
        device_id=below, device_id_type=MESH,
    )
    copy_h2.start()

    for copy in copies_b:
        copy.wait_recv()
    from_earlier = weigh(at.from_earlier, 1, groups, lambda k: in_b[k])
    from_later = weigh(at.from_later, 1, groups, lambda k: in_b[k])
    for i in range(GROUP):
        out_c[i] = (
            out_c[i]
            + table[g, at.falling + i] * from_earlier
            + table[g, at.rising + i] * from_later
        )
    copies_c = []
    for k in range(1, GROUP):
        to = lax.rem(m + k, GROUP)
        copy = pltpu.make_async_remote_copy(
            src_ref=out_c.at[to], dst_ref=in_c.at[held], send_sem=c_send.at[k], recv_sem=c_recv.at[k],
            device_id=(g * GROUP + to, p), device_id_type=MESH,
        )
        copy.start()
        copies_c.append(copy)
    in_c[held] = out_c[m]

    fine_rows = lax.broadcasted_iota(jnp.int32, (2 * nx, nz), 0)

    def interpolant(values, beyond):
        high, low = parts(values)
        along_x = dot(refine_x[...], high) + dot(refine_x[...], low)
        along_x = along_x + jnp.where(fine_rows == 2 * nx - 1, 0.5 * beyond, 0.0)
        high, low = parts(along_x)
        return dot(refine_z[...], high, True) + dot(refine_z[...], low, True)

    zi = lax.broadcasted_iota(jnp.int32, (2 * nz, 2 * nx), 0)
    xi = lax.broadcasted_iota(jnp.int32, (2 * nz, 2 * nx), 1)
    kept = ((zi | xi) & 1) == 0
    fine[0] = jnp.where(kept, 0.0, u[0] - interpolant(c, halo))

    copy_h2.wait_recv()
    last = s == slabs - 1
    after = jnp.where(last, coarse_t[...], next_c[...])
    middle = 0.5 * (coarse_t[...] + after)
    fine[1] = u[1] - interpolant(middle[:nx], middle[nx : nx + 1])

    for copy in copies_s + copies_a + copies_t + copies_b + copies_x + copies_c + [copy_h1, copy_h2]:
        copy.wait_send()
    for copy in copies_x:
        copy.wait_recv()
    x_earlier = pen(0) * in_x[0, 0:1, :]
    x_later = pen(n_pen) * in_x[0, 1:2, :]
    for k in range(1, n_pen):
        x_earlier = x_earlier + pen(k) * in_x[k, 0:1, :]
        x_later = x_later + pen(n_pen + k) * in_x[k, 1:2, :]
    rest = rest + x_falling[...] * x_earlier + x_rising[...] * x_later
    for copy in copies_c:
        copy.wait_recv()
    coarse[...] = (in_c[...].reshape(nx, nz) + rest).T


def finish(part, coarse, select, fine_hbm, coarse_hbm, even, sem):
    odd_out = pltpu.make_async_copy(part.at[1], fine_hbm.at[1], sem.at[0])
    coarse_out = pltpu.make_async_copy(coarse, coarse_hbm.at[0], sem.at[1])
    odd_out.start()
    coarse_out.start()
    high, low = parts(coarse[...])
    high, low = parts(dot(select[0], high) + dot(select[0], low))
    even[...] = part[0] + dot(high, select[1], True) + dot(low, select[1], True)
    even_out = pltpu.make_async_copy(even, fine_hbm.at[0], sem.at[2])
    even_out.start()
    odd_out.wait()
    coarse_out.wait()
    even_out.wait()


def tables(slabs, n_pen, nx, nz):
    groups = slabs // GROUP
    bx = Blocks(nx * n_pen, n_pen)
    by = Blocks(slabs, groups)
    bz = Blocks(nz, 1)

    pz = np.stack(split(bz.diagonal[0].T))
    left = np.zeros((n_pen, 2, nx + 16, 2 * nx), ml_dtypes.bfloat16)
    inverse = inverse_mass(nz)
    ends = np.zeros((n_pen, nx + 8, nz), np.float32)
    ends[:, nx] = inverse[:, 0] / 3.0
    ends[:, nx + 1] = inverse[:, -1] * (-2.0 / 3.0)
    pens = np.zeros((n_pen, 2 * n_pen + 4), np.float32)
    for b in range(n_pen):
        states = np.zeros((16, 2 * nx))
        states[0] = states[10] = bx.to_later[b]
        states[1] = states[11] = bx.to_earlier[b]
        left[b, 0], left[b, 1] = split(np.concatenate([bx.diagonal[b], states]))
        ends[b, :nx, 0] = bx.falling[b]
        ends[b, :nx, 1] = bx.rising[b]
        pens[b, :n_pen] = bx.from_earlier[b]
        pens[b, n_pen : 2 * n_pen] = bx.from_later[b]
        if b == 0:
            ends[b, :nx, 2] = -bx.own_first / 3.0
            pens[b, 2 * n_pen] = -bx.first_to_later / 3.0
        if b == n_pen - 1:
            ends[b, :nx, 3] = bx.own_last * 2.0 / 3.0
            pens[b, 2 * n_pen + 3] = bx.last_to_earlier * 2.0 / 3.0

    at = Scalars(groups)
    table = np.zeros((groups + n_pen, at.size), np.float32)
    table[groups:, : pens.shape[1]] = pens
    for b in range(groups):
        table[b, at.local : at.to_later] = by.diagonal[b].reshape(-1)
        table[b, at.to_later : at.to_earlier] = by.to_later[b]
        table[b, at.to_earlier : at.falling] = by.to_earlier[b]
        table[b, at.falling : at.rising] = by.falling[b]
        table[b, at.rising : at.from_earlier] = by.rising[b]
        table[b, at.from_earlier : at.from_later] = by.from_earlier[b]
        table[b, at.from_later :] = by.from_later[b]
    return at, left, pz, ends, table


def per_device(slabs, n_pen, density):
    nz, nx = density.shape[1] // 2, density.shape[2] // 2
    groups = slabs // GROUP
    part = nx // GROUP
    at, *operands = tables(slabs, n_pen, nx, nz)
    left, pz, ends, table = operands
    operands = [pltpu.with_memory_space_constraint(a, pltpu.HBM) for a in (density, *operands)]
    anywhere = pl.BlockSpec(memory_space=pl.ANY)
    vector = pl.BlockSpec(memory_space=pltpu.VMEM)
    dma = pltpu.SemaphoreType.DMA
    spread = (2 * nz, nz), (2 * nx, nx)

    def tile(*shape):
        return pltpu.VMEM(shape, F32)

    partial, coarse, select = pl.pallas_call(
        functools.partial(kernel, (slabs, n_pen, groups, nx, nz, at)),
        out_shape=(
            tile(*density.shape),
            tile(nz, nx),
            pltpu.VMEM((2, 2 * nz, nz), BF16),
        ),
        in_specs=[anywhere] * 5,
        out_specs=(vector, vector, vector),
        scratch_shapes=[
            tile(*density.shape),
            pltpu.VMEM(left.shape[1:], BF16),
            pltpu.VMEM(pz.shape, BF16),
            tile(*ends.shape[1:]),
            pltpu.SMEM(table.shape, F32),
            pltpu.VMEM(spread[1], BF16),
            pltpu.VMEM(spread[0], BF16),
            tile(nx + 8, nz),
            tile(8, nz), tile(8, nz),
            tile(nx + 8, nz),
            tile(GROUP, 2 * part, nz), tile(GROUP, 2 * part, nz),
            tile(4, nz), tile(GROUP, 4, nz),
            tile(2, part, nz), tile(groups, part, nz),
            tile(2, 2, nz), tile(groups, 2, nz),
            tile(GROUP, part, nz), tile(GROUP, part, nz),
            tile(2, nz), tile(n_pen, 2, nz),
            tile(nx, nz), tile(nx, nz),
            dma((6,)),
            dma, dma, dma, dma,
            *[pltpu.SemaphoreType.REGULAR] * 4,
            dma((GROUP,)), dma((GROUP,)), dma((GROUP,)), dma((GROUP,)),
            dma((groups,)), dma((groups,)), dma((groups,)), dma((groups,)),
            dma((GROUP,)), dma((GROUP,)), dma((n_pen,)), dma((n_pen,)),
        ],
        compiler_params=pltpu.CompilerParams(
            collective_id=0, has_side_effects=True, vmem_limit_bytes=32 * 1024 * 1024
        ),
        name="decompose",
    )(*operands)
    return pl.pallas_call(
        finish,
        out_shape=(
            jax.ShapeDtypeStruct(density.shape, F32),
            jax.ShapeDtypeStruct((1, nz, nx), F32),
        ),
        in_specs=[vector] * 3,
        out_specs=(anywhere, anywhere),
        scratch_shapes=[tile(2 * nz, 2 * nx), dma((3,))],
        compiler_params=pltpu.CompilerParams(vmem_limit_bytes=16 * 1024 * 1024),
        name="finish",
    )(partial, coarse, select)


def solution(mesh):
    slabs, n_pen = mesh.shape["slab"], mesh.shape["pen"]
    return jax.shard_map(
        functools.partial(per_device, slabs, n_pen),
        mesh=mesh,
        in_specs=(P("slab", None, "pen"),),
        out_specs=(P("slab", None, "pen"), P("slab", None, "pen")),
        check_vma=False,
    )
```

```python
import functools
import math

import jax
import jax.numpy as jnp
import ml_dtypes
import numpy as np
from jax import lax
from jax.experimental import pallas as pl
from jax.experimental.pallas import tpu as pltpu
from jax.sharding import PartitionSpec as P

MESH = pl.DeviceIdType.MESH
DECAY = math.log(2.0 + math.sqrt(3.0))
GROUP = 8
STATE_ROWS = 8
F32 = jnp.float32
BF16 = jnp.bfloat16


def inverse_mass(m):
    i = np.arange(m)[:, None]
    j = np.arange(m)[None, :]
    low, high = np.minimum(i, j), np.maximum(i, j)
    sign = np.where((high - low) % 2 == 0, 1.0, -1.0)
    ends = (1 - np.exp(-2 * (low + 1) * DECAY)) * (1 - np.exp(-2 * (m - high) * DECAY))
    scale = 3.0 / (2 * math.sqrt(3.0) * (1 - np.exp(-2 * (m + 1) * DECAY)))
    return scale * sign * np.exp(-(high - low) * DECAY) * ends


def refine_matrix(m):
    matrix = np.zeros((2 * m, m))
    j = np.arange(m)
    matrix[2 * j, j] = 1.0
    matrix[2 * j[:-1] + 1, j[:-1]] = 0.5
    matrix[2 * j[:-1] + 1, j[:-1] + 1] = 0.5
    matrix[2 * m - 1, m - 1] = 1.0
    return matrix


def project_matrix(m):
    j = np.arange(m)
    load = np.zeros((m, 2 * m + 2))
    w = np.where(j == m - 1, 1.0, 0.5)
    for offset, weight in ((-2, 0.5), (-1, 3.0), (0, 5.0), (1, 3.0), (2, 0.5)):
        keep = 2 * j + offset >= 0
        load[j[keep], 2 * j[keep] + offset] = weight / 6.0
    load[0, 0] = 4.5 / 6.0
    load[m - 1, 2 * m - 2] = (4.0 + w[-1] + 0.5) / 6.0
    load[m - 1, 2 * m - 1] = (1.0 + 4.0 * w[-1]) / 6.0
    return inverse_mass(m) @ load[:, : 2 * m]


def falling(m, i, start):
    d = i - start
    sign = np.where(d % 2 == 0, 1.0, -1.0)
    ends = (1 - np.exp(-2.0 * (m - i) * DECAY)) / (1 - np.exp(-2.0 * (m - start) * DECAY))
    return sign * np.exp(-d * DECAY) * ends


def rising(m, i, start):
    d = start - i
    sign = np.where(d % 2 == 0, 1.0, -1.0)
    ends = (1 - np.exp(-2.0 * (i + 1) * DECAY)) / (1 - np.exp(-2.0 * (start + 1) * DECAY))
    return sign * np.exp(-d * DECAY) * ends


class Blocks:
    def __init__(self, m, n):
        whole = project_matrix(m)
        size = m // n
        rows = np.arange(size)
        self.diagonal = np.stack(
            [whole[b * size : (b + 1) * size, 2 * b * size : 2 * (b + 1) * size] for b in range(n)]
        )
        self.to_later = np.zeros((n, 2 * size))
        self.to_earlier = np.zeros((n, 2 * size))
        self.later_first = np.zeros(n)
        self.earlier_last = np.zeros(n)
        self.falling = np.zeros((n, size))
        self.rising = np.zeros((n, size))
        self.from_earlier = np.zeros((n, n))
        self.from_later = np.zeros((n, n))
        inverse = inverse_mass(m)
        self.own_first = inverse[:size, 0]
        self.own_last = inverse[m - size :, m - 1]
        for b in range(n):
            columns = slice(2 * b * size, 2 * (b + 1) * size)
            first, last = b * size, (b + 1) * size - 1
            if b < n - 1:
                self.to_later[b] = whole[last + 1, columns]
            if b > 0:
                self.to_earlier[b] = whole[first - 1, columns]
            self.falling[b] = falling(m, first + rows, first)
            self.rising[b] = rising(m, first + rows, last)
            for c in range(n):
                if c < b:
                    self.from_earlier[b, c] = falling(m, first, (c + 1) * size)
                if c > b:
                    self.from_later[b, c] = rising(m, last, c * size - 1)
        self.first_to_later = inverse[size, 0] if n > 1 else 0.0
        self.last_to_earlier = inverse[m - size - 1, m - 1] if n > 1 else 0.0


def split(matrix):
    matrix = np.asarray(matrix, np.float32)
    high = matrix.astype(ml_dtypes.bfloat16)
    low = (matrix - high.astype(np.float32)).astype(ml_dtypes.bfloat16)
    return high, low


def parts(value):
    high = value.astype(BF16)
    return high, (value - high.astype(F32)).astype(BF16)


def dot(a, b, transposed=False):
    dims = (((1,), (1 if transposed else 0,)), ((), ()))
    return lax.dot_general(a, b, dims, preferred_element_type=F32)


def dot3(a, b, transposed=False):
    return (
        dot(a[0], b[0], transposed) + dot(a[0], b[1], transposed) + dot(a[1], b[0], transposed)
    )


class Scalars:
    def __init__(self, groups):
        g = GROUP
        self.local = 0
        self.to_later = self.local + 2 * g * g
        self.to_earlier = self.to_later + 2 * g
        self.falling = self.to_earlier + 2 * g
        self.rising = self.falling + g
        self.from_earlier = self.rising + g
        self.from_later = self.from_earlier + groups
        self.size = self.from_later + groups


def kernel(
    sizes,
    u_hbm, left_hbm, pz_hbm, ends_hbm, table_hbm,
    fine, coarse, select,
    u, left, pz, ends, table, refine_x, refine_z, coarse_t, halo_in, halo_out, next_c,
    out_a, in_a, out_s, in_s, out_b, in_b, out_t, in_t, out_c, in_c, out_x, in_x,
    x_falling, x_rising,
    load_sem,
    h1_send, h1_recv, h2_send, h2_recv,
    onward, sideways, along, across, a_send, a_recv, s_send, s_recv, b_send, b_recv, t_send, t_recv, c_send, c_recv, x_send, x_recv,
):
    slabs, n_pen, groups, nx, nz, at = sizes
    part = nx // GROUP
    s = lax.axis_index("slab")
    p = lax.axis_index("pen")
    g = s // GROUP
    m = lax.rem(s, GROUP)

    load_u0 = pltpu.make_async_copy(u_hbm.at[0], u.at[0], load_sem.at[0])
    load_left = pltpu.make_async_copy(left_hbm.at[p], left, load_sem.at[1])
    load_u1 = pltpu.make_async_copy(u_hbm.at[1], u.at[1], load_sem.at[2])
    load_pz = pltpu.make_async_copy(pz_hbm, pz, load_sem.at[3])
    load_ends = pltpu.make_async_copy(ends_hbm.at[p], ends, load_sem.at[4])
    load_table = pltpu.make_async_copy(table_hbm, table, load_sem.at[5])
    load_u0.start()
    load_left.start()

    turns = groups // 2
    turn, side = lax.rem(g, turns), g // turns

    def turned(member, at_turn):
        there = 2 * at_turn // turns
        half = GROUP // 2
        return member + there * (half - GROUP * (member // half))

    held = turned(m, turn)

    def group_at(ahead, flips):
        return lax.rem(side + flips, 2) * turns + lax.rem(turn + ahead, turns)

    def partner(step):
        group = group_at(*step)
        return group, group * GROUP + turned(held, lax.rem(group, turns))

    steps = sorted(range(turns), key=lambda k: -min(k, turns - k))
    far_first = [(k, flips) for k in steps for flips in (1, 0) if (k, flips) != (0, 0)]
    pair = turn + 1 - 2 * lax.rem(turn, 2)
    fellow = (side * turns + pair) * GROUP + m
    other_half = lax.rem(2 * turn - pair + turns, turns)
    abreast = [
        (lax.rem(side + flips, 2) * turns + other_half) * GROUP + turned(held, other_half)
        for flips in (0, 1)
    ]
    beside = partner((0, 1))[1]
    members = [(g * GROUP + lax.rem(m + k, GROUP), p) for k in range(1, GROUP)]
    others = [(device, p) for device in (fellow, *abreast, beside)]
    around = n_pen // 2
    ring, place = p // around, lax.rem(p, around)

    def pen_at(ahead, flips):
        return lax.rem(ring + flips, 2) * around + lax.rem(place + ahead, around)

    next_pen, previous_pen, across_pen = pen_at(1, 0), pen_at(around - 1, 0), pen_at(0, 1)
    around_first = sorted(range(around), key=lambda k: -min(k, around - k))
    far_pens = [(k, flips) for flips in (1, 0) for k in around_first if (k, flips) != (0, 0)]
    peers = [(s, q) for q in (across_pen, next_pen, previous_pen)]
    above = (lax.rem(s + 1, slabs), p)
    below = (lax.rem(s + slabs - 1, slabs), p)
    barrier = pltpu.get_barrier_semaphore()
    for device in members:
        pl.semaphore_signal(barrier, inc=1, device_id=device, device_id_type=MESH)
    for load in (load_u1, load_pz, load_ends, load_table):
        load.start()
    greeted = [above] + others + peers
    for device in greeted:
        pl.semaphore_signal(barrier, inc=1, device_id=device, device_id_type=MESH)

    def spread_matrix(m, weight):
        row = lax.broadcasted_iota(jnp.int32, (2 * m, m), 0)
        column = lax.broadcasted_iota(jnp.int32, (2 * m, m), 1)
        return weight(row, row - 2 * column).astype(BF16)

    def even(row, away):
        return jnp.where(away == 0, 1.0, 0.0)

    def inner(row, away):
        return jnp.where(away == 0, 1.0, jnp.where(jnp.abs(away) == 1, 0.5, 0.0))

    def ending(row, away):
        return jnp.where((row == 2 * nz - 1) & (away == 1), 1.0, inner(row, away))

    select[0] = spread_matrix(nz, even)
    select[1] = spread_matrix(nx, even)
    refine_x[...] = spread_matrix(nx, inner)
    refine_z[...] = spread_matrix(nz, ending)
    row = lax.broadcasted_iota(jnp.int32, (nx, 2 * nx), 0)
    column = lax.broadcasted_iota(jnp.int32, (nx, 2 * nx), 1)
    take_x = jnp.where(column == 2 * row, 1.0, 0.0).astype(BF16)

    load_u0.wait()
    load_left.wait()
    u0 = parts(u[0])
    lx = (left[0], left[1])
    t0 = dot3(lx, u0, True)
    tc = parts(dot(take_x, u0[0], True) + dot(take_x, u0[1], True))
    load_u1.wait()
    t1 = dot3(lx, parts(u[1]), True)
    load_pz.wait()
    to_z = (pz[0], pz[1])
    y0 = dot3(parts(t0), to_z)
    y1 = dot3(parts(t1), to_z)
    c = dot(tc[0], select[0]) + dot(tc[1], select[0])
    coarse_t[:nx, :] = c
    load_ends.wait()
    load_table.wait()

    def pen(k):
        return table[groups + p, k]

    z_ends = ends[nx : nx + 1, :], ends[nx + 1 : nx + 2, :]
    d = c[:, 0:1] * z_ends[0] + c[:, nz - 1 : nz] * z_ends[1]
    cz = c - d
    cz_first, cz_last = cz[0:1, :], cz[nx - 1 : nx, :]
    ex = ends[:nx, 2:3] * cz_first + ends[:nx, 3:4] * cz_last
    rows8 = lax.broadcasted_iota(jnp.int32, (STATE_ROWS, nz), 0)
    czx_state = jnp.where(
        rows8 == 0,
        pen(2 * n_pen) * cz_first + pen(2 * n_pen + 1) * cz_last,
        pen(2 * n_pen + 2) * cz_first + pen(2 * n_pen + 3) * cz_last,
    )
    czx = cz + ex
    s0 = jnp.where(s == 0, F32(0.5), F32(0.0))
    s1 = jnp.where(s == 0, F32(-1.0 / 12.0), jnp.where(s == slabs - 1, F32(-0.8), F32(0.0)))
    p0 = y0[:nx] + s0 * czx
    p1 = y1[:nx] + s1 * czx
    n0 = y0[nx : nx + STATE_ROWS] + s0 * czx_state
    n1 = y1[nx + STATE_ROWS : nx + 2 * STATE_ROWS] + s1 * jnp.roll(czx_state, 2, 0)
    out_a[:, 0:part, :] = p0.reshape(GROUP, part, nz)
    out_a[:, part : 2 * part, :] = p1.reshape(GROUP, part, nz)
    out_s[...] = jnp.where(rows8 < 2, n0, n1)[0:4]
    in_a[m] = out_a[held]
    in_s[m] = out_s[...]
    halo_out[...] = c[0:8, :]

    pl.semaphore_wait(barrier, len(members) + len(greeted))

    copies_s, copies_a = [], []
    for k in range(1, GROUP):
        copy = pltpu.make_async_remote_copy(
            src_ref=out_s, dst_ref=in_s.at[m], send_sem=s_send.at[k], recv_sem=s_recv.at[k],
            device_id=(g * GROUP + lax.rem(m + k, GROUP), p), device_id_type=MESH,
        )
        copy.start()
        copies_s.append(copy)
    for k in range(1, GROUP):
        to = lax.rem(m + k, GROUP)
        copy = pltpu.make_async_remote_copy(
            src_ref=out_a.at[turned(to, turn)], dst_ref=in_a.at[m],
            send_sem=a_send.at[k], recv_sem=a_recv.at[k],
            device_id=(g * GROUP + to, p), device_id_type=MESH,
        )
        copy.start()
        copies_a.append(copy)
    pl.semaphore_signal(onward, inc=1, device_id=(fellow, p), device_id_type=MESH)
    pl.semaphore_signal(sideways, inc=1, device_id=(beside, p), device_id_type=MESH)
    pl.semaphore_signal(along, inc=1, device_id=(s, previous_pen), device_id_type=MESH)
    in_b[g] = jnp.zeros((part, nz), F32)
    in_t[g] = jnp.zeros((2, nz), F32)
    rest = d - ex
    x_falling[...] = jnp.broadcast_to(ends[:nx, 0:1], (nx, nz))
    x_rising[...] = jnp.broadcast_to(ends[:nx, 1:2], (nx, nz))

    pl.semaphore_wait(along, 1)
    pl.semaphore_signal(across, inc=1, device_id=(s, across_pen), device_id_type=MESH)

    def weigh(base, step, count, get):
        total = table[g, base] * get(0)
        for k in range(1, count):
            total = total + table[g, base + k * step] * get(k)
        return total

    def plane(k):
        return in_a[k // 2, (k % 2) * part : (k % 2 + 1) * part, :]

    def states(base):
        even = weigh(base, 2, GROUP, lambda k: in_s[k])
        odd = weigh(base + 1, 2, GROUP, lambda k: in_s[k])
        return even[0:2] + odd[2:4]

    def to_groups(source, landing, send_sem, recv_sem):
        copies = []
        for k, step in enumerate(far_first):
            to, device = partner(step)
            copy = pltpu.make_async_remote_copy(
                src_ref=source.at[jnp.where(to > g, 0, 1)], dst_ref=landing.at[g],
                send_sem=send_sem.at[k], recv_sem=recv_sem.at[k],
                device_id=(device, p), device_id_type=MESH,
            )
            copy.start()
            copies.append(copy)
        return copies

    for copy in copies_s:
        copy.wait_recv()
    out_t[0] = states(at.to_later)
    out_t[1] = states(at.to_earlier)
    pl.semaphore_wait(onward, 1)
    pl.semaphore_wait(sideways, 1)
    copies_t = to_groups(out_t, in_t, t_send, t_recv)
    own_states = states(at.local + 2 * GROUP * m)

    for copy in copies_a:
        copy.wait_recv()
    out_b[0] = weigh(at.to_later, 1, 2 * GROUP, plane)
    out_b[1] = weigh(at.to_earlier, 1, 2 * GROUP, plane)
    copies_b = to_groups(out_b, in_b, b_send, b_recv)

    pl.semaphore_wait(across, 1)
    copy_h1 = pltpu.make_async_remote_copy(
        src_ref=halo_out, dst_ref=halo_in, send_sem=h1_send, recv_sem=h1_recv,
        device_id=(s, lax.rem(p + n_pen - 1, n_pen)), device_id_type=MESH,
    )
    copy_h1.start()

    for i in range(GROUP):
        out_c[i] = weigh(at.local + 2 * GROUP * i, 1, 2 * GROUP, plane)

    for copy in copies_t:
        copy.wait_recv()
    own_states = (
        own_states
        + table[g, at.falling + m] * weigh(at.from_earlier, 1, groups, lambda k: in_t[k])
        + table[g, at.rising + m] * weigh(at.from_later, 1, groups, lambda k: in_t[k])
        - czx_state[0:2]
    )
    out_x[...] = own_states
    in_x[p] = own_states
    copies_x = []
    for k, step in enumerate(far_pens):
        copy = pltpu.make_async_remote_copy(
            src_ref=out_x, dst_ref=in_x.at[p], send_sem=x_send.at[k], recv_sem=x_recv.at[k],
            device_id=(s, pen_at(*step)), device_id_type=MESH,
        )
        copy.start()
        copies_x.append(copy)

    copy_h1.wait_recv()
    halo = jnp.where(p == n_pen - 1, c[nx - 1 : nx, :], halo_in[0:1, :])
    coarse_t[nx : nx + 8, :] = jnp.broadcast_to(halo, (8, nz))
    copy_h2 = pltpu.make_async_remote_copy(
        src_ref=coarse_t, dst_ref=next_c, send_sem=h2_send, recv_sem=h2_recv,
        device_id=below, device_id_type=MESH,
    )
    copy_h2.start()

    for copy in copies_b:
        copy.wait_recv()
    from_earlier = weigh(at.from_earlier, 1, groups, lambda k: in_b[k])
    from_later = weigh(at.from_later, 1, groups, lambda k: in_b[k])

    def finished(row):
        out_c[row] = (
            out_c[row]
            + table[g, at.falling + row] * from_earlier
            + table[g, at.rising + row] * from_later
        )

    rank = jnp.where(m < 2, 1 - m, m)
    copies_c, landings_c = [], []
    for k in range(GROUP - 1):
        nth = k + jnp.where(k >= rank, 1, 0)
        to = jnp.where(nth < 2, 1 - nth, nth)
        finished(to)
        copy = pltpu.make_async_remote_copy(
            src_ref=out_c.at[to], dst_ref=in_c.at[held], send_sem=c_send.at[k], recv_sem=c_recv.at[m],
            device_id=(g * GROUP + to, p), device_id_type=MESH,
        )
        copy.start()
        copies_c.append(copy)
        landings_c.append(
            pltpu.make_async_remote_copy(
                src_ref=out_c.at[to], dst_ref=in_c.at[turned(to, turn)],
                send_sem=c_send.at[k], recv_sem=c_recv.at[to],
                device_id=(g * GROUP + to, p), device_id_type=MESH,
            )
        )
    finished(m)
    in_c[held] = out_c[m]

    fine_rows = lax.broadcasted_iota(jnp.int32, (2 * nx, nz), 0)

    def interpolant(values, beyond):
        high, low = parts(values)
        along_x = dot(refine_x[...], high) + dot(refine_x[...], low)
        along_x = along_x + jnp.where(fine_rows == 2 * nx - 1, 0.5 * beyond, 0.0)
        high, low = parts(along_x)
        return dot(refine_z[...], high, True) + dot(refine_z[...], low, True)

    zi = lax.broadcasted_iota(jnp.int32, (2 * nz, 2 * nx), 0)
    xi = lax.broadcasted_iota(jnp.int32, (2 * nz, 2 * nx), 1)
    kept = ((zi | xi) & 1) == 0
    fine[0] = jnp.where(kept, 0.0, u[0] - interpolant(c, halo))

    copy_h2.wait_recv()
    last = s == slabs - 1
    after = jnp.where(last, coarse_t[...], next_c[...])
    middle = 0.5 * (coarse_t[...] + after)
    fine[1] = u[1] - interpolant(middle[:nx], middle[nx : nx + 1])

    for copy in copies_s + copies_a + copies_t + copies_b + copies_x + copies_c + [copy_h1, copy_h2]:
        copy.wait_send()
    for copy in copies_x:
        copy.wait_recv()
    x_earlier = pen(0) * in_x[0, 0:1, :]
    x_later = pen(n_pen) * in_x[0, 1:2, :]
    for k in range(1, n_pen):
        x_earlier = x_earlier + pen(k) * in_x[k, 0:1, :]
        x_later = x_later + pen(n_pen + k) * in_x[k, 1:2, :]
    rest = rest + x_falling[...] * x_earlier + x_rising[...] * x_later
    for landing in landings_c:
        landing.wait_recv()
    coarse[...] = (in_c[...].reshape(nx, nz) + rest).T


def finish(part, coarse, select, fine_hbm, coarse_hbm, even, sem):
    odd_out = pltpu.make_async_copy(part.at[1], fine_hbm.at[1], sem.at[0])
    coarse_out = pltpu.make_async_copy(coarse, coarse_hbm.at[0], sem.at[1])
    odd_out.start()
    coarse_out.start()
    high, low = parts(coarse[...])
    high, low = parts(dot(select[0], high) + dot(select[0], low))
    even[...] = part[0] + dot(high, select[1], True) + dot(low, select[1], True)
    even_out = pltpu.make_async_copy(even, fine_hbm.at[0], sem.at[2])
    even_out.start()
    odd_out.wait()
    coarse_out.wait()
    even_out.wait()


def tables(slabs, n_pen, nx, nz):
    groups = slabs // GROUP
    bx = Blocks(nx * n_pen, n_pen)
    by = Blocks(slabs, groups)
    bz = Blocks(nz, 1)

    pz = np.stack(split(bz.diagonal[0].T))
    left = np.zeros((n_pen, 2, nx + 16, 2 * nx), ml_dtypes.bfloat16)
    inverse = inverse_mass(nz)
    ends = np.zeros((n_pen, nx + 8, nz), np.float32)
    ends[:, nx] = inverse[:, 0] / 3.0
    ends[:, nx + 1] = inverse[:, -1] * (-2.0 / 3.0)
    pens = np.zeros((n_pen, 2 * n_pen + 4), np.float32)
    for b in range(n_pen):
        states = np.zeros((16, 2 * nx))
        states[0] = states[10] = bx.to_later[b]
        states[1] = states[11] = bx.to_earlier[b]
        left[b, 0], left[b, 1] = split(np.concatenate([bx.diagonal[b], states]))
        ends[b, :nx, 0] = bx.falling[b]
        ends[b, :nx, 1] = bx.rising[b]
        pens[b, :n_pen] = bx.from_earlier[b]
        pens[b, n_pen : 2 * n_pen] = bx.from_later[b]
        if b == 0:
            ends[b, :nx, 2] = -bx.own_first / 3.0
            pens[b, 2 * n_pen] = -bx.first_to_later / 3.0
        if b == n_pen - 1:
            ends[b, :nx, 3] = bx.own_last * 2.0 / 3.0
            pens[b, 2 * n_pen + 3] = bx.last_to_earlier * 2.0 / 3.0

    at = Scalars(groups)
    table = np.zeros((groups + n_pen, at.size), np.float32)
    table[groups:, : pens.shape[1]] = pens
    for b in range(groups):
        table[b, at.local : at.to_later] = by.diagonal[b].reshape(-1)
        table[b, at.to_later : at.to_earlier] = by.to_later[b]
        table[b, at.to_earlier : at.falling] = by.to_earlier[b]
        table[b, at.falling : at.rising] = by.falling[b]
        table[b, at.rising : at.from_earlier] = by.rising[b]
        table[b, at.from_earlier : at.from_later] = by.from_earlier[b]
        table[b, at.from_later :] = by.from_later[b]
    return at, left, pz, ends, table


def per_device(slabs, n_pen, density):
    nz, nx = density.shape[1] // 2, density.shape[2] // 2
    groups = slabs // GROUP
    part = nx // GROUP
    at, *operands = tables(slabs, n_pen, nx, nz)
    left, pz, ends, table = operands
    operands = [pltpu.with_memory_space_constraint(a, pltpu.HBM) for a in (density, *operands)]
    anywhere = pl.BlockSpec(memory_space=pl.ANY)
    vector = pl.BlockSpec(memory_space=pltpu.VMEM)
    dma = pltpu.SemaphoreType.DMA
    spread = (2 * nz, nz), (2 * nx, nx)

    def tile(*shape):
        return pltpu.VMEM(shape, F32)

    partial, coarse, select = pl.pallas_call(
        functools.partial(kernel, (slabs, n_pen, groups, nx, nz, at)),
        out_shape=(
            tile(*density.shape),
            tile(nz, nx),
            pltpu.VMEM((2, 2 * nz, nz), BF16),
        ),
        in_specs=[anywhere] * 5,
        out_specs=(vector, vector, vector),
        scratch_shapes=[
            tile(*density.shape),
            pltpu.VMEM(left.shape[1:], BF16),
            pltpu.VMEM(pz.shape, BF16),
            tile(*ends.shape[1:]),
            pltpu.SMEM(table.shape, F32),
            pltpu.VMEM(spread[1], BF16),
            pltpu.VMEM(spread[0], BF16),
            tile(nx + 8, nz),
            tile(8, nz), tile(8, nz),
            tile(nx + 8, nz),
            tile(GROUP, 2 * part, nz), tile(GROUP, 2 * part, nz),
            tile(4, nz), tile(GROUP, 4, nz),
            tile(2, part, nz), tile(groups, part, nz),
            tile(2, 2, nz), tile(groups, 2, nz),
            tile(GROUP, part, nz), tile(GROUP, part, nz),
            tile(2, nz), tile(n_pen, 2, nz),
            tile(nx, nz), tile(nx, nz),
            dma((6,)),
            dma, dma, dma, dma,
            *[pltpu.SemaphoreType.REGULAR] * 4,
            dma((GROUP,)), dma((GROUP,)), dma((GROUP,)), dma((GROUP,)),
            dma((groups,)), dma((groups,)), dma((groups,)), dma((groups,)),
            dma((GROUP,)), dma((GROUP,)), dma((n_pen,)), dma((n_pen,)),
        ],
        compiler_params=pltpu.CompilerParams(
            collective_id=0, has_side_effects=True, vmem_limit_bytes=32 * 1024 * 1024
        ),
        name="decompose",
    )(*operands)
    return pl.pallas_call(
        finish,
        out_shape=(
            jax.ShapeDtypeStruct(density.shape, F32),
            jax.ShapeDtypeStruct((1, nz, nx), F32),
        ),
        in_specs=[vector] * 3,
        out_specs=(anywhere, anywhere),
        scratch_shapes=[tile(2 * nz, 2 * nx), dma((3,))],
        compiler_params=pltpu.CompilerParams(vmem_limit_bytes=16 * 1024 * 1024),
        name="finish",
    )(partial, coarse, select)


def solution(mesh):
    slabs, n_pen = mesh.shape["slab"], mesh.shape["pen"]
    return jax.shard_map(
        functools.partial(per_device, slabs, n_pen),
        mesh=mesh,
        in_specs=(P("slab", None, "pen"),),
        out_specs=(P("slab", None, "pen"), P("slab", None, "pen")),
        check_vma=False,
    )
```

```python
import functools
import math

import jax
import jax.numpy as jnp
import ml_dtypes
import numpy as np
from jax import lax
from jax.experimental import pallas as pl
from jax.experimental.pallas import tpu as pltpu
from jax.sharding import PartitionSpec as P

MESH = pl.DeviceIdType.MESH
DECAY = math.log(2.0 + math.sqrt(3.0))
GROUP = 8
STATE_ROWS = 8
F32 = jnp.float32
BF16 = jnp.bfloat16


def inverse_mass(m):
    i = np.arange(m)[:, None]
    j = np.arange(m)[None, :]
    low, high = np.minimum(i, j), np.maximum(i, j)
    sign = np.where((high - low) % 2 == 0, 1.0, -1.0)
    ends = (1 - np.exp(-2 * (low + 1) * DECAY)) * (1 - np.exp(-2 * (m - high) * DECAY))
    scale = 3.0 / (2 * math.sqrt(3.0) * (1 - np.exp(-2 * (m + 1) * DECAY)))
    return scale * sign * np.exp(-(high - low) * DECAY) * ends


def refine_matrix(m):
    matrix = np.zeros((2 * m, m))
    j = np.arange(m)
    matrix[2 * j, j] = 1.0
    matrix[2 * j[:-1] + 1, j[:-1]] = 0.5
    matrix[2 * j[:-1] + 1, j[:-1] + 1] = 0.5
    matrix[2 * m - 1, m - 1] = 1.0
    return matrix


def project_matrix(m):
    j = np.arange(m)
    load = np.zeros((m, 2 * m + 2))
    w = np.where(j == m - 1, 1.0, 0.5)
    for offset, weight in ((-2, 0.5), (-1, 3.0), (0, 5.0), (1, 3.0), (2, 0.5)):
        keep = 2 * j + offset >= 0
        load[j[keep], 2 * j[keep] + offset] = weight / 6.0
    load[0, 0] = 4.5 / 6.0
    load[m - 1, 2 * m - 2] = (4.0 + w[-1] + 0.5) / 6.0
    load[m - 1, 2 * m - 1] = (1.0 + 4.0 * w[-1]) / 6.0
    return inverse_mass(m) @ load[:, : 2 * m]


def falling(m, i, start):
    d = i - start
    sign = np.where(d % 2 == 0, 1.0, -1.0)
    ends = (1 - np.exp(-2.0 * (m - i) * DECAY)) / (1 - np.exp(-2.0 * (m - start) * DECAY))
    return sign * np.exp(-d * DECAY) * ends


def rising(m, i, start):
    d = start - i
    sign = np.where(d % 2 == 0, 1.0, -1.0)
    ends = (1 - np.exp(-2.0 * (i + 1) * DECAY)) / (1 - np.exp(-2.0 * (start + 1) * DECAY))
    return sign * np.exp(-d * DECAY) * ends


class Blocks:
    def __init__(self, m, n):
        whole = project_matrix(m)
        size = m // n
        rows = np.arange(size)
        self.diagonal = np.stack(
            [whole[b * size : (b + 1) * size, 2 * b * size : 2 * (b + 1) * size] for b in range(n)]
        )
        self.to_later = np.zeros((n, 2 * size))
        self.to_earlier = np.zeros((n, 2 * size))
        self.later_first = np.zeros(n)
        self.earlier_last = np.zeros(n)
        self.falling = np.zeros((n, size))
        self.rising = np.zeros((n, size))
        self.from_earlier = np.zeros((n, n))
        self.from_later = np.zeros((n, n))
        inverse = inverse_mass(m)
        self.own_first = inverse[:size, 0]
        self.own_last = inverse[m - size :, m - 1]
        for b in range(n):
            columns = slice(2 * b * size, 2 * (b + 1) * size)
            first, last = b * size, (b + 1) * size - 1
            if b < n - 1:
                self.to_later[b] = whole[last + 1, columns]
            if b > 0:
                self.to_earlier[b] = whole[first - 1, columns]
            self.falling[b] = falling(m, first + rows, first)
            self.rising[b] = rising(m, first + rows, last)
            for c in range(n):
                if c < b:
                    self.from_earlier[b, c] = falling(m, first, (c + 1) * size)
                if c > b:
                    self.from_later[b, c] = rising(m, last, c * size - 1)
        self.first_to_later = inverse[size, 0] if n > 1 else 0.0
        self.last_to_earlier = inverse[m - size - 1, m - 1] if n > 1 else 0.0


def split(matrix):
    matrix = np.asarray(matrix, np.float32)
    high = matrix.astype(ml_dtypes.bfloat16)
    low = (matrix - high.astype(np.float32)).astype(ml_dtypes.bfloat16)
    return high, low


def parts(value):
    high = value.astype(BF16)
    return high, (value - high.astype(F32)).astype(BF16)


def dot(a, b, transposed=False):
    dims = (((1,), (1 if transposed else 0,)), ((), ()))
    return lax.dot_general(a, b, dims, preferred_element_type=F32)


def dot3(a, b, transposed=False):
    return (
        dot(a[0], b[0], transposed) + dot(a[0], b[1], transposed) + dot(a[1], b[0], transposed)
    )


class Scalars:
    def __init__(self, groups):
        g = GROUP
        self.local = 0
        self.to_later = self.local + 2 * g * g
        self.to_earlier = self.to_later + 2 * g
        self.falling = self.to_earlier + 2 * g
        self.rising = self.falling + g
        self.from_earlier = self.rising + g
        self.from_later = self.from_earlier + groups
        self.size = self.from_later + groups


def kernel(
    sizes,
    u_hbm, left_hbm, pz_hbm, ends_hbm, table_hbm,
    fine, coarse, select,
    u, left, pz, ends, table, refine_x, refine_z, coarse_t, halo_in, halo_out, next_c,
    out_a, in_a, out_s, in_s, out_b, in_b, out_t, in_t, out_c, in_c, out_x, in_x,
    x_falling, x_rising,
    load_sem,
    h1_send, h1_recv, h2_send, h2_recv,
    onward, sideways, along, across, a_send, a_recv, s_send, s_recv, b_send, b_recv, t_send, t_recv, c_send, c_recv, x_send, x_recv,
):
    slabs, n_pen, groups, nx, nz, at = sizes
    part = nx // GROUP
    s = lax.axis_index("slab")
    p = lax.axis_index("pen")
    g = s // GROUP
    m = lax.rem(s, GROUP)

    load_u0 = pltpu.make_async_copy(u_hbm.at[0], u.at[0], load_sem.at[0])
    load_left = pltpu.make_async_copy(left_hbm.at[p], left, load_sem.at[1])
    load_u1 = pltpu.make_async_copy(u_hbm.at[1], u.at[1], load_sem.at[2])
    load_pz = pltpu.make_async_copy(pz_hbm, pz, load_sem.at[3])
    load_ends = pltpu.make_async_copy(ends_hbm.at[p], ends, load_sem.at[4])
    load_table = pltpu.make_async_copy(table_hbm, table, load_sem.at[5])

    turns = groups // 2
    turn, side = lax.rem(g, turns), g // turns

    def turned(member, at_turn):
        there = 2 * at_turn // turns
        half = GROUP // 2
        return member + there * (half - GROUP * (member // half))

    held = turned(m, turn)

    def group_at(ahead, flips):
        return lax.rem(side + flips, 2) * turns + lax.rem(turn + ahead, turns)

    def partner(step):
        group = group_at(*step)
        return group, group * GROUP + turned(held, lax.rem(group, turns))

    steps = sorted(range(turns), key=lambda k: -min(k, turns - k))
    far_first = [(k, flips) for k in steps for flips in (1, 0) if (k, flips) != (0, 0)]
    pair = turn + 1 - 2 * lax.rem(turn, 2)
    fellow = (side * turns + pair) * GROUP + m
    other_half = lax.rem(2 * turn - pair + turns, turns)
    abreast = [
        (lax.rem(side + flips, 2) * turns + other_half) * GROUP + turned(held, other_half)
        for flips in (0, 1)
    ]
    beside = partner((0, 1))[1]
    members = [(g * GROUP + lax.rem(m + k, GROUP), p) for k in range(1, GROUP)]
    around = n_pen // 2
    ring, place = p // around, lax.rem(p, around)

    def pen_at(ahead, flips):
        return lax.rem(ring + flips, 2) * around + lax.rem(place + ahead, around)

    next_pen, previous_pen, across_pen = pen_at(1, 0), pen_at(around - 1, 0), pen_at(0, 1)
    peers = [(s, q) for q in (across_pen, next_pen, previous_pen)]
    below = (lax.rem(s + slabs - 1, slabs), p)
    barrier = pltpu.get_barrier_semaphore()
    for device in members:
        pl.semaphore_signal(barrier, inc=1, device_id=device, device_id_type=MESH)
    for load in (load_u0, load_left, load_u1, load_pz, load_ends, load_table):
        load.start()
    greeted = peers[:1] + [(fellow, p), (beside, p)] + peers[1:] + [(device, p) for device in abreast]
    for device in greeted:
        pl.semaphore_signal(barrier, inc=1, device_id=device, device_id_type=MESH)

    def spread_matrix(m, weight):
        row = lax.broadcasted_iota(jnp.int32, (2 * m, m), 0)
        column = lax.broadcasted_iota(jnp.int32, (2 * m, m), 1)
        return weight(row, row - 2 * column).astype(BF16)

    def even(row, away):
        return jnp.where(away == 0, 1.0, 0.0)

    def inner(row, away):
        return jnp.where(away == 0, 1.0, jnp.where(jnp.abs(away) == 1, 0.5, 0.0))

    def ending(row, away):
        return jnp.where((row == 2 * nz - 1) & (away == 1), 1.0, inner(row, away))

    select[0] = spread_matrix(nz, even)
    select[1] = spread_matrix(nx, even)
    refine_x[...] = spread_matrix(nx, inner)
    refine_z[...] = spread_matrix(nz, ending)
    row = lax.broadcasted_iota(jnp.int32, (nx, 2 * nx), 0)
    column = lax.broadcasted_iota(jnp.int32, (nx, 2 * nx), 1)
    take_x = jnp.where(column == 2 * row, 1.0, 0.0).astype(BF16)

    load_u0.wait()
    load_left.wait()
    u0 = parts(u[0])
    lx = (left[0], left[1])
    t0 = dot3(lx, u0, True)
    tc = parts(dot(take_x, u0[0], True) + dot(take_x, u0[1], True))
    load_u1.wait()
    t1 = dot3(lx, parts(u[1]), True)
    load_pz.wait()
    to_z = (pz[0], pz[1])
    y0 = dot3(parts(t0), to_z)
    y1 = dot3(parts(t1), to_z)
    c = dot(tc[0], select[0]) + dot(tc[1], select[0])
    coarse_t[:nx, :] = c
    load_ends.wait()
    load_table.wait()

    def pen(k):
        return table[groups + p, k]

    z_ends = ends[nx : nx + 1, :], ends[nx + 1 : nx + 2, :]
    d = c[:, 0:1] * z_ends[0] + c[:, nz - 1 : nz] * z_ends[1]
    cz = c - d
    cz_first, cz_last = cz[0:1, :], cz[nx - 1 : nx, :]
    ex = ends[:nx, 2:3] * cz_first + ends[:nx, 3:4] * cz_last
    rows8 = lax.broadcasted_iota(jnp.int32, (STATE_ROWS, nz), 0)
    czx_state = jnp.where(
        rows8 == 0,
        pen(2 * n_pen) * cz_first + pen(2 * n_pen + 1) * cz_last,
        pen(2 * n_pen + 2) * cz_first + pen(2 * n_pen + 3) * cz_last,
    )
    czx = cz + ex
    s0 = jnp.where(s == 0, F32(0.5), F32(0.0))
    s1 = jnp.where(s == 0, F32(-1.0 / 12.0), jnp.where(s == slabs - 1, F32(-0.8), F32(0.0)))
    p0 = y0[:nx] + s0 * czx
    p1 = y1[:nx] + s1 * czx
    n0 = y0[nx : nx + STATE_ROWS] + s0 * czx_state
    n1 = y1[nx + STATE_ROWS : nx + 2 * STATE_ROWS] + s1 * jnp.roll(czx_state, 2, 0)
    out_a[:, 0:part, :] = p0.reshape(GROUP, part, nz)
    out_a[:, part : 2 * part, :] = p1.reshape(GROUP, part, nz)
    out_s[...] = jnp.where(rows8 < 2, n0, n1)[0:4]
    in_a[m] = out_a[held]
    in_s[m] = out_s[...]
    halo_out[...] = c[0:8, :]

    pl.semaphore_wait(barrier, len(members) + len(greeted))

    copies_s, copies_a = [], []
    for k in range(1, GROUP):
        copy = pltpu.make_async_remote_copy(
            src_ref=out_s, dst_ref=in_s.at[m], send_sem=s_send.at[k], recv_sem=s_recv.at[k],
            device_id=(g * GROUP + lax.rem(m + k, GROUP), p), device_id_type=MESH,
        )
        copy.start()
        copies_s.append(copy)
    for k in range(1, GROUP):
        to = lax.rem(m + k, GROUP)
        copy = pltpu.make_async_remote_copy(
            src_ref=out_a.at[turned(to, turn)], dst_ref=in_a.at[m],
            send_sem=a_send.at[k], recv_sem=a_recv.at[k],
            device_id=(g * GROUP + to, p), device_id_type=MESH,
        )
        copy.start()
        copies_a.append(copy)
    pl.semaphore_signal(onward, inc=1, device_id=(fellow, p), device_id_type=MESH)
    pl.semaphore_signal(sideways, inc=1, device_id=(beside, p), device_id_type=MESH)
    pl.semaphore_signal(along, inc=1, device_id=(s, previous_pen), device_id_type=MESH)
    in_b[g] = jnp.zeros((part, nz), F32)
    in_t[g] = jnp.zeros((2, nz), F32)
    rest = d - ex
    x_falling[...] = jnp.broadcast_to(ends[:nx, 0:1], (nx, nz))
    x_rising[...] = jnp.broadcast_to(ends[:nx, 1:2], (nx, nz))

    pl.semaphore_wait(along, 1)
    pl.semaphore_signal(across, inc=1, device_id=(s, across_pen), device_id_type=MESH)

    def weigh(base, step, count, get):
        total = table[g, base] * get(0)
        for k in range(1, count):
            total = total + table[g, base + k * step] * get(k)
        return total

    def plane(k):
        return in_a[k // 2, (k % 2) * part : (k % 2 + 1) * part, :]

    def states(base):
        even = weigh(base, 2, GROUP, lambda k: in_s[k])
        odd = weigh(base + 1, 2, GROUP, lambda k: in_s[k])
        return even[0:2] + odd[2:4]

    def to_groups(source, landing, send_sem, recv_sem):
        copies = []
        for k, step in enumerate(far_first):
            to, device = partner(step)
            copy = pltpu.make_async_remote_copy(
                src_ref=source.at[jnp.where(to > g, 0, 1)], dst_ref=landing.at[g],
                send_sem=send_sem.at[k], recv_sem=recv_sem.at[k],
                device_id=(device, p), device_id_type=MESH,
            )
            copy.start()
            copies.append(copy)
        return copies

    for copy in copies_s:
        copy.wait_recv()
    out_t[0] = states(at.to_later)
    out_t[1] = states(at.to_earlier)
    pl.semaphore_wait(onward, 1)
    pl.semaphore_wait(sideways, 1)
    copies_t = to_groups(out_t, in_t, t_send, t_recv)
    own_states = states(at.local + 2 * GROUP * m)

    for copy in copies_a:
        copy.wait_recv()
    out_b[0] = weigh(at.to_later, 1, 2 * GROUP, plane)
    out_b[1] = weigh(at.to_earlier, 1, 2 * GROUP, plane)
    copies_b = to_groups(out_b, in_b, b_send, b_recv)

    pl.semaphore_wait(across, 1)
    copy_h1 = pltpu.make_async_remote_copy(
        src_ref=halo_out, dst_ref=halo_in, send_sem=h1_send, recv_sem=h1_recv,
        device_id=(s, lax.rem(p + n_pen - 1, n_pen)), device_id_type=MESH,
    )
    copy_h1.start()

    for i in range(GROUP):
        out_c[i] = weigh(at.local + 2 * GROUP * i, 1, 2 * GROUP, plane)

    for copy in copies_t:
        copy.wait_recv()
    own_states = (
        own_states
        + table[g, at.falling + m] * weigh(at.from_earlier, 1, groups, lambda k: in_t[k])
        + table[g, at.rising + m] * weigh(at.from_later, 1, groups, lambda k: in_t[k])
        - czx_state[0:2]
    )
    out_x[...] = own_states
    in_x[p] = own_states
    copies_x, landings_x = [], []
    for k in range(n_pen - 1):
        to = k + jnp.where(k >= p, 1, 0)
        copy = pltpu.make_async_remote_copy(
            src_ref=out_x, dst_ref=in_x.at[p], send_sem=x_send.at[k], recv_sem=x_recv.at[p],
            device_id=(s, to), device_id_type=MESH,
        )
        copy.start()
        copies_x.append(copy)
        landings_x.append(
            pltpu.make_async_remote_copy(
                src_ref=out_x, dst_ref=in_x.at[to], send_sem=x_send.at[k], recv_sem=x_recv.at[to],
                device_id=(s, to), device_id_type=MESH,
            )
        )

    copy_h1.wait_recv()
    halo = jnp.where(p == n_pen - 1, c[nx - 1 : nx, :], halo_in[0:1, :])
    coarse_t[nx : nx + 8, :] = jnp.broadcast_to(halo, (8, nz))
    copy_h2 = pltpu.make_async_remote_copy(
        src_ref=coarse_t, dst_ref=next_c, send_sem=h2_send, recv_sem=h2_recv,
        device_id=below, device_id_type=MESH,
    )
    copy_h2.start()

    for copy in copies_b:
        copy.wait_recv()
    from_earlier = weigh(at.from_earlier, 1, groups, lambda k: in_b[k])
    from_later = weigh(at.from_later, 1, groups, lambda k: in_b[k])

    def finished(row):
        out_c[row] = (
            out_c[row]
            + table[g, at.falling + row] * from_earlier
            + table[g, at.rising + row] * from_later
        )

    rank = jnp.where(m < 2, 1 - m, m)
    copies_c, landings_c = [], []
    for k in range(GROUP - 1):
        nth = k + jnp.where(k >= rank, 1, 0)
        to = jnp.where(nth < 2, 1 - nth, nth)
        finished(to)
        copy = pltpu.make_async_remote_copy(
            src_ref=out_c.at[to], dst_ref=in_c.at[held], send_sem=c_send.at[k], recv_sem=c_recv.at[m],
            device_id=(g * GROUP + to, p), device_id_type=MESH,
        )
        copy.start()
        copies_c.append(copy)
        landings_c.append(
            pltpu.make_async_remote_copy(
                src_ref=out_c.at[to], dst_ref=in_c.at[turned(to, turn)],
                send_sem=c_send.at[k], recv_sem=c_recv.at[to],
                device_id=(g * GROUP + to, p), device_id_type=MESH,
            )
        )
    finished(m)
    in_c[held] = out_c[m]

    fine_rows = lax.broadcasted_iota(jnp.int32, (2 * nx, nz), 0)

    def interpolant(values, beyond):
        high, low = parts(values)
        along_x = dot(refine_x[...], high) + dot(refine_x[...], low)
        along_x = along_x + jnp.where(fine_rows == 2 * nx - 1, 0.5 * beyond, 0.0)
        high, low = parts(along_x)
        return dot(refine_z[...], high, True) + dot(refine_z[...], low, True)

    zi = lax.broadcasted_iota(jnp.int32, (2 * nz, 2 * nx), 0)
    xi = lax.broadcasted_iota(jnp.int32, (2 * nz, 2 * nx), 1)
    kept = ((zi | xi) & 1) == 0
    fine[0] = jnp.where(kept, 0.0, u[0] - interpolant(c, halo))

    copy_h2.wait_recv()
    last = s == slabs - 1
    after = jnp.where(last, coarse_t[...], next_c[...])
    middle = 0.5 * (coarse_t[...] + after)
    fine[1] = u[1] - interpolant(middle[:nx], middle[nx : nx + 1])

    for copy in copies_s + copies_a + copies_t + copies_b + copies_x + copies_c + [copy_h1, copy_h2]:
        copy.wait_send()
    for landing in landings_x:
        landing.wait_recv()
    x_earlier = pen(0) * in_x[0, 0:1, :]
    x_later = pen(n_pen) * in_x[0, 1:2, :]
    for k in range(1, n_pen):
        x_earlier = x_earlier + pen(k) * in_x[k, 0:1, :]
        x_later = x_later + pen(n_pen + k) * in_x[k, 1:2, :]
    rest = rest + x_falling[...] * x_earlier + x_rising[...] * x_later
    for landing in landings_c:
        landing.wait_recv()
    coarse[...] = (in_c[...].reshape(nx, nz) + rest).T


def finish(part, coarse, select, fine_hbm, coarse_hbm, even, sem):
    odd_out = pltpu.make_async_copy(part.at[1], fine_hbm.at[1], sem.at[0])
    coarse_out = pltpu.make_async_copy(coarse, coarse_hbm.at[0], sem.at[1])
    odd_out.start()
    coarse_out.start()
    high, low = parts(coarse[...])
    high, low = parts(dot(select[0], high) + dot(select[0], low))
    even[...] = part[0] + dot(high, select[1], True) + dot(low, select[1], True)
    even_out = pltpu.make_async_copy(even, fine_hbm.at[0], sem.at[2])
    even_out.start()
    odd_out.wait()
    coarse_out.wait()
    even_out.wait()


def tables(slabs, n_pen, nx, nz):
    groups = slabs // GROUP
    bx = Blocks(nx * n_pen, n_pen)
    by = Blocks(slabs, groups)
    bz = Blocks(nz, 1)

    pz = np.stack(split(bz.diagonal[0].T))
    left = np.zeros((n_pen, 2, nx + 16, 2 * nx), ml_dtypes.bfloat16)
    inverse = inverse_mass(nz)
    ends = np.zeros((n_pen, nx + 8, nz), np.float32)
    ends[:, nx] = inverse[:, 0] / 3.0
    ends[:, nx + 1] = inverse[:, -1] * (-2.0 / 3.0)
    pens = np.zeros((n_pen, 2 * n_pen + 4), np.float32)
    for b in range(n_pen):
        states = np.zeros((16, 2 * nx))
        states[0] = states[10] = bx.to_later[b]
        states[1] = states[11] = bx.to_earlier[b]
        left[b, 0], left[b, 1] = split(np.concatenate([bx.diagonal[b], states]))
        ends[b, :nx, 0] = bx.falling[b]
        ends[b, :nx, 1] = bx.rising[b]
        pens[b, :n_pen] = bx.from_earlier[b]
        pens[b, n_pen : 2 * n_pen] = bx.from_later[b]
        if b == 0:
            ends[b, :nx, 2] = -bx.own_first / 3.0
            pens[b, 2 * n_pen] = -bx.first_to_later / 3.0
        if b == n_pen - 1:
            ends[b, :nx, 3] = bx.own_last * 2.0 / 3.0
            pens[b, 2 * n_pen + 3] = bx.last_to_earlier * 2.0 / 3.0

    at = Scalars(groups)
    table = np.zeros((groups + n_pen, at.size), np.float32)
    table[groups:, : pens.shape[1]] = pens
    for b in range(groups):
        table[b, at.local : at.to_later] = by.diagonal[b].reshape(-1)
        table[b, at.to_later : at.to_earlier] = by.to_later[b]
        table[b, at.to_earlier : at.falling] = by.to_earlier[b]
        table[b, at.falling : at.rising] = by.falling[b]
        table[b, at.rising : at.from_earlier] = by.rising[b]
        table[b, at.from_earlier : at.from_later] = by.from_earlier[b]
        table[b, at.from_later :] = by.from_later[b]
    return at, left, pz, ends, table


def per_device(slabs, n_pen, density):
    nz, nx = density.shape[1] // 2, density.shape[2] // 2
    groups = slabs // GROUP
    part = nx // GROUP
    at, *operands = tables(slabs, n_pen, nx, nz)
    left, pz, ends, table = operands
    operands = [pltpu.with_memory_space_constraint(a, pltpu.HBM) for a in (density, *operands)]
    anywhere = pl.BlockSpec(memory_space=pl.ANY)
    vector = pl.BlockSpec(memory_space=pltpu.VMEM)
    dma = pltpu.SemaphoreType.DMA
    spread = (2 * nz, nz), (2 * nx, nx)

    def tile(*shape):
        return pltpu.VMEM(shape, F32)

    partial, coarse, select = pl.pallas_call(
        functools.partial(kernel, (slabs, n_pen, groups, nx, nz, at)),
        out_shape=(
            tile(*density.shape),
            tile(nz, nx),
            pltpu.VMEM((2, 2 * nz, nz), BF16),
        ),
        in_specs=[anywhere] * 5,
        out_specs=(vector, vector, vector),
        scratch_shapes=[
            tile(*density.shape),
            pltpu.VMEM(left.shape[1:], BF16),
            pltpu.VMEM(pz.shape, BF16),
            tile(*ends.shape[1:]),
            pltpu.SMEM(table.shape, F32),
            pltpu.VMEM(spread[1], BF16),
            pltpu.VMEM(spread[0], BF16),
            tile(nx + 8, nz),
            tile(8, nz), tile(8, nz),
            tile(nx + 8, nz),
            tile(GROUP, 2 * part, nz), tile(GROUP, 2 * part, nz),
            tile(4, nz), tile(GROUP, 4, nz),
            tile(2, part, nz), tile(groups, part, nz),
            tile(2, 2, nz), tile(groups, 2, nz),
            tile(GROUP, part, nz), tile(GROUP, part, nz),
            tile(2, nz), tile(n_pen, 2, nz),
            tile(nx, nz), tile(nx, nz),
            dma((6,)),
            dma, dma, dma, dma,
            *[pltpu.SemaphoreType.REGULAR] * 4,
            dma((GROUP,)), dma((GROUP,)), dma((GROUP,)), dma((GROUP,)),
            dma((groups,)), dma((groups,)), dma((groups,)), dma((groups,)),
            dma((GROUP,)), dma((GROUP,)), dma((n_pen,)), dma((n_pen,)),
        ],
        compiler_params=pltpu.CompilerParams(
            collective_id=0, has_side_effects=True, vmem_limit_bytes=32 * 1024 * 1024
        ),
        name="decompose",
    )(*operands)
    return pl.pallas_call(
        finish,
        out_shape=(
            jax.ShapeDtypeStruct(density.shape, F32),
            jax.ShapeDtypeStruct((1, nz, nx), F32),
        ),
        in_specs=[vector] * 3,
        out_specs=(anywhere, anywhere),
        scratch_shapes=[tile(2 * nz, 2 * nx), dma((3,))],
        compiler_params=pltpu.CompilerParams(vmem_limit_bytes=16 * 1024 * 1024),
        name="finish",
    )(partial, coarse, select)


def solution(mesh):
    slabs, n_pen = mesh.shape["slab"], mesh.shape["pen"]
    return jax.shard_map(
        functools.partial(per_device, slabs, n_pen),
        mesh=mesh,
        in_specs=(P("slab", None, "pen"),),
        out_specs=(P("slab", None, "pen"), P("slab", None, "pen")),
        check_vma=False,
    )
```

```python
import functools
import math

import jax
import jax.numpy as jnp
import ml_dtypes
import numpy as np
from jax import lax
from jax.experimental import pallas as pl
from jax.experimental.pallas import tpu as pltpu
from jax.sharding import PartitionSpec as P

MESH = pl.DeviceIdType.MESH
DECAY = math.log(2.0 + math.sqrt(3.0))
GROUP = 8
STATE_ROWS = 8
F32 = jnp.float32
BF16 = jnp.bfloat16


def inverse_mass(m):
    i = np.arange(m)[:, None]
    j = np.arange(m)[None, :]
    low, high = np.minimum(i, j), np.maximum(i, j)
    sign = np.where((high - low) % 2 == 0, 1.0, -1.0)
    ends = (1 - np.exp(-2 * (low + 1) * DECAY)) * (1 - np.exp(-2 * (m - high) * DECAY))
    scale = 3.0 / (2 * math.sqrt(3.0) * (1 - np.exp(-2 * (m + 1) * DECAY)))
    return scale * sign * np.exp(-(high - low) * DECAY) * ends


def refine_matrix(m):
    matrix = np.zeros((2 * m, m))
    j = np.arange(m)
    matrix[2 * j, j] = 1.0
    matrix[2 * j[:-1] + 1, j[:-1]] = 0.5
    matrix[2 * j[:-1] + 1, j[:-1] + 1] = 0.5
    matrix[2 * m - 1, m - 1] = 1.0
    return matrix


def project_matrix(m):
    j = np.arange(m)
    load = np.zeros((m, 2 * m + 2))
    w = np.where(j == m - 1, 1.0, 0.5)
    for offset, weight in ((-2, 0.5), (-1, 3.0), (0, 5.0), (1, 3.0), (2, 0.5)):
        keep = 2 * j + offset >= 0
        load[j[keep], 2 * j[keep] + offset] = weight / 6.0
    load[0, 0] = 4.5 / 6.0
    load[m - 1, 2 * m - 2] = (4.0 + w[-1] + 0.5) / 6.0
    load[m - 1, 2 * m - 1] = (1.0 + 4.0 * w[-1]) / 6.0
    return inverse_mass(m) @ load[:, : 2 * m]


def falling(m, i, start):
    d = i - start
    sign = np.where(d % 2 == 0, 1.0, -1.0)
    ends = (1 - np.exp(-2.0 * (m - i) * DECAY)) / (1 - np.exp(-2.0 * (m - start) * DECAY))
    return sign * np.exp(-d * DECAY) * ends


def rising(m, i, start):
    d = start - i
    sign = np.where(d % 2 == 0, 1.0, -1.0)
    ends = (1 - np.exp(-2.0 * (i + 1) * DECAY)) / (1 - np.exp(-2.0 * (start + 1) * DECAY))
    return sign * np.exp(-d * DECAY) * ends


class Blocks:
    def __init__(self, m, n):
        whole = project_matrix(m)
        size = m // n
        rows = np.arange(size)
        self.diagonal = np.stack(
            [whole[b * size : (b + 1) * size, 2 * b * size : 2 * (b + 1) * size] for b in range(n)]
        )
        self.to_later = np.zeros((n, 2 * size))
        self.to_earlier = np.zeros((n, 2 * size))
        self.later_first = np.zeros(n)
        self.earlier_last = np.zeros(n)
        self.falling = np.zeros((n, size))
        self.rising = np.zeros((n, size))
        self.from_earlier = np.zeros((n, n))
        self.from_later = np.zeros((n, n))
        inverse = inverse_mass(m)
        self.own_first = inverse[:size, 0]
        self.own_last = inverse[m - size :, m - 1]
        for b in range(n):
            columns = slice(2 * b * size, 2 * (b + 1) * size)
            first, last = b * size, (b + 1) * size - 1
            if b < n - 1:
                self.to_later[b] = whole[last + 1, columns]
            if b > 0:
                self.to_earlier[b] = whole[first - 1, columns]
            self.falling[b] = falling(m, first + rows, first)
            self.rising[b] = rising(m, first + rows, last)
            for c in range(n):
                if c < b:
                    self.from_earlier[b, c] = falling(m, first, (c + 1) * size)
                if c > b:
                    self.from_later[b, c] = rising(m, last, c * size - 1)
        self.first_to_later = inverse[size, 0] if n > 1 else 0.0
        self.last_to_earlier = inverse[m - size - 1, m - 1] if n > 1 else 0.0


def split(matrix):
    matrix = np.asarray(matrix, np.float32)
    high = matrix.astype(ml_dtypes.bfloat16)
    low = (matrix - high.astype(np.float32)).astype(ml_dtypes.bfloat16)
    return high, low


def parts(value):
    high = value.astype(BF16)
    return high, (value - high.astype(F32)).astype(BF16)


def dot(a, b, transposed=False):
    dims = (((1,), (1 if transposed else 0,)), ((), ()))
    return lax.dot_general(a, b, dims, preferred_element_type=F32)


def dot3(a, b, transposed=False):
    return (
        dot(a[0], b[0], transposed) + dot(a[0], b[1], transposed) + dot(a[1], b[0], transposed)
    )


class Scalars:
    def __init__(self, groups):
        g = GROUP
        self.local = 0
        self.to_later = self.local + 2 * g * g
        self.to_earlier = self.to_later + 2 * g
        self.falling = self.to_earlier + 2 * g
        self.rising = self.falling + g
        self.from_earlier = self.rising + g
        self.from_later = self.from_earlier + groups
        self.size = self.from_later + groups


def kernel(
    sizes,
    u_hbm, left_hbm, pz_hbm, ends_hbm, table_hbm,
    fine, coarse, select,
    u, left, pz, ends, table, refine_x, refine_z, coarse_t, halo_in, halo_out, next_c,
    out_a, in_a, out_s, in_s, out_b, in_b, out_t, in_t, out_c, in_c, out_x, in_x,
    x_falling, x_rising,
    load_sem,
    h1_send, h1_recv, h2_send, h2_recv,
    onward, sideways, along, across, a_send, a_recv, s_send, s_recv, b_send, b_recv, t_send, t_recv, c_send, c_recv, x_send, x_recv,
):
    slabs, n_pen, groups, nx, nz, at = sizes
    part = nx // GROUP
    s = lax.axis_index("slab")
    p = lax.axis_index("pen")
    g = s // GROUP
    m = lax.rem(s, GROUP)

    load_u0 = pltpu.make_async_copy(u_hbm.at[0], u.at[0], load_sem.at[0])
    load_left = pltpu.make_async_copy(left_hbm.at[p], left, load_sem.at[1])
    load_u1 = pltpu.make_async_copy(u_hbm.at[1], u.at[1], load_sem.at[2])
    load_pz = pltpu.make_async_copy(pz_hbm, pz, load_sem.at[3])
    load_ends = pltpu.make_async_copy(ends_hbm.at[p], ends, load_sem.at[4])
    load_table = pltpu.make_async_copy(table_hbm, table, load_sem.at[5])
    load_u0.start()
    load_left.start()

    turns = groups // 2
    turn, side = lax.rem(g, turns), g // turns

    def turned(member, at_turn):
        there = 2 * at_turn // turns
        half = GROUP // 2
        return member + there * (half - GROUP * (member // half))

    held = turned(m, turn)

    def group_at(ahead, flips):
        return lax.rem(side + flips, 2) * turns + lax.rem(turn + ahead, turns)

    def partner(step):
        group = group_at(*step)
        return group, group * GROUP + turned(held, lax.rem(group, turns))

    steps = sorted(range(turns), key=lambda k: -min(k, turns - k))
    far_first = [(k, flips) for k in steps for flips in (1, 0) if (k, flips) != (0, 0)]
    pair = turn + 1 - 2 * lax.rem(turn, 2)
    fellow = (side * turns + pair) * GROUP + m
    other_half = lax.rem(2 * turn - pair + turns, turns)
    abreast = [
        (lax.rem(side + flips, 2) * turns + other_half) * GROUP + turned(held, other_half)
        for flips in (0, 1)
    ]
    beside = partner((0, 1))[1]
    members = [(g * GROUP + lax.rem(m + k, GROUP), p) for k in range(1, GROUP)]
    others = [(device, p) for device in (fellow, *abreast, beside)]
    around = n_pen // 2
    ring, place = p // around, lax.rem(p, around)

    def pen_at(ahead, flips):
        return lax.rem(ring + flips, 2) * around + lax.rem(place + ahead, around)

    next_pen, previous_pen, across_pen = pen_at(1, 0), pen_at(around - 1, 0), pen_at(0, 1)
    around_first = sorted(range(around), key=lambda k: -min(k, around - k))
    far_pens = [(k, flips) for flips in (1, 0) for k in around_first if (k, flips) != (0, 0)]
    peers = [(s, q) for q in (across_pen, next_pen, previous_pen)]
    above = (lax.rem(s + 1, slabs), p)
    below = (lax.rem(s + slabs - 1, slabs), p)
    barrier = pltpu.get_barrier_semaphore()
    for device in members:
        pl.semaphore_signal(barrier, inc=1, device_id=device, device_id_type=MESH)
    for load in (load_u1, load_pz, load_ends, load_table):
        load.start()
    greeted = [above] + others + peers
    for device in greeted:
        pl.semaphore_signal(barrier, inc=1, device_id=device, device_id_type=MESH)

    def spread_matrix(m, weight):
        row = lax.broadcasted_iota(jnp.int32, (2 * m, m), 0)
        column = lax.broadcasted_iota(jnp.int32, (2 * m, m), 1)
        return weight(row, row - 2 * column).astype(BF16)

    def even(row, away):
        return jnp.where(away == 0, 1.0, 0.0)

    def inner(row, away):
        return jnp.where(away == 0, 1.0, jnp.where(jnp.abs(away) == 1, 0.5, 0.0))

    def ending(row, away):
        return jnp.where((row == 2 * nz - 1) & (away == 1), 1.0, inner(row, away))

    select[0] = spread_matrix(nz, even)
    select[1] = spread_matrix(nx, even)
    refine_x[...] = spread_matrix(nx, inner)
    refine_z[...] = spread_matrix(nz, ending)
    row = lax.broadcasted_iota(jnp.int32, (nx, 2 * nx), 0)
    column = lax.broadcasted_iota(jnp.int32, (nx, 2 * nx), 1)
    take_x = jnp.where(column == 2 * row, 1.0, 0.0).astype(BF16)

    load_u0.wait()
    load_left.wait()
    u0 = parts(u[0])
    lx = (left[0], left[1])
    t0 = dot3(lx, u0, True)
    tc = parts(dot(take_x, u0[0], True) + dot(take_x, u0[1], True))
    load_u1.wait()
    t1 = dot3(lx, parts(u[1]), True)
    load_pz.wait()
    to_z = (pz[0], pz[1])
    y0 = dot3(parts(t0), to_z)
    y1 = dot3(parts(t1), to_z)
    c = dot(tc[0], select[0]) + dot(tc[1], select[0])
    coarse_t[:nx, :] = c
    load_ends.wait()
    load_table.wait()

    def pen(k):
        return table[groups + p, k]

    z_ends = ends[nx : nx + 1, :], ends[nx + 1 : nx + 2, :]
    d = c[:, 0:1] * z_ends[0] + c[:, nz - 1 : nz] * z_ends[1]
    cz = c - d
    cz_first, cz_last = cz[0:1, :], cz[nx - 1 : nx, :]
    ex = ends[:nx, 2:3] * cz_first + ends[:nx, 3:4] * cz_last
    rows8 = lax.broadcasted_iota(jnp.int32, (STATE_ROWS, nz), 0)
    czx_state = jnp.where(
        rows8 == 0,
        pen(2 * n_pen) * cz_first + pen(2 * n_pen + 1) * cz_last,
        pen(2 * n_pen + 2) * cz_first + pen(2 * n_pen + 3) * cz_last,
    )
    czx = cz + ex
    s0 = jnp.where(s == 0, F32(0.5), F32(0.0))
    s1 = jnp.where(s == 0, F32(-1.0 / 12.0), jnp.where(s == slabs - 1, F32(-0.8), F32(0.0)))
    p0 = y0[:nx] + s0 * czx
    p1 = y1[:nx] + s1 * czx
    n0 = y0[nx : nx + STATE_ROWS] + s0 * czx_state
    n1 = y1[nx + STATE_ROWS : nx + 2 * STATE_ROWS] + s1 * jnp.roll(czx_state, 2, 0)
    out_a[:, 0:part, :] = p0.reshape(GROUP, part, nz)
    out_a[:, part : 2 * part, :] = p1.reshape(GROUP, part, nz)
    out_s[...] = jnp.where(rows8 < 2, n0, n1)[0:4]
    in_a[m] = out_a[held]
    in_s[m] = out_s[...]
    halo_out[...] = c[0:8, :]

    pl.semaphore_wait(barrier, len(members) + len(greeted))

    copies_s, copies_a = [], []
    for k in range(1, GROUP):
        copy = pltpu.make_async_remote_copy(
            src_ref=out_s, dst_ref=in_s.at[m], send_sem=s_send.at[k], recv_sem=s_recv.at[k],
            device_id=(g * GROUP + lax.rem(m + k, GROUP), p), device_id_type=MESH,
        )
        copy.start()
        copies_s.append(copy)
    for k in range(1, GROUP):
        to = lax.rem(m + k, GROUP)
        copy = pltpu.make_async_remote_copy(
            src_ref=out_a.at[turned(to, turn)], dst_ref=in_a.at[m],
            send_sem=a_send.at[k], recv_sem=a_recv.at[k],
            device_id=(g * GROUP + to, p), device_id_type=MESH,
        )
        copy.start()
        copies_a.append(copy)
    pl.semaphore_signal(onward, inc=1, device_id=(fellow, p), device_id_type=MESH)
    pl.semaphore_signal(sideways, inc=1, device_id=(beside, p), device_id_type=MESH)
    pl.semaphore_signal(along, inc=1, device_id=(s, previous_pen), device_id_type=MESH)
    in_b[g] = jnp.zeros((part, nz), F32)
    in_t[g] = jnp.zeros((2, nz), F32)
    rest = d - ex
    x_falling[...] = jnp.broadcast_to(ends[:nx, 0:1], (nx, nz))
    x_rising[...] = jnp.broadcast_to(ends[:nx, 1:2], (nx, nz))

    pl.semaphore_wait(along, 1)
    pl.semaphore_signal(across, inc=1, device_id=(s, across_pen), device_id_type=MESH)

    def weigh(base, step, count, get):
        total = table[g, base] * get(0)
        for k in range(1, count):
            total = total + table[g, base + k * step] * get(k)
        return total

    def plane(k):
        return in_a[k // 2, (k % 2) * part : (k % 2 + 1) * part, :]

    def states(base):
        even = weigh(base, 2, GROUP, lambda k: in_s[k])
        odd = weigh(base + 1, 2, GROUP, lambda k: in_s[k])
        return even[0:2] + odd[2:4]

    def to_groups(source, landing, send_sem, recv_sem):
        copies = []
        for k, step in enumerate(far_first):
            to, device = partner(step)
            copy = pltpu.make_async_remote_copy(
                src_ref=source.at[jnp.where(to > g, 0, 1)], dst_ref=landing.at[g],
                send_sem=send_sem.at[k], recv_sem=recv_sem.at[k],
                device_id=(device, p), device_id_type=MESH,
            )
            copy.start()
            copies.append(copy)
        return copies

    for copy in copies_s:
        copy.wait_recv()
    out_t[0] = states(at.to_later)
    out_t[1] = states(at.to_earlier)
    pl.semaphore_wait(onward, 1)
    pl.semaphore_wait(sideways, 1)
    copies_t = to_groups(out_t, in_t, t_send, t_recv)
    own_states = states(at.local + 2 * GROUP * m)

    for copy in copies_a:
        copy.wait_recv()
    out_b[0] = weigh(at.to_later, 1, 2 * GROUP, plane)
    out_b[1] = weigh(at.to_earlier, 1, 2 * GROUP, plane)
    copies_b = to_groups(out_b, in_b, b_send, b_recv)

    pl.semaphore_wait(across, 1)
    copy_h1 = pltpu.make_async_remote_copy(
        src_ref=halo_out, dst_ref=halo_in, send_sem=h1_send, recv_sem=h1_recv,
        device_id=(s, lax.rem(p + n_pen - 1, n_pen)), device_id_type=MESH,
    )
    copy_h1.start()

    for i in range(GROUP):
        out_c[i] = weigh(at.local + 2 * GROUP * i, 1, 2 * GROUP, plane)

    for copy in copies_t:
        copy.wait_recv()
    own_states = (
        own_states
        + table[g, at.falling + m] * weigh(at.from_earlier, 1, groups, lambda k: in_t[k])
        + table[g, at.rising + m] * weigh(at.from_later, 1, groups, lambda k: in_t[k])
        - czx_state[0:2]
    )
    out_x[...] = own_states
    in_x[p] = own_states
    copies_x = []
    for k, step in enumerate(far_pens):
        copy = pltpu.make_async_remote_copy(
            src_ref=out_x, dst_ref=in_x.at[p], send_sem=x_send.at[k], recv_sem=x_recv.at[k],
            device_id=(s, pen_at(*step)), device_id_type=MESH,
        )
        copy.start()
        copies_x.append(copy)

    copy_h1.wait_recv()
    halo = jnp.where(p == n_pen - 1, c[nx - 1 : nx, :], halo_in[0:1, :])
    coarse_t[nx : nx + 8, :] = jnp.broadcast_to(halo, (8, nz))
    copy_h2 = pltpu.make_async_remote_copy(
        src_ref=coarse_t, dst_ref=next_c, send_sem=h2_send, recv_sem=h2_recv,
        device_id=below, device_id_type=MESH,
    )
    copy_h2.start()

    for copy in copies_b:
        copy.wait_recv()
    from_earlier = weigh(at.from_earlier, 1, groups, lambda k: in_b[k])
    from_later = weigh(at.from_later, 1, groups, lambda k: in_b[k])

    def finished(row):
        out_c[row] = (
            out_c[row]
            + table[g, at.falling + row] * from_earlier
            + table[g, at.rising + row] * from_later
        )

    rank = jnp.where(m < 2, 1 - m, m)
    copies_c, landings_c = [], []
    for k in range(GROUP - 1):
        nth = k + jnp.where(k >= rank, 1, 0)
        to = jnp.where(nth < 2, 1 - nth, nth)
        finished(to)
        copy = pltpu.make_async_remote_copy(
            src_ref=out_c.at[to], dst_ref=in_c.at[held], send_sem=c_send.at[k], recv_sem=c_recv.at[m],
            device_id=(g * GROUP + to, p), device_id_type=MESH,
        )
        copy.start()
        copies_c.append(copy)
        landings_c.append(
            pltpu.make_async_remote_copy(
                src_ref=out_c.at[to], dst_ref=in_c.at[turned(to, turn)],
                send_sem=c_send.at[k], recv_sem=c_recv.at[to],
                device_id=(g * GROUP + to, p), device_id_type=MESH,
            )
        )
    finished(m)
    in_c[held] = out_c[m]

    fine_rows = lax.broadcasted_iota(jnp.int32, (2 * nx, nz), 0)

    def interpolant(values, beyond):
        high, low = parts(values)
        along_x = dot(refine_x[...], high) + dot(refine_x[...], low)
        along_x = along_x + jnp.where(fine_rows == 2 * nx - 1, 0.5 * beyond, 0.0)
        high, low = parts(along_x)
        return dot(refine_z[...], high, True) + dot(refine_z[...], low, True)

    zi = lax.broadcasted_iota(jnp.int32, (2 * nz, 2 * nx), 0)
    xi = lax.broadcasted_iota(jnp.int32, (2 * nz, 2 * nx), 1)
    kept = ((zi | xi) & 1) == 0
    fine[0] = jnp.where(kept, 0.0, u[0] - interpolant(c, halo))

    copy_h2.wait_recv()
    last = s == slabs - 1
    after = jnp.where(last, coarse_t[...], next_c[...])
    middle = 0.5 * (coarse_t[...] + after)
    fine[1] = u[1] - interpolant(middle[:nx], middle[nx : nx + 1])

    for copy in copies_s + copies_a + copies_t + copies_b + copies_x + copies_c + [copy_h1, copy_h2]:
        copy.wait_send()
    for copy in copies_x:
        copy.wait_recv()
    x_earlier = pen(0) * in_x[0, 0:1, :]
    x_later = pen(n_pen) * in_x[0, 1:2, :]
    for k in range(1, n_pen):
        x_earlier = x_earlier + pen(k) * in_x[k, 0:1, :]
        x_later = x_later + pen(n_pen + k) * in_x[k, 1:2, :]
    rest = rest + x_falling[...] * x_earlier + x_rising[...] * x_later
    for landing in landings_c:
        landing.wait_recv()
    coarse[...] = (in_c[...].reshape(nx, nz) + rest).T


def finish(part, coarse, select, fine_hbm, coarse_hbm, even, sem):
    odd_out = pltpu.make_async_copy(part.at[1], fine_hbm.at[1], sem.at[0])
    coarse_out = pltpu.make_async_copy(coarse, coarse_hbm.at[0], sem.at[1])
    odd_out.start()
    coarse_out.start()
    along_z = jnp.concatenate([select[0], select[0]], 1)
    along_x = jnp.concatenate([select[1], select[1]], 1)
    spread = dot(along_z, jnp.concatenate(parts(coarse[...]), 0))
    even[...] = part[0] + dot(jnp.concatenate(parts(spread), 1), along_x, True)
    even_out = pltpu.make_async_copy(even, fine_hbm.at[0], sem.at[2])
    even_out.start()
    odd_out.wait()
    coarse_out.wait()
    even_out.wait()


def tables(slabs, n_pen, nx, nz):
    groups = slabs // GROUP
    bx = Blocks(nx * n_pen, n_pen)
    by = Blocks(slabs, groups)
    bz = Blocks(nz, 1)

    pz = np.stack(split(bz.diagonal[0].T))
    left = np.zeros((n_pen, 2, nx + 16, 2 * nx), ml_dtypes.bfloat16)
    inverse = inverse_mass(nz)
    ends = np.zeros((n_pen, nx + 8, nz), np.float32)
    ends[:, nx] = inverse[:, 0] / 3.0
    ends[:, nx + 1] = inverse[:, -1] * (-2.0 / 3.0)
    pens = np.zeros((n_pen, 2 * n_pen + 4), np.float32)
    for b in range(n_pen):
        states = np.zeros((16, 2 * nx))
        states[0] = states[10] = bx.to_later[b]
        states[1] = states[11] = bx.to_earlier[b]
        left[b, 0], left[b, 1] = split(np.concatenate([bx.diagonal[b], states]))
        ends[b, :nx, 0] = bx.falling[b]
        ends[b, :nx, 1] = bx.rising[b]
        pens[b, :n_pen] = bx.from_earlier[b]
        pens[b, n_pen : 2 * n_pen] = bx.from_later[b]
        if b == 0:
            ends[b, :nx, 2] = -bx.own_first / 3.0
            pens[b, 2 * n_pen] = -bx.first_to_later / 3.0
        if b == n_pen - 1:
            ends[b, :nx, 3] = bx.own_last * 2.0 / 3.0
            pens[b, 2 * n_pen + 3] = bx.last_to_earlier * 2.0 / 3.0

    at = Scalars(groups)
    table = np.zeros((groups + n_pen, at.size), np.float32)
    table[groups:, : pens.shape[1]] = pens
    for b in range(groups):
        table[b, at.local : at.to_later] = by.diagonal[b].reshape(-1)
        table[b, at.to_later : at.to_earlier] = by.to_later[b]
        table[b, at.to_earlier : at.falling] = by.to_earlier[b]
        table[b, at.falling : at.rising] = by.falling[b]
        table[b, at.rising : at.from_earlier] = by.rising[b]
        table[b, at.from_earlier : at.from_later] = by.from_earlier[b]
        table[b, at.from_later :] = by.from_later[b]
    return at, left, pz, ends, table


def per_device(slabs, n_pen, density):
    nz, nx = density.shape[1] // 2, density.shape[2] // 2
    groups = slabs // GROUP
    part = nx // GROUP
    at, *operands = tables(slabs, n_pen, nx, nz)
    left, pz, ends, table = operands
    operands = [pltpu.with_memory_space_constraint(a, pltpu.HBM) for a in (density, *operands)]
    anywhere = pl.BlockSpec(memory_space=pl.ANY)
    vector = pl.BlockSpec(memory_space=pltpu.VMEM)
    dma = pltpu.SemaphoreType.DMA
    spread = (2 * nz, nz), (2 * nx, nx)

    def tile(*shape):
        return pltpu.VMEM(shape, F32)

    partial, coarse, select = pl.pallas_call(
        functools.partial(kernel, (slabs, n_pen, groups, nx, nz, at)),
        out_shape=(
            tile(*density.shape),
            tile(nz, nx),
            pltpu.VMEM((2, 2 * nz, nz), BF16),
        ),
        in_specs=[anywhere] * 5,
        out_specs=(vector, vector, vector),
        scratch_shapes=[
            tile(*density.shape),
            pltpu.VMEM(left.shape[1:], BF16),
            pltpu.VMEM(pz.shape, BF16),
            tile(*ends.shape[1:]),
            pltpu.SMEM(table.shape, F32),
            pltpu.VMEM(spread[1], BF16),
            pltpu.VMEM(spread[0], BF16),
            tile(nx + 8, nz),
            tile(8, nz), tile(8, nz),
            tile(nx + 8, nz),
            tile(GROUP, 2 * part, nz), tile(GROUP, 2 * part, nz),
            tile(4, nz), tile(GROUP, 4, nz),
            tile(2, part, nz), tile(groups, part, nz),
            tile(2, 2, nz), tile(groups, 2, nz),
            tile(GROUP, part, nz), tile(GROUP, part, nz),
            tile(2, nz), tile(n_pen, 2, nz),
            tile(nx, nz), tile(nx, nz),
            dma((6,)),
            dma, dma, dma, dma,
            *[pltpu.SemaphoreType.REGULAR] * 4,
            dma((GROUP,)), dma((GROUP,)), dma((GROUP,)), dma((GROUP,)),
            dma((groups,)), dma((groups,)), dma((groups,)), dma((groups,)),
            dma((GROUP,)), dma((GROUP,)), dma((n_pen,)), dma((n_pen,)),
        ],
        compiler_params=pltpu.CompilerParams(
            collective_id=0, has_side_effects=True, vmem_limit_bytes=32 * 1024 * 1024
        ),
        name="decompose",
    )(*operands)
    return pl.pallas_call(
        finish,
        out_shape=(
            jax.ShapeDtypeStruct(density.shape, F32),
            jax.ShapeDtypeStruct((1, nz, nx), F32),
        ),
        in_specs=[vector] * 3,
        out_specs=(anywhere, anywhere),
        scratch_shapes=[tile(2 * nz, 2 * nx), dma((3,))],
        compiler_params=pltpu.CompilerParams(vmem_limit_bytes=16 * 1024 * 1024),
        name="finish",
    )(partial, coarse, select)


def solution(mesh):
    slabs, n_pen = mesh.shape["slab"], mesh.shape["pen"]
    return jax.shard_map(
        functools.partial(per_device, slabs, n_pen),
        mesh=mesh,
        in_specs=(P("slab", None, "pen"),),
        out_specs=(P("slab", None, "pen"), P("slab", None, "pen")),
        check_vma=False,
    )
```
